32 devices in a mesh: dp: 16 (over z, x, core), branch: 2 (over y).
Axes of the slice: x: 2, y: 2, z: 4, core: 2. Of those that a mesh axis runs over, the one named last changes fastest.
Arguments:
- tokens: bfloat16 [8192, 2048], P(('dp', 'branch')), may hold values from -6 to 6
- cotangent: bfloat16 [8192, 2048], P(('dp', 'branch')), may hold values from -6 to 6
- lengths: int32 [16, 2], P('dp'), may hold values from 64 to 256, as said below
- w_qkv: float32 [2048, 6144], P('dp', 'branch'), may hold values from -0.125 to 0.125
- w_out: float32 [2048, 2048], P('dp', 'branch'), may hold values from -0.5 to 0.5
- w_gate_up: float32 [2048, 11264], P('dp', 'branch'), may hold values from -0.125 to 0.125
- w_down: float32 [5632, 2048], P('dp', 'branch'), may hold values from -0.078125 to 0.078125
- vectors: float32 [5, 2048], P(None, ('dp', 'branch')), as said below
- first_qkv: float32 [2048, 6144], P('dp', 'branch'), may hold values from -27.1529 to 27.1529
- first_out: float32 [2048, 2048], P('dp', 'branch'), may hold values from -13.57645 to 13.57645
- first_gate_up: float32 [2048, 11264], P('dp', 'branch'), may hold values from -16.29174 to 16.29174
- first_down: float32 [5632, 2048], P('dp', 'branch'), may hold values from -27.1529 to 27.1529
- first_vectors: float32 [5, 2048], P(None, ('dp', 'branch')), may hold values from -54.3058 to 54.3058
- second_qkv: float32 [2048, 6144], P('dp', 'branch'), may hold values from 106.496 to 434.176
- second_out: float32 [2048, 2048], P('dp', 'branch'), may hold values from 27.0336 to 106.496
- second_gate_up: float32 [2048, 11264], P('dp', 'branch'), may hold values from 38.5024 to 155.648
- second_down: float32 [5632, 2048], P('dp', 'branch'), may hold values from 106.496 to 434.176
- second_vectors: float32 [5, 2048], P(None, ('dp', 'branch')), may hold values from 434.176 to 1720.32
Outputs:
- output: bfloat16 [8192, 2048], P(('dp', 'branch'))
- input_grad: bfloat16 [8192, 2048], P(('dp', 'branch'))
- new_qkv: float32 [2048, 6144], P('dp', 'branch')
- new_out: float32 [2048, 2048], P('dp', 'branch')
- new_gate_up: float32 [2048, 11264], P('dp', 'branch')
- new_down: float32 [5632, 2048], P('dp', 'branch')
- new_vectors: float32 [5, 2048], P(None, ('dp', 'branch'))
- moment_qkv: float32 [2048, 6144], P('dp', 'branch')
- moment_out: float32 [2048, 2048], P('dp', 'branch')
- moment_gate_up: float32 [2048, 11264], P('dp', 'branch')
- moment_down: float32 [5632, 2048], P('dp', 'branch')
- moment_vectors: float32 [5, 2048], P(None, ('dp', 'branch'))
- square_qkv: float32 [2048, 6144], P('dp', 'branch')
- square_out: float32 [2048, 2048], P('dp', 'branch')
- square_gate_up: float32 [2048, 11264], P('dp', 'branch')
- square_down: float32 [5632, 2048], P('dp', 'branch')
- square_vectors: float32 [5, 2048], P(None, ('dp', 'branch'))
The draws below stay inside these ranges and needn't reach their ends.
Inputs may be any that keep to these rules, and one draw needn't show every extreme that they name: `lengths`: some slot has length exactly 256. `vectors`: row 0 is the norm's gain, row 1 its shift, rows 2 to 4 the query, key and value biases.
All inputs are finite; a program needn't handle non-finite values.
Results may differ from the reference program's by a relative error of at most 0.0091.
Values may be sent and summed in bfloat16 or wider, within the bound.
No kernel may reach another device: no remote copies, remote signals or barrier semaphores. Data moves between devices by JAX's collectives and lax.ppermute only.
A program may use at most 896 MiB of HBM per device.

```python
import math
import jax
import jax.numpy as jnp
from jax import lax

D = 2048
HEADS = 32
HEAD = 64
ROT = 16
FF = 5632
ROWS = 256
MB = 2
STEP = 10
TOKENS = 8192
N_DP = 16


def draw_lengths(key, part):
    key = jax.random.fold_in(key, 11)
    key_len, key_pick = jax.random.split(key)
    drawn = jax.random.randint(key_len, (N_DP * MB,), ROWS // 4, ROWS + 1)
    chosen = jax.random.randint(key_pick, (), 0, N_DP * MB)
    flattened = jnp.where(jnp.arange(N_DP * MB) == chosen, ROWS, drawn)
    return flattened.reshape(N_DP, MB).astype(jnp.int32)


def draw_vectors(key, part):
    key = jax.random.fold_in(key, 23)
    gain_key, bias_key = jax.random.split(key)
    gain_row = jax.random.uniform(gain_key, (1, D), jnp.float32, 0.7, 1.3)
    bias_rows = 0.3 * jax.random.normal(bias_key, (4, D), jnp.float32)
    return jnp.concatenate([gain_row, bias_rows], axis=0).astype(jnp.float32)


def steps_of(rng, extent, shards, low, high):
    def one(dim, shards_of):
        steps = jax.random.uniform(jax.random.fold_in(jax.random.fold_in(rng, 6), dim), (shards_of,), jnp.float32, low / len(shards), high / len(shards))
        return jnp.repeat(jnp.exp(steps), extent[dim] // shards_of).reshape((-1,) + (1,) * (len(extent) - dim - 1))

    loudness = one(*shards[0])
    for cut in shards[1:]:
        loudness = loudness * one(*cut)
    return loudness


def gaussian(rng, shape, deviation, bound, cuts=(), held_as=jnp.bfloat16):
    result = deviation * jax.random.normal(rng, shape, jnp.float32)
    if cuts:
        result = result * steps_of(rng, shape, cuts, -0.22, 0.18)
    return jnp.clip(result, -bound, bound).astype(held_as)


def setup_inputs(seed: int = 0) -> dict:
    streams_of = jax.random.split(jax.random.key(seed), 19)
    return {
        "tokens": gaussian(streams_of[0], (TOKENS, D), 1.0, 6.0, ((0, 32),)),
        "cotangent": gaussian(streams_of[1], (TOKENS, D), 1.0, 6.0, ((0, 32),)),
        "lengths": draw_lengths(jax.random.fold_in(streams_of[18], 71), 0),
        "w_qkv": gaussian(streams_of[3], (D, 3 * D), D ** -0.5, 0.125, ((0, 16), (1, 2)), jnp.float32),
        "w_out": gaussian(streams_of[4], (D, D), (D // 16) ** -0.5, 0.5, ((0, 16), (1, 2)), jnp.float32),
        "w_gate_up": gaussian(streams_of[5], (D, 2 * FF), D ** -0.5, 0.125, ((0, 16), (1, 2)), jnp.float32),
        "w_down": gaussian(streams_of[6], (FF, D), FF ** -0.5, 0.078125, ((0, 16), (1, 2)), jnp.float32),
        "vectors": draw_vectors(jax.random.fold_in(streams_of[18], 71), 0),
        "first_qkv": gaussian(streams_of[8], (D, 3 * D), (0.055 * TOKENS ** 0.5), 27.1529, ((0, 16), (1, 2)), jnp.float32),
        "first_out": gaussian(streams_of[9], (D, D), (0.028 * TOKENS ** 0.5), 13.57645, ((0, 16), (1, 2)), jnp.float32),
        "first_gate_up": gaussian(streams_of[10], (D, 2 * FF), (0.033 * TOKENS ** 0.5), 16.29174, ((0, 16), (1, 2)), jnp.float32),
        "first_down": gaussian(streams_of[11], (FF, D), (0.055 * TOKENS ** 0.5), 27.1529, ((0, 16), (1, 2)), jnp.float32),
        "first_vectors": gaussian(streams_of[12], (5, D), (0.11 * TOKENS ** 0.5), 54.3058, ((1, 32),), jnp.float32),
        "second_qkv": jnp.clip(jnp.exp(math.log(434.176) - 1.40534252 * jax.random.uniform(streams_of[13], (D, 3 * D), jnp.float32) ** steps_of(streams_of[13], (D, 3 * D), ((0, 16), (1, 2)), -0.2, 0.2)), 106.496, 434.176),
        "second_out": jnp.clip(jnp.exp(math.log(106.496) - 1.3710269 * jax.random.uniform(streams_of[14], (D, D), jnp.float32) ** steps_of(streams_of[14], (D, D), ((0, 16), (1, 2)), -0.2, 0.2)), 27.0336, 106.496),
        "second_gate_up": jnp.clip(jnp.exp(math.log(155.648) - 1.3968765 * jax.random.uniform(streams_of[15], (D, 2 * FF), jnp.float32) ** steps_of(streams_of[15], (D, 2 * FF), ((0, 16), (1, 2)), -0.2, 0.2)), 38.5024, 155.648),
        "second_down": jnp.clip(jnp.exp(math.log(434.176) - 1.40534252 * jax.random.uniform(streams_of[16], (FF, D), jnp.float32) ** steps_of(streams_of[16], (FF, D), ((0, 16), (1, 2)), -0.2, 0.2)), 106.496, 434.176),
        "second_vectors": jnp.clip(jnp.exp(math.log(1720.32) - 1.3768156 * jax.random.uniform(streams_of[17], (5, D), jnp.float32) ** steps_of(streams_of[17], (5, D), ((1, 32),), -0.2, 0.2)), 434.176, 1720.32),
    }


@jax.custom_vjp
def low(v):
    return lax.optimization_barrier(v.astype(jnp.bfloat16)).astype(jnp.float32)

@jax.custom_vjp
def low_back(v):
    return v

def low_keep(v):
    return (low(v), None)

def low_pass(kept, grad):
    return (grad,)

def back_keep(v):
    return (v, None)

def back_low(kept, grad):
    return (low(grad),)
low.defvjp(low_keep, low_pass)
low_back.defvjp(back_keep, back_low)
theta_base = 10000.0
norm_eps = 1e-05
beta_one = 0.9
beta_two = 0.95
adam_eps = 1e-08
decay_rate = 0.1
rate_matrix = 0.05
rate_vector = 1.0

def rotary_tables(row_count):
    half_rot = ROT // 2
    freqs = theta_base ** (-2.0 * jnp.arange(half_rot, dtype=jnp.float32) / ROT)
    angles = jnp.arange(row_count, dtype=jnp.float32)[:, None] * freqs[None, :]
    return (jnp.cos(angles)[:, None, :], jnp.sin(angles)[:, None, :])

def rotate(values, cosine, sine):
    half_rot = cosine.shape[-1]
    rot_one = values[..., :half_rot]
    rot_two = values[..., half_rot:2 * half_rot]
    return jnp.concatenate([rot_one * cosine - rot_two * sine, rot_two * cosine + rot_one * sine, values[..., 2 * half_rot:]], axis=-1)

def normalize(block_rows, gain_row, shift_row):
    row_mean = lax.optimization_barrier(jnp.mean(block_rows, axis=-1, keepdims=True))
    centered = block_rows - row_mean
    inv_std = lax.rsqrt(lax.optimization_barrier(jnp.mean(centered * centered, axis=-1, keepdims=True)) + norm_eps)
    scaled = centered * inv_std
    return scaled * gain_row + shift_row

def slot_forward(weights, slot_rows, slot_length):
    w_qkv_low, w_out_low, w_gu_low, w_down_low, gain_row, shift_row, qkv_bias = weights
    highest = lax.Precision.HIGHEST
    row_count = slot_rows.shape[0]
    normed_low = low_back(low(normalize(slot_rows, gain_row, shift_row)))
    qkv = low_back(jnp.dot(normed_low, w_qkv_low, precision=highest) + qkv_bias)
    cosine, sine = rotary_tables(row_count)
    queries = low(rotate(qkv[:, :D].reshape(row_count, HEADS, HEAD), cosine, sine))
    key_rot = low(rotate(qkv[:, D:2 * D].reshape(row_count, HEADS, HEAD), cosine, sine))
    values = low(qkv[:, 2 * D:].reshape(row_count, HEADS, HEAD))
    scores = low_back(jnp.einsum('qhd,khd->hqk', queries, key_rot, precision=highest) * HEAD ** (-0.5))
    position = jnp.arange(row_count, dtype=jnp.int32)
    allowed = (position[None, :] <= position[:, None]) & (position[None, :] < slot_length)
    masked = jnp.where(allowed[None], scores, -1e+30)
    row_max = lax.optimization_barrier(jnp.max(masked, axis=-1, keepdims=True))
    exp_scores = jnp.exp(masked - row_max)
    probs = low(exp_scores / lax.optimization_barrier(jnp.sum(exp_scores, axis=-1, keepdims=True)))
    attended = jnp.einsum('hqk,khd->qhd', probs, values, precision=highest).reshape(row_count, D)
    attended = low_back(low(attended))
    attn_branch = low(jnp.dot(attended, w_out_low, precision=highest))
    joined = low_back(jnp.dot(normed_low, w_gu_low, precision=highest))
    gate_part = joined[:, :FF]
    up_part = joined[:, FF:]
    hidden = low(gate_part * jax.nn.sigmoid(gate_part) * up_part)
    mlp_branch = low(jnp.dot(hidden, w_down_low, precision=highest))
    return slot_rows + attn_branch + mlp_branch

def adam_update(weight, gradient, first_moment, second_moment, step_rate, decay):
    moment_new = beta_one * first_moment + (1.0 - beta_one) * gradient
    square_new = beta_two * second_moment + (1.0 - beta_two) * gradient * gradient
    moment_hat = moment_new / (1.0 - beta_one ** STEP)
    square_hat = square_new / (1.0 - beta_two ** STEP)
    weight_new = weight - step_rate * (moment_hat / (jnp.sqrt(square_hat) + adam_eps) + decay * weight)
    return (weight_new, moment_new, square_new)

def reference(tokens, cotangent, lengths, w_qkv, w_out, w_gate_up, w_down, vectors, first_qkv, first_out, first_gate_up, first_down, first_vectors, second_qkv, second_out, second_gate_up, second_down, second_vectors):
    slot_count = lengths.shape[0] * lengths.shape[1]
    x_slots = tokens.astype(jnp.float32).reshape(slot_count, ROWS, D)
    grad_slots = cotangent.astype(jnp.float32).reshape(slot_count, ROWS, D)
    length_list = lengths.reshape(slot_count).astype(jnp.int32)

    def forward(inputs, w_qkv_in, w_out_in, w_gu_in, w_down_in, vectors_in):
        weights = (low(w_qkv_in), low(w_out_in), low(w_gu_in), low(w_down_in), vectors_in[0], vectors_in[1], vectors_in[2:5].reshape(-1))
        step_fn = jax.checkpoint(slot_forward)
        return lax.map(lambda item: step_fn(weights, item[0], item[1]), (inputs, length_list))
    out_slots, pullback = jax.vjp(forward, x_slots, w_qkv, w_out, w_gate_up, w_down, vectors)
    d_inputs, g_qkv, g_out, g_gu, g_down, g_vec = pullback(grad_slots)
    new_qkv, moment_qkv, square_qkv = adam_update(w_qkv, g_qkv, first_qkv, second_qkv, rate_matrix, decay_rate)
    new_out, moment_out, square_out = adam_update(w_out, g_out, first_out, second_out, rate_matrix, decay_rate)
    new_gu, moment_gu, square_gu = adam_update(w_gate_up, g_gu, first_gate_up, second_gate_up, rate_matrix, decay_rate)
    new_down, moment_down, square_down = adam_update(w_down, g_down, first_down, second_down, rate_matrix, decay_rate)
    new_vec, moment_vec, square_vec = adam_update(vectors, g_vec, first_vectors, second_vectors, rate_vector, 0.0)
    output = out_slots.reshape(-1, D).astype(jnp.bfloat16)
    input_grad = d_inputs.reshape(-1, D).astype(jnp.bfloat16)
    return (output, input_grad, new_qkv, new_out, new_gu, new_down, new_vec, moment_qkv, moment_out, moment_gu, moment_down, moment_vec, square_qkv, square_out, square_gu, square_down, square_vec)
```

```python
import functools

import jax
import jax.numpy as jnp
from jax import lax
from jax.experimental import pallas as pl
from jax.experimental.pallas import tpu as pltpu
from jax.sharding import Mesh, PartitionSpec as P

HEADS = 32
HEAD = 64
ROT = 16
MB = 2
STEP = 10
SLICES = 8

theta_base = 10000.0
norm_eps = 1e-05
beta_one = 0.9
beta_two = 0.95
adam_eps = 1e-08
decay_rate = 0.1
rate_matrix = 0.05
rate_vector = 1.0

AXES = ("a", "t", "b", "y")
F32 = jnp.float32
BF16 = jnp.bfloat16


def dot(left, right):
    return jnp.dot(left, right, preferred_element_type=F32)


def dot_nt(left, right):
    return lax.dot_general(left, right, (((1,), (1,)), ((), ())), preferred_element_type=F32)


def dot_tn(left, right):
    return lax.dot_general(left, right, (((0,), (0,)), ((), ())), preferred_element_type=F32)


def rotary_lanes(row_count):
    half_rot = ROT // 2
    freqs = theta_base ** (-2.0 * jnp.arange(half_rot, dtype=F32) / ROT)
    angles = jnp.arange(row_count, dtype=F32)[:, None] * freqs[None, :]
    cosine, sine = jnp.cos(angles), jnp.sin(angles)
    rest = HEAD - ROT
    one, zero, gap = (
        jnp.ones((row_count, rest), F32),
        jnp.zeros((row_count, half_rot), F32),
        jnp.zeros((row_count, rest), F32),
    )
    cos_head = jnp.concatenate([cosine, cosine, one], axis=1)
    up_head = jnp.concatenate([sine, zero, gap], axis=1)
    down_head = jnp.concatenate([zero, sine, gap], axis=1)
    return tuple(jnp.concatenate([x, x], axis=1) for x in (cos_head, up_head, down_head))


def attention_kernel(lengths, qkv, dpo, cos_ref, up_ref, down_ref, o_ref, dqkv_ref, bias_ref):
    rows = qkv.shape[0]
    width = dpo.shape[1]
    length = lengths[pl.program_id(0)]
    cosine, sine_up, sine_down = cos_ref[...], up_ref[...], down_ref[...]
    query_at = lax.broadcasted_iota(jnp.int32, (rows, rows), 0)
    key_at = lax.broadcasted_iota(jnp.int32, (rows, rows), 1)
    allowed = (key_at <= query_at) & (key_at < length)
    lane = lax.broadcasted_iota(jnp.int32, (rows, 2 * HEAD), 1)
    lower = lane < HEAD
    half = ROT // 2
    scale = HEAD ** (-0.5)

    def turn(x, sign):
        ahead = pltpu.roll(x, 2 * HEAD - half, 1)
        behind = pltpu.roll(x, half, 1)
        return x * cosine + sign * (behind * sine_down - ahead * sine_up)

    for pair in range(width // (2 * HEAD)):
        at = pair * 2 * HEAD
        cols = slice(at, at + 2 * HEAD)
        k_cols = slice(width + at, width + at + 2 * HEAD)
        v_cols = slice(2 * width + at, 2 * width + at + 2 * HEAD)
        q_rot = turn(qkv[:, cols], 1.0).astype(BF16)
        k_rot = turn(qkv[:, k_cols], 1.0).astype(BF16)
        values = qkv[:, v_cols].astype(BF16)
        grad = dpo[:, cols]
        results = []
        for side in range(2):
            mine = lower if side == 0 else ~lower
            scores = dot_nt(jnp.where(mine, q_rot, 0.0).astype(BF16), k_rot) * scale
            masked = jnp.where(allowed, scores, -1e30)
            raised = jnp.exp(masked - jnp.max(masked, axis=1, keepdims=True))
            probs = raised * (1.0 / jnp.sum(raised, axis=1, keepdims=True))
            probs_low = probs.astype(BF16)
            out = dot(probs_low, values)
            d_probs = dot_nt(jnp.where(mine, grad, 0.0).astype(BF16), values)
            d_values = dot_tn(probs_low, grad)
            inner = jnp.sum(probs * d_probs, axis=1, keepdims=True)
            d_scores = (probs * (d_probs - inner)).astype(BF16)
            d_query = dot(d_scores, k_rot) * scale
            d_keys = dot_tn(d_scores, q_rot) * scale
            results.append((out, d_query, d_keys, d_values))
        out, d_query, d_keys, d_values = (
            jnp.where(lower, first, second) for first, second in zip(*results)
        )
        o_ref[:, cols] = out.astype(BF16)
        for spot, value in (
            (cols, turn(d_query, -1.0)),
            (k_cols, turn(d_keys, -1.0)),
            (v_cols, d_values),
        ):
            low = value.astype(BF16)
            dqkv_ref[:, spot] = low
            bias_ref[0, :, spot] = jnp.sum(low.astype(F32), axis=0, keepdims=True)


def attention(qkv, dpo, lengths, tables):
    slots = lengths.shape[0]
    rows = qkv.shape[0] // slots
    wide, width = qkv.shape[1], dpo.shape[1]
    table = pl.BlockSpec((rows, 2 * HEAD), lambda i, lens: (0, 0))
    return pl.pallas_call(
        attention_kernel,
        grid_spec=pltpu.PrefetchScalarGridSpec(
            num_scalar_prefetch=1,
            grid=(slots,),
            in_specs=[
                pl.BlockSpec((rows, wide), lambda i, lens: (i, 0)),
                pl.BlockSpec((rows, width), lambda i, lens: (i, 0)),
                table,
                table,
                table,
            ],
            out_specs=[
                pl.BlockSpec((rows, width), lambda i, lens: (i, 0)),
                pl.BlockSpec((rows, wide), lambda i, lens: (i, 0)),
                pl.BlockSpec((1, 1, wide), lambda i, lens: (i, 0, 0)),
            ],
        ),
        out_shape=[
            jax.ShapeDtypeStruct((qkv.shape[0], width), BF16),
            jax.ShapeDtypeStruct((qkv.shape[0], wide), BF16),
            jax.ShapeDtypeStruct((slots, 1, wide), F32),
        ],
        compiler_params=pltpu.CompilerParams(vmem_limit_bytes=40 * 2**20),
        name="attention",
    )(lengths, qkv, dpo, *tables)


def normalize(block_rows, gain_row, shift_row):
    row_mean = jnp.mean(block_rows, axis=-1, keepdims=True)
    centered = block_rows - row_mean
    inv_std = lax.rsqrt(jnp.mean(centered * centered, axis=-1, keepdims=True) + norm_eps)
    scaled = centered * inv_std
    return (scaled * gain_row + shift_row, scaled, inv_std)


def adam_update(weight, gradient, first_moment, second_moment, step_rate, decay):
    moment_new = beta_one * first_moment + (1.0 - beta_one) * gradient
    square_new = beta_two * second_moment + (1.0 - beta_two) * gradient * gradient
    moment_hat = moment_new / (1.0 - beta_one**STEP)
    square_hat = square_new / (1.0 - beta_two**STEP)
    weight_new = weight - step_rate * (
        moment_hat / (jnp.sqrt(square_hat) + adam_eps) + decay * weight
    )
    return (weight_new, moment_new, square_new)


def bits(count):
    found = []
    step = 1
    while step < count:
        found.append(step)
        step *= 2
    return found


def per_device(
    sizes,
    tokens,
    cotangent,
    lengths,
    w_qkv,
    w_out,
    w_gate_up,
    w_down,
    vectors,
    first_qkv,
    first_out,
    first_gate_up,
    first_down,
    first_vectors,
    second_qkv,
    second_out,
    second_gate_up,
    second_down,
    second_vectors,
):
    n_a, n_t, n_b, n_y = sizes
    total = n_a * n_t * n_b * n_y
    at_a, at_t, at_b, at_y = (lax.axis_index(name) for name in AXES)
    row_count, width = tokens.shape
    w_rows = w_qkv.shape[0]
    d_rows = w_down.shape[0]
    half = w_out.shape[1]

    def swap(value, name, step):
        mask = {"y": 1, "b": n_y, "t": n_y * n_b, "a": n_y * n_b * n_t}[name] * step
        return lax.ppermute(value, AXES, [(i, i ^ mask) for i in range(total)])

    n_blocks = w_qkv.shape[1] // (n_t * n_b * w_rows)
    head_cols = n_b * w_rows
    ff_cols = n_b * d_rows
    qkv_low = w_qkv.astype(BF16).reshape(w_rows, n_blocks, n_t, head_cols)
    gu_low = w_gate_up.astype(BF16).reshape(w_rows, n_a, n_t, ff_cols)
    qkv_part = qkv_low.transpose(2, 0, 1, 3).reshape(n_t, w_rows, n_blocks * head_cols)
    gu_part = gu_low.transpose(2, 0, 1, 3).reshape(n_t, w_rows, n_a * ff_cols)
    joined = jnp.concatenate([qkv_part, gu_part], axis=2)
    joined = lax.all_to_all(joined, "t", split_axis=0, concat_axis=0, tiled=True)
    qkv_own, gu_own = joined[:, :, : qkv_part.shape[2]], joined[:, :, qkv_part.shape[2] :]

    r_bits = [("a", s) for s in reversed(bits(n_a))] + [("b", s) for s in bits(n_b)]

    def gather_rows(part):
        part = part[None, :, None]
        for name, step in r_bits:
            other = swap(part, name, step)
            dim, at, size = (0, at_a, part.shape[0]) if name == "a" else (2, at_b, part.shape[2])
            upper = (at // step) % 2 == 1
            first, second = jnp.where(upper, other, part), jnp.where(upper, part, other)
            if name == "a":
                part = jnp.concatenate([first, second], axis=0)
            else:
                part = jnp.concatenate([first, second], axis=2)
        return part

    upper_y = at_y == 1

    def both(own):
        other = swap(own, "y", 1)
        return own, other

    def ordered(own, other):
        return jnp.where(upper_y, other, own), jnp.where(upper_y, own, other)

    def full_rows(part):
        return gather_rows(part).reshape(width, part.shape[-1])

    def pair_of(part):
        parts = [part[None, :, None]]
        masks = [{"a": 0, "b": 0}]
        for name, step in r_bits:
            parts = parts + [swap(p, name, step) for p in parts]
            masks = masks + [{**m, name: m[name] + step} for m in masks]
        others = [swap(p, "y", 1) for p in parts]
        return place(parts, masks), place(others, masks)

    def place(parts, masks):
        table = {(m["a"], m["b"]): p for m, p in zip(masks, parts)}
        for name, step in r_bits:
            at = at_a if name == "a" else at_b
            upper = (at // step) % 2 == 1
            fresh = {}
            for (ka, kb), value in table.items():
                mate = (ka ^ step, kb) if name == "a" else (ka, kb ^ step)
                fresh[(ka, kb)] = jnp.where(upper, table[mate], value)
            table = fresh
        return jnp.concatenate(
            [
                jnp.concatenate([table[(ka, kb)] for kb in range(n_b)], axis=2)
                for ka in range(n_a)
            ],
            axis=0,
        )

    def flat(value):
        return value.reshape(-1, value.shape[-1])

    gu_mine, gu_other = (flat(v) for v in pair_of(gu_own))
    down_mine, down_other = (flat(v) for v in pair_of(w_down.astype(BF16)[None]))
    qkv_mine, qkv_other = (flat(v) for v in pair_of(qkv_own))
    out_mine, out_other = (flat(v) for v in pair_of(w_out.astype(BF16)[None]))
    down_full = jnp.concatenate(ordered(down_mine, down_other), axis=1)
    qkv_full = jnp.concatenate(ordered(qkv_mine, qkv_other), axis=1)
    out_full = jnp.concatenate(ordered(out_mine, out_other), axis=1)

    grads = lax.all_gather(cotangent, "t", axis=0, tiled=True)
    all_vectors = lax.all_gather(vectors, AXES, axis=1, tiled=True)
    gain_row = all_vectors[0]
    shift_row = all_vectors[1]
    normed_own, scaled_own, inv_own = normalize(tokens.astype(F32), gain_row, shift_row)
    normed = lax.all_gather(normed_own.astype(BF16), "t", axis=0, tiled=True)
    group_lengths = lax.all_gather(lengths[0], "t", axis=0, tiled=False)
    slot_lengths = lax.dynamic_index_in_dim(group_lengths, at_y, 1, keepdims=False)
    bias = all_vectors[2:5].reshape(3 * n_a, n_t, head_cols)
    bias = lax.dynamic_index_in_dim(bias, at_t, 1, keepdims=False).reshape(1, -1)

    joined_mine, joined_other = dot(normed, gu_mine), dot(normed, gu_other)
    gate, up = ordered(joined_mine, joined_other)
    d_hidden = dot_nt(grads, down_full)
    sig = jax.nn.sigmoid(gate)
    act = gate * sig
    hidden = (act * up).astype(BF16)
    d_gate = (d_hidden * up * sig * (1.0 + gate * (1.0 - sig))).astype(BF16)
    d_up = (d_hidden * act).astype(BF16)
    d_mine, d_other = ordered(d_gate, d_up)

    qkv = dot(normed, qkv_full) + bias
    dpo = dot_nt(grads, out_full).astype(BF16)
    attended, d_qkv, bias_sums = attention(qkv, dpo, slot_lengths, rotary_lanes(row_count))

    def halves_y(value):
        kept, sent = ordered(value[:, : value.shape[1] // 2], value[:, value.shape[1] // 2 :])
        return kept, sent

    def reduce_rest(kept, sent, parts_shape):
        summed = kept + swap(sent.astype(BF16), "y", 1).astype(F32)
        summed = summed.reshape(parts_shape + (summed.shape[-1],))
        for name, step in r_bits:
            dim = 0 if name == "a" else 2
            at = at_a if name == "a" else at_b
            size = summed.shape[dim] // 2
            low_half = lax.slice_in_dim(summed, 0, size, axis=dim)
            high_half = lax.slice_in_dim(summed, size, 2 * size, axis=dim)
            upper = (at // step) % 2 == 1
            keep = jnp.where(upper, high_half, low_half)
            send = jnp.where(upper, low_half, high_half)
            summed = keep + swap(send.astype(BF16), name, step).astype(F32)
        return summed

    shape_w = (n_a, n_t, n_b, w_rows)
    g_gu = reduce_rest(dot_tn(normed, d_mine), dot_tn(normed, d_other), shape_w)
    g_down = reduce_rest(*halves_y(dot_tn(hidden, grads)), (n_a, 1, n_b, d_rows))
    g_qkv = reduce_rest(*halves_y(dot_tn(normed, d_qkv)), shape_w)
    g_out = reduce_rest(*halves_y(dot_tn(attended, grads)), (n_a, 1, n_b, w_rows))
    g_joined = jnp.concatenate([g_qkv[0, :, 0], g_gu[0, :, 0]], axis=2).astype(BF16)
    g_joined = lax.all_to_all(g_joined, "t", split_axis=0, concat_axis=0, tiled=True)
    g_qkv = g_joined[:, :, : n_blocks * head_cols].reshape(n_t, w_rows, n_blocks, head_cols)
    g_gu = g_joined[:, :, n_blocks * head_cols :].reshape(n_t, w_rows, n_a, ff_cols)
    own_qkv = g_qkv.transpose(1, 2, 0, 3).reshape(w_qkv.shape).astype(F32)
    own_gu = g_gu.transpose(1, 2, 0, 3).reshape(w_gate_up.shape).astype(F32)
    own_out = g_out.reshape(w_out.shape)
    own_down = g_down.reshape(w_down.shape)

    branch_part = dot(attended, out_full) + dot(hidden, down_full)
    normal_part = dot_nt(d_qkv, qkv_full) + dot_nt(d_mine, gu_mine) + dot_nt(d_other, gu_other)

    def scatter_rows(part, order):
        part = part.astype(BF16).reshape((2,) * len(order) + (row_count, width))
        steps = bits(n_t)
        for which in order:
            step = steps[len(order) - 1 - which]
            upper = (at_t // step) % 2 == 1
            low_half = lax.index_in_dim(part, 0, which, keepdims=True)
            high_half = lax.index_in_dim(part, 1, which, keepdims=True)
            keep = jnp.where(upper, high_half, low_half)
            send = jnp.where(upper, low_half, high_half)
            got = swap(send, "t", step)
            part = keep.astype(F32) + got.astype(F32)
            if which != order[-1]:
                part = part.astype(BF16)
        return part.reshape(row_count, width)

    n_bits = len(bits(n_t))
    order_one = [n_bits - 1] + list(range(n_bits - 1))
    order_two = [n_bits - 1] + list(reversed(range(n_bits - 1)))
    branch_own = scatter_rows(branch_part, order_one)
    normal_own = scatter_rows(normal_part, order_two)

    output = (tokens.astype(F32) + branch_own).astype(BF16)
    g_normed = normal_own
    d_scaled = g_normed * gain_row
    input_grad = cotangent.astype(F32) + inv_own * (
        d_scaled
        - jnp.mean(d_scaled, axis=-1, keepdims=True)
        - scaled_own * jnp.mean(d_scaled * scaled_own, axis=-1, keepdims=True)
    )
    g_bias = jnp.sum(bias_sums, axis=0).reshape(3 * n_a, 1, head_cols)
    here = (jnp.arange(n_t) == at_t)[None, :, None]
    g_bias = jnp.where(here, g_bias, 0.0).reshape(3, width)
    vector_part = jnp.concatenate(
        [
            jnp.sum(g_normed * scaled_own, axis=0)[None],
            jnp.sum(g_normed, axis=0)[None],
            g_bias,
        ],
        axis=0,
    )
    vector_grad = lax.psum_scatter(vector_part, AXES, scatter_dimension=1, tiled=True)

    new_qkv, moment_qkv, square_qkv = adam_update(
        w_qkv, own_qkv, first_qkv, second_qkv, rate_matrix, decay_rate
    )
    new_out, moment_out, square_out = adam_update(
        w_out, own_out, first_out, second_out, rate_matrix, decay_rate
    )
    new_gu, moment_gu, square_gu = adam_update(
        w_gate_up, own_gu, first_gate_up, second_gate_up, rate_matrix, decay_rate
    )
    new_down, moment_down, square_down = adam_update(
        w_down, own_down, first_down, second_down, rate_matrix, decay_rate
    )
    new_vec, moment_vec, square_vec = adam_update(
        vectors, vector_grad, first_vectors, second_vectors, rate_vector, 0.0
    )
    return (
        output,
        input_grad.astype(BF16),
        new_qkv,
        new_out,
        new_gu,
        new_down,
        new_vec,
        moment_qkv,
        moment_out,
        moment_gu,
        moment_down,
        moment_vec,
        square_qkv,
        square_out,
        square_gu,
        square_down,
        square_vec,
    )


def solution(mesh):
    n_dp, n_y = mesh.shape["dp"], mesh.shape["branch"]
    n_b = max(1, HEAD * n_dp // (HEADS * HEAD))
    n_t = min(SLICES, n_dp // n_b)
    sizes = (n_dp // (n_t * n_b), n_t, n_b, n_y)
    split = Mesh(mesh.devices.reshape(sizes), AXES)
    dp = ("a", "t", "b")
    rows = P(AXES, None)
    matrix = P(dp, "y")
    vector = P(None, AXES)
    weights = (matrix, matrix, matrix, matrix, vector)
    return jax.shard_map(
        functools.partial(per_device, sizes),
        mesh=split,
        in_specs=(rows, rows, P(dp, None)) + weights * 3,
        out_specs=(rows, rows) + weights * 3,
        check_vma=False,
    )
```

```python
import functools

import jax
import jax.numpy as jnp
from jax import lax
from jax.experimental import pallas as pl
from jax.experimental.pallas import tpu as pltpu
from jax.sharding import Mesh, PartitionSpec as P

HEADS = 32
HEAD = 64
ROT = 16
MB = 2
STEP = 10
SLICES = 8
LANES = 128

theta_base = 10000.0
norm_eps = 1e-05
beta_one = 0.9
beta_two = 0.95
adam_eps = 1e-08
decay_rate = 0.1
rate_matrix = 0.05
rate_vector = 1.0

AXES = ("a", "t", "b", "y")
F32 = jnp.float32
BF16 = jnp.bfloat16


def dot(left, right):
    return jnp.dot(left, right, preferred_element_type=F32)


def dot_nt(left, right):
    return lax.dot_general(left, right, (((1,), (1,)), ((), ())), preferred_element_type=F32)


def dot_tn(left, right):
    return lax.dot_general(left, right, (((0,), (0,)), ((), ())), preferred_element_type=F32)


def rotary_lanes(row_count):
    half_rot = ROT // 2
    freqs = theta_base ** (-2.0 * jnp.arange(half_rot, dtype=F32) / ROT)
    angles = jnp.arange(row_count, dtype=F32)[:, None] * freqs[None, :]
    cosine, sine = jnp.cos(angles), jnp.sin(angles)
    rest = HEAD - ROT
    one, zero, gap = (
        jnp.ones((row_count, rest), F32),
        jnp.zeros((row_count, half_rot), F32),
        jnp.zeros((row_count, rest), F32),
    )
    cos_head = jnp.concatenate([cosine, cosine, one], axis=1)
    up_head = jnp.concatenate([sine, zero, gap], axis=1)
    down_head = jnp.concatenate([zero, sine, gap], axis=1)
    return tuple(jnp.concatenate([x, x], axis=1) for x in (cos_head, up_head, down_head))


def normalize(block_rows, gain_row, shift_row):
    row_mean = jnp.mean(block_rows, axis=-1, keepdims=True)
    centered = block_rows - row_mean
    inv_std = lax.rsqrt(jnp.mean(centered * centered, axis=-1, keepdims=True) + norm_eps)
    scaled = centered * inv_std
    return (scaled * gain_row + shift_row, scaled, inv_std)


def adam_update(weight, gradient, first_moment, second_moment, step_rate, decay):
    moment_new = beta_one * first_moment + (1.0 - beta_one) * gradient
    square_new = beta_two * second_moment + (1.0 - beta_two) * gradient * gradient
    moment_hat = moment_new / (1.0 - beta_one**STEP)
    square_hat = square_new / (1.0 - beta_two**STEP)
    weight_new = weight - step_rate * (
        moment_hat / (jnp.sqrt(square_hat) + adam_eps) + decay * weight
    )
    return (weight_new, moment_new, square_new)


def bits(count):
    found = []
    step = 1
    while step < count:
        found.append(step)
        step *= 2
    return found


def params(count):
    return pltpu.CompilerParams(
        dimension_semantics=("arbitrary",) * count, vmem_limit_bytes=56 * 2**20
    )


def cost(flops, bytes_moved, transcendentals=0):
    return pl.CostEstimate(
        flops=int(flops), bytes_accessed=int(bytes_moved), transcendentals=int(transcendentals)
    )


def place(here, parts, masks, target, sems, first_sem):
    copies = []
    for n, (part, (ma, mb, my)) in enumerate(zip(parts, masks)):
        copy = pltpu.make_async_copy(
            part, target(here[0] ^ ma, here[2] ^ mb, here[3] ^ my), sems.at[first_sem + n]
        )
        copy.start()
        copies.append(copy)
    return copies


def by_rows(ref, first, count):
    return lambda a, b, y: ref.at[y, a, pl.ds(first, count), b]


def place_gu(here, parts, masks, ref, sems, first_sem):
    count = len(masks)
    copies = []
    for n in range(2):
        cut = parts[n * count].shape[0]
        target = by_rows(ref, n * (ref.shape[2] - cut), cut)
        copies += place(
            here, parts[n * count : (n + 1) * count], masks, target, sems, first_sem + n * count
        )
    return copies


def by_columns(ref, width):
    return lambda a, b, y: ref.at[a, :, b, :, pl.ds(pl.multiple_of(y * width, 128), width)]


def prep_kernel(sizes, n_blocks, head_cols, d_rows, unit, qkv, gu, qkv_out, gu_out):
    n_a, n_t, n_b, _ = sizes
    ff_cols = n_b * d_rows
    for t in range(n_t):
        for block in range(n_blocks):
            at = (block * n_t + t) * head_cols
            qkv_out[t, :, block * head_cols : (block + 1) * head_cols] = qkv[
                :, at : at + head_cols
            ].astype(BF16)
        pieces = []
        gap = jnp.zeros((gu.shape[0], unit - d_rows), F32)
        for a in range(n_a):
            for b in range(n_b):
                at = (a * n_t + t) * ff_cols + b * d_rows
                pieces += [gu[:, at : at + d_rows], gap]
        gu_out[t] = jnp.concatenate(pieces, axis=1).astype(BF16)


def prep(sizes, unit, w_qkv, w_gu, d_rows):
    n_a, n_t, n_b, _ = sizes
    rows = w_qkv.shape[0]
    head_cols = n_b * rows
    n_blocks = w_qkv.shape[1] // (n_t * head_cols)
    tile = 16
    wide_q, wide_g = n_blocks * head_cols, n_a * n_b * unit
    return pl.pallas_call(
        functools.partial(prep_kernel, sizes, n_blocks, head_cols, d_rows, unit),
        grid=(rows // tile,),
        in_specs=[
            pl.BlockSpec((tile, w_qkv.shape[1]), lambda i: (i, 0)),
            pl.BlockSpec((tile, w_gu.shape[1]), lambda i: (i, 0)),
        ],
        out_specs=[
            pl.BlockSpec((n_t, tile, wide_q), lambda i: (0, i, 0)),
            pl.BlockSpec((n_t, tile, wide_g), lambda i: (0, i, 0)),
        ],
        out_shape=[
            jax.ShapeDtypeStruct((n_t, rows, wide_q), BF16),
            jax.ShapeDtypeStruct((n_t, rows, wide_g), BF16),
        ],
        compiler_params=params(1),
        cost_estimate=cost(0, 20 * w_gu.size),
        name="prep",
    )(w_qkv, w_gu)


def adam(weight, gradient, first_moment, second_moment):
    return adam_update(weight, gradient, first_moment, second_moment, rate_matrix, decay_rate)


def finish_gu_kernel(sizes, d_rows, unit, g, w, m, v, w_out, m_out, v_out):
    n_a, n_t, n_b, _ = sizes
    pieces = []
    for a in range(n_a):
        for t in range(n_t):
            for b in range(n_b):
                at = (a * n_b + b) * unit
                pieces.append(g[t, :, at : at + d_rows].astype(F32))
    grad = jnp.concatenate(pieces, axis=1)
    w_out[...], m_out[...], v_out[...] = adam(w[...], grad, m[...], v[...])


def finish_qkv_kernel(sizes, head_cols, g, w, m, v, w_out, m_out, v_out):
    n_t = sizes[1]
    for block in range(w.shape[1] // (n_t * head_cols)):
        for t in range(n_t):
            at = (block * n_t + t) * head_cols
            cols = slice(at, at + head_cols)
            tile, lane = block * head_cols // LANES, block * head_cols % LANES
            grad = g[t, tile, :, lane : lane + head_cols].astype(F32)
            w_out[:, cols], m_out[:, cols], v_out[:, cols] = adam(
                w[:, cols], grad, m[:, cols], v[:, cols]
            )


def finish(kernel, name, gradient, weight, first, second):
    tile = 16
    rows, cols = weight.shape
    matrix = pl.BlockSpec((tile, cols), lambda i: (i, 0))
    lead, lanes = gradient.shape[:-2], gradient.shape[-1]
    gradient_block = pl.BlockSpec(
        lead + (tile, lanes), lambda i: (0,) * len(lead) + (i, 0)
    )
    return pl.pallas_call(
        kernel,
        grid=(rows // tile,),
        in_specs=[
            gradient_block,
            matrix,
            matrix,
            matrix,
        ],
        out_specs=[matrix] * 3,
        out_shape=[jax.ShapeDtypeStruct(weight.shape, F32)] * 3,
        compiler_params=params(1),
        cost_estimate=cost(20 * weight.size, 26 * weight.size),
        name=name,
    )(gradient, weight, first, second)


ANYWHERE = pl.BlockSpec(memory_space=pl.ANY)


def mlp_kernel(masks, steps, here, vec, x_even, x_odd, dy_even, dy_odd, *rest):
    count = len(masks)
    gu_parts, down_parts = rest[: 2 * count], rest[2 * count : 3 * count]
    normed, grads_out, hidden, d_joined, gu, down, rows, sems, row_sems = rest[-9:]
    step = pl.program_id(0)
    slot = normed.shape[0]

    def fetch(n):
        spot = pl.ds(n // 2 * slot, slot)
        sources = (x_odd, dy_odd) if n % 2 else (x_even, dy_even)
        return [
            pltpu.make_async_copy(
                source.at[spot], rows.at[n % 2, pl.ds(m * slot, slot)], row_sems.at[n % 2, m]
            )
            for m, source in enumerate(sources)
        ]

    @pl.when(step == 0)
    def _():
        for copy in fetch(0):
            copy.start()
        copies = place_gu(here, gu_parts, masks, gu, sems, 0)
        target = by_columns(down, down.shape[4] // 2)
        copies += place(here, down_parts, masks, target, sems, 2 * count)
        for copy in copies:
            copy.wait()

    for n in range(steps):

        @pl.when(step == n)
        def _(n=n):
            if n + 1 < steps:
                for copy in fetch(n + 1):
                    copy.start()
            for copy in fetch(n):
                copy.wait()

    now = step % 2
    low = normalize(rows[now, :slot].astype(F32), vec[0:1], vec[1:2])[0].astype(BF16)
    dy = rows[now, slot:]
    normed[...] = low
    grads_out[...] = dy
    wide = gu.shape[5]
    gate = dot(low, gu[0].reshape(-1, wide))
    up = dot(low, gu[1].reshape(-1, wide))
    d_hidden = dot_nt(dy, down[...].reshape(wide, -1))
    sig = jax.nn.sigmoid(gate)
    act = gate * sig
    hidden[...] = (act * up).astype(BF16)
    d_joined[0] = (d_hidden * up * sig * (1.0 + gate * (1.0 - sig))).astype(BF16)
    d_joined[1] = (d_hidden * act).astype(BF16)


def mlp(here, masks, held, vec, gu_parts, down_parts, sizes, unit):
    n_a, n_t, n_b, n_y = sizes
    width = held[0].shape[1]
    slot = held[0].shape[0] * 2 // n_t
    wide = n_a * n_b * unit
    rows = n_t * slot
    w_rows = gu_parts[0].shape[1]
    return pl.pallas_call(
        functools.partial(mlp_kernel, masks, n_t),
        grid_spec=pltpu.PrefetchScalarGridSpec(
            num_scalar_prefetch=1,
            grid=(n_t,),
            in_specs=[pl.BlockSpec(vec.shape, lambda i, h: (0, 0))]
            + [ANYWHERE] * (3 * len(masks) + 4),
            out_specs=[
                pl.BlockSpec((slot, width), lambda i, h: (i, 0)),
                pl.BlockSpec((slot, width), lambda i, h: (i, 0)),
                pl.BlockSpec((slot, wide), lambda i, h: (i, 0)),
                pl.BlockSpec((2, slot, wide), lambda i, h: (0, i, 0)),
            ],
            scratch_shapes=[
                pltpu.VMEM((n_y, n_a, n_t, n_b, w_rows, wide), BF16),
                pltpu.VMEM((n_a, 1, n_b, unit, width), BF16),
                pltpu.VMEM((2, 2 * slot, width), BF16),
                pltpu.SemaphoreType.DMA((3 * len(masks),)),
                pltpu.SemaphoreType.DMA((2, 2)),
            ],
        ),
        out_shape=[
            jax.ShapeDtypeStruct((rows, width), BF16),
            jax.ShapeDtypeStruct((rows, width), BF16),
            jax.ShapeDtypeStruct((rows, wide), BF16),
            jax.ShapeDtypeStruct((2, rows, wide), BF16),
        ],
        compiler_params=params(1),
        name="mlp",
    )(here, vec, *held, *gu_parts, *down_parts)


def attention_kernel(
    masks, here, lengths, normed, dy, bias, cos_ref, up_ref, down_ref, *rest
):
    count = len(masks)
    qkv_parts, out_parts = rest[:count], rest[count : 2 * count]
    o_ref, dqkv_ref, bias_ref, w_qkv, w_out, sems = rest[2 * count :]

    @pl.when(pl.program_id(0) == 0)
    def _():
        copies = place(here, qkv_parts, masks, by_columns(w_qkv, w_qkv.shape[4] // 2), sems, 0)
        copies += place(here, out_parts, masks, by_columns(w_out, w_out.shape[4] // 2), sems, count)
        for copy in copies:
            copy.wait()

    rows = normed.shape[0]
    wide = w_qkv.shape[4]
    width = wide // 3
    qkv = dot(normed[...], w_qkv[...].reshape(-1, wide)) + bias[...]
    dpo = dot_nt(dy[...], w_out[...].reshape(width, -1)).astype(BF16)
    length = lengths[pl.program_id(0)]
    cosine, sine_up, sine_down = cos_ref[...], up_ref[...], down_ref[...]
    query_at = lax.broadcasted_iota(jnp.int32, (rows, rows), 0)
    key_at = lax.broadcasted_iota(jnp.int32, (rows, rows), 1)
    allowed = (key_at <= query_at) & (key_at < length)
    lane = lax.broadcasted_iota(jnp.int32, (rows, 2 * HEAD), 1)
    lower = lane < HEAD
    half = ROT // 2
    scale = HEAD ** (-0.5)

    def turn(x, sign):
        ahead = pltpu.roll(x, 2 * HEAD - half, 1)
        behind = pltpu.roll(x, half, 1)
        return x * cosine + sign * (behind * sine_down - ahead * sine_up)

    for pair in range(width // (2 * HEAD)):
        at = pair * 2 * HEAD
        cols = slice(at, at + 2 * HEAD)
        k_cols = slice(width + at, width + at + 2 * HEAD)
        v_cols = slice(2 * width + at, 2 * width + at + 2 * HEAD)
        q_rot = turn(qkv[:, cols], 1.0).astype(BF16)
        k_rot = turn(qkv[:, k_cols], 1.0).astype(BF16)
        values = qkv[:, v_cols].astype(BF16)
        grad = dpo[:, cols]
        results = []
        for side in range(2):
            mine = lower if side == 0 else ~lower
            scores = dot_nt(jnp.where(mine, q_rot, 0.0).astype(BF16), k_rot) * scale
            masked = jnp.where(allowed, scores, -1e30)
            raised = jnp.exp(masked - jnp.max(masked, axis=1, keepdims=True))
            probs = raised * (1.0 / jnp.sum(raised, axis=1, keepdims=True))
            probs_low = probs.astype(BF16)
            out = dot(probs_low, values)
            d_probs = dot_nt(jnp.where(mine, grad, 0.0).astype(BF16), values)
            d_values = dot_tn(probs_low, grad)
            inner = jnp.sum(probs * d_probs, axis=1, keepdims=True)
            d_scores = (probs * (d_probs - inner)).astype(BF16)
            d_query = dot(d_scores, k_rot) * scale
            d_keys = dot_tn(d_scores, q_rot) * scale
            results.append((out, d_query, d_keys, d_values))
        out, d_query, d_keys, d_values = (
            jnp.where(lower, first, second) for first, second in zip(*results)
        )
        o_ref[:, cols] = out.astype(BF16)
        for spot, value in (
            (cols, turn(d_query, -1.0)),
            (k_cols, turn(d_keys, -1.0)),
            (v_cols, d_values),
        ):
            low = value.astype(BF16)
            dqkv_ref[:, spot] = low
            bias_ref[0, :, spot] = jnp.sum(low.astype(F32), axis=0, keepdims=True)


def attention(here, masks, lengths, normed, dy, bias, qkv_parts, out_parts, sizes):
    n_a, n_t, n_b, _ = sizes
    slots = lengths.shape[0]
    slot, width = dy.shape[0] // slots, dy.shape[1]
    tables = rotary_lanes(slot)
    wide = bias.shape[1]
    table = pl.BlockSpec((slot, 2 * HEAD), lambda i, h, lens: (0, 0))
    w_rows = qkv_parts[0].shape[1]
    return pl.pallas_call(
        functools.partial(attention_kernel, masks),
        grid_spec=pltpu.PrefetchScalarGridSpec(
            num_scalar_prefetch=2,
            grid=(n_t,),
            in_specs=[
                pl.BlockSpec((slot, width), lambda i, h, lens: (i, 0)),
                pl.BlockSpec((slot, width), lambda i, h, lens: (i, 0)),
                pl.BlockSpec((1, wide), lambda i, h, lens: (0, 0)),
                table,
                table,
                table,
            ]
            + [ANYWHERE] * (2 * len(masks)),
            out_specs=[
                pl.BlockSpec((slot, wide // 3), lambda i, h, lens: (i, 0)),
                pl.BlockSpec((slot, wide), lambda i, h, lens: (i, 0)),
                pl.BlockSpec((1, 1, wide), lambda i, h, lens: (i, 0, 0)),
            ],
            scratch_shapes=[
                pltpu.VMEM((n_a, n_t, n_b, w_rows, wide), BF16),
                pltpu.VMEM((n_a, 1, n_b, w_rows, width), BF16),
                pltpu.SemaphoreType.DMA((2 * len(masks),)),
            ],
        ),
        out_shape=[
            jax.ShapeDtypeStruct((n_t * slot, wide // 3), BF16),
            jax.ShapeDtypeStruct((n_t * slot, wide), BF16),
            jax.ShapeDtypeStruct((n_t, 1, wide), F32),
        ],
        compiler_params=params(1),
        cost_estimate=cost(
            4 * n_t * slot * width * wide, 5 * n_t * slot * width * 2, n_t * slot * slot * 8
        ),
        name="attention",
    )(here, lengths, normed, dy, bias, *tables, *qkv_parts, *out_parts)


def grads_cols_kernel(where, left, d_sent, d_kept, sent, kept):
    tall = left[...]
    shape = (tall.shape[0], -1)
    sent[...] = dot_tn(tall, d_sent[...].reshape(shape)).astype(BF16)
    kept[...] = dot_tn(tall, d_kept[...].reshape(shape))


def grads_cols(where, normed, d_cols, name):
    rows, width = normed.shape
    half_rows = width // 2
    steps = 4
    tile = half_rows // steps
    if d_cols.ndim == 3:
        d_half = d_cols.shape[2]
        d_specs = [
            pl.BlockSpec((1, rows, d_half), lambda i, w: (1 - w[1], 0, 0)),
            pl.BlockSpec((1, rows, d_half), lambda i, w: (w[1], 0, 0)),
        ]
    else:
        d_half = d_cols.shape[1] // 2
        d_specs = [
            pl.BlockSpec((rows, d_half), lambda i, w: (0, 1 - w[1])),
            pl.BlockSpec((rows, d_half), lambda i, w: (0, w[1])),
        ]
    return pl.pallas_call(
        grads_cols_kernel,
        grid_spec=pltpu.PrefetchScalarGridSpec(
            num_scalar_prefetch=1,
            grid=(steps,),
            in_specs=[pl.BlockSpec((rows, tile), lambda i, w: (0, w[0] * steps + i))] + d_specs,
            out_specs=[pl.BlockSpec((tile, d_half), lambda i, w: (i, 0))] * 2,
        ),
        out_shape=[
            jax.ShapeDtypeStruct((half_rows, d_half), BF16),
            jax.ShapeDtypeStruct((half_rows, d_half), F32),
        ],
        compiler_params=params(1),
        cost_estimate=cost(2 * rows * width * d_half, 2 * rows * width + 4 * rows * d_half),
        name=name,
    )(where, normed, d_cols, d_cols)


def grads_rows_kernel(where, far, near, dy_sent, dy_kept, *outs):
    sent, kept = dy_sent[...], dy_kept[...]
    outs[0][...] = dot_tn(far[...], sent).astype(BF16)
    outs[1][...] = dot_tn(far[...], kept)
    outs[2][...] = dot_tn(near[...], sent).astype(BF16)
    outs[3][...] = dot_tn(near[...], kept)


def grads_rows(where, left, dy, name):
    rows, wide = left.shape
    width = dy.shape[1]
    half, dy_half = wide // 2, width // 2
    steps = 4
    tile = dy_half // steps
    block = (rows, tile)
    return pl.pallas_call(
        grads_rows_kernel,
        grid_spec=pltpu.PrefetchScalarGridSpec(
            num_scalar_prefetch=1,
            grid=(steps,),
            in_specs=[
                pl.BlockSpec((rows, half), lambda i, w: (0, w[0])),
                pl.BlockSpec((rows, half), lambda i, w: (0, 1 - w[0])),
                pl.BlockSpec(block, lambda i, w: (0, (1 - w[1]) * steps + i)),
                pl.BlockSpec(block, lambda i, w: (0, w[1] * steps + i)),
            ],
            out_specs=[pl.BlockSpec((half, tile), lambda i, w: (0, i))] * 4,
        ),
        out_shape=[jax.ShapeDtypeStruct((half, dy_half), t) for t in (BF16, F32, BF16, F32)],
        compiler_params=params(1),
        cost_estimate=cost(2 * rows * width * wide, 2 * rows * (width + wide) + 3 * wide * width),
        name=name,
    )(where, left, left, dy, dy)


def grads_attention_kernel(where, tall, d_sent, d_kept, far, near, dy_sent, dy_kept, *outs):
    step, steps = pl.program_id(0), pl.num_programs(0)
    left = tall[...]
    tile, half = left.shape[1], far.shape[1]
    part, first = step // (steps // 2), step % (steps // 2) * tile
    for out, d_cols, dy in ((outs[0], d_sent, dy_sent), (outs[1], d_kept, dy_kept)):
        result = dot_tn(left, d_cols[...]).astype(out.dtype)
        tiles = out.shape[1] - 1
        for n in range(tiles):
            spot = pl.ds(pl.multiple_of(first, tile), tile)
            out[part, n, spot, :] = result[:, n * LANES : (n + 1) * LANES]
        spot = pl.ds(pl.multiple_of(step * half, half), half)
        columns = dy[...]
        out[0, tiles, spot, :] = dot_tn(far[...], columns).astype(out.dtype)
        out[1, tiles, spot, :] = dot_tn(near[...], columns).astype(out.dtype)


def grads_attention(where, normed, d_qkv, attended, dy):
    rows, width = normed.shape
    d_half, half, dy_half = d_qkv.shape[1] // 2, attended.shape[1] // 2, width // 2
    steps = dy_half // LANES
    tile = width // steps
    block = (rows, LANES)
    shape = (2, d_half // LANES + 1, steps * half, LANES)
    assert shape[2] == width // 2

    def tall(i, w):
        return (0, jnp.where(i < steps // 2, w[0], 1 - w[0]) * (steps // 2) + i % (steps // 2))

    return pl.pallas_call(
        grads_attention_kernel,
        grid_spec=pltpu.PrefetchScalarGridSpec(
            num_scalar_prefetch=1,
            grid=(steps,),
            in_specs=[
                pl.BlockSpec((rows, tile), tall),
                pl.BlockSpec((rows, d_half), lambda i, w: (0, 1 - w[1])),
                pl.BlockSpec((rows, d_half), lambda i, w: (0, w[1])),
                pl.BlockSpec((rows, half), lambda i, w: (0, w[0])),
                pl.BlockSpec((rows, half), lambda i, w: (0, 1 - w[0])),
                pl.BlockSpec(block, lambda i, w: (0, (1 - w[1]) * steps + i)),
                pl.BlockSpec(block, lambda i, w: (0, w[1] * steps + i)),
            ],
            out_specs=[pl.BlockSpec(shape, lambda i, w: (0, 0, 0, 0))] * 2,
        ),
        out_shape=[jax.ShapeDtypeStruct(shape, t) for t in (BF16, F32)],
        compiler_params=params(1),
        name="grads_attention",
    )(where, normed, d_qkv, d_qkv, attended, attended, dy, dy)


def row_blocks(kernel, name, here, kept, inputs, parts, scratch, slot, width, n_t):
    def slot_of(i, h):
        return i % 2 * 4 + i // 2 * 2 + (0 if kept else 1)

    in_specs = []
    for value in inputs:
        block = (slot, value.shape[-1])
        if value.ndim == 3:
            block = (value.shape[0],) + block
            in_specs.append(pl.BlockSpec(block, lambda i, h: (0, slot_of(i, h), 0)))
        else:
            in_specs.append(pl.BlockSpec(block, lambda i, h: (slot_of(i, h), 0)))
    return pl.pallas_call(
        kernel,
        grid_spec=pltpu.PrefetchScalarGridSpec(
            num_scalar_prefetch=1,
            grid=(n_t // 2,),
            in_specs=in_specs + [ANYWHERE] * len(parts),
            out_specs=pl.BlockSpec((slot, width), lambda i, h: (i, 0)),
            scratch_shapes=scratch + [pltpu.SemaphoreType.DMA((len(parts),))],
        ),
        out_shape=jax.ShapeDtypeStruct((n_t // 2 * slot, width), BF16),
        compiler_params=params(1),
        name=name + ("_kept" if kept else "_sent"),
    )(here, *inputs, *parts)


def branch_kernel(masks, here, o, hidden, *rest):
    count = len(masks)
    out_parts, down_parts = rest[:count], rest[count : 2 * count]
    out, w_out, down, sems = rest[2 * count :]

    @pl.when(pl.program_id(0) == 0)
    def _():
        copies = place(here, out_parts, masks, by_columns(w_out, w_out.shape[4] // 2), sems, 0)
        copies += place(here, down_parts, masks, by_columns(down, down.shape[4] // 2), sems, count)
        for copy in copies:
            copy.wait()

    width = w_out.shape[4]
    branch = dot(o[...], w_out[...].reshape(-1, width))
    branch += dot(hidden[...], down[...].reshape(-1, width))
    out[...] = branch.astype(BF16)


def normal_kernel(masks, here, d_qkv, d_joined, *rest):
    count = len(masks)
    qkv_parts, gu_parts = rest[:count], rest[count : 3 * count]
    out, w_qkv, gu, sems = rest[3 * count :]

    @pl.when(pl.program_id(0) == 0)
    def _():
        copies = place(here, qkv_parts, masks, by_columns(w_qkv, w_qkv.shape[4] // 2), sems, 0)
        copies += place_gu(here, gu_parts, masks, gu, sems, count)
        for copy in copies:
            copy.wait()

    wide = w_qkv.shape[4]
    width = w_qkv.size // wide
    normal = dot_nt(d_qkv[...], w_qkv[...].reshape(width, -1))
    normal += dot_nt(d_joined[0], gu[0].reshape(width, -1))
    normal += dot_nt(d_joined[1], gu[1].reshape(width, -1))
    out[...] = normal.astype(BF16)


def after(value, *others):
    return lax.optimization_barrier((value,) + others)[0]


def per_device(
    sizes,
    tokens,
    cotangent,
    lengths,
    w_qkv,
    w_out,
    w_gate_up,
    w_down,
    vectors,
    first_qkv,
    first_out,
    first_gate_up,
    first_down,
    first_vectors,
    second_qkv,
    second_out,
    second_gate_up,
    second_down,
    second_vectors,
):
    barrier = lax.optimization_barrier
    n_a, n_t, n_b, n_y = sizes
    total = n_a * n_t * n_b * n_y
    at_a, at_t, at_b, at_y = (lax.axis_index(name).astype(jnp.int32) for name in AXES)
    here = jnp.stack([at_a, at_t, at_b, at_y])
    row_count, width = tokens.shape
    w_rows = w_qkv.shape[0]
    d_rows = w_down.shape[0]
    head_cols = n_b * w_rows
    unit = d_rows
    while unit % 16 or n_a * n_b * unit % 128:
        unit += 1

    def swap(value, name, step):
        mask = {"y": 1, "b": n_y, "t": n_y * n_b, "a": n_y * n_b * n_t}[name] * step
        return lax.ppermute(value, AXES, [(i, i ^ mask) for i in range(total)])

    def exchange(value):
        return lax.all_to_all(value, "t", split_axis=0, concat_axis=0, tiled=True)

    r_bits = [("a", s) for s in reversed(bits(n_a))] + [("b", s) for s in bits(n_b)]
    masks = [(0, 0, 0)]
    for name, step in r_bits:
        masks = masks + [
            (m[0] + step * (name == "a"), m[1] + step * (name == "b"), 0) for m in masks
        ]
    masks = tuple(masks + [(m[0], m[1], 1) for m in masks])

    small = 5 * vectors.shape[1] + lengths.shape[1]
    padded = -(-small // 128) * 128
    packed = jnp.concatenate(
        [
            vectors.reshape(1, 1, -1),
            lengths.astype(F32).reshape(1, 1, -1),
            jnp.zeros((1, 1, padded - small), F32),
        ],
        axis=2,
    )
    packed = jnp.broadcast_to(packed, (total, 1, padded))
    packed = lax.all_to_all(packed, AXES, split_axis=0, concat_axis=0, tiled=True)
    packed = packed.reshape(total, padded)

    def spread_top(part):
        parts = [part]
        for name, step in r_bits:
            parts = parts + [swap(p, name, step) for p in parts]
        return parts

    def over_y(value):
        return swap(value, "y", 1)

    def over_y_rest(parts):
        return [over_y(part) for part in parts[1:]]

    def over_top(value):
        return swap(value.astype(BF16), "a", top)

    def summed(kept, *got):
        return functools.reduce(lambda one, two: one.astype(F32) + two.astype(F32), got, kept)

    top = n_a // 2
    down_own = jnp.pad(w_down.astype(BF16), ((0, unit - d_rows), (0, 0)))[None]
    out_own = w_out.astype(BF16)[None]
    qkv_own, gu_own = prep(sizes, unit, w_qkv, w_gate_up, d_rows)
    x_top, x_middle, qkv_own, gu_own, down_own, out_own, packed = barrier(
        (
            swap(tokens, "t", n_t // 2),
            swap(tokens, "t", n_t // 4),
            qkv_own,
            gu_own,
            down_own,
            out_own,
            packed,
        )
    )

    gu_own, down_parts, down_other, x_far, cotangent = barrier(
        (
            exchange(gu_own),
            spread_top(down_own),
            over_y(down_own),
            swap(x_top, "t", n_t // 4),
            cotangent,
        )
    )
    cut = n_t // 2
    gu_first, gu_second = barrier((gu_own[:cut], gu_own[cut:]))
    gu_parts, gu_other, down_far, dy_top, dy_middle, gu_second, qkv_own = barrier(
        (
            spread_top(gu_first),
            over_y(gu_first),
            over_y_rest(down_parts),
            swap(cotangent, "t", n_t // 2),
            swap(cotangent, "t", n_t // 4),
            gu_second,
            qkv_own,
        )
    )
    down_parts = down_parts + [down_other] + down_far
    x_even = jnp.concatenate([tokens, x_middle, x_top, x_far], axis=0)
    gu_two, gu_two_other, gu_far, dy_far, x_odd, qkv_own = barrier(
        (
            spread_top(gu_second),
            over_y(gu_second),
            over_y_rest(gu_parts),
            swap(dy_top, "t", n_t // 4),
            swap(x_even, "t", 1),
            qkv_own,
        )
    )
    dy_even = jnp.concatenate([cotangent, dy_middle, dy_top, dy_far], axis=0)
    gu_two_far, qkv_own, dy_odd = barrier(
        (over_y_rest(gu_two), exchange(qkv_own), swap(dy_even, "t", 1))
    )
    gu_parts = gu_parts + [gu_other] + gu_far + gu_two + [gu_two_other] + gu_two_far

    all_vectors = packed[:, : 5 * vectors.shape[1]].reshape(total, 5, -1)
    all_vectors = all_vectors.transpose(1, 0, 2).reshape(5, width)
    group = packed[:, 5 * vectors.shape[1] : small].reshape(n_a, n_t, n_b, n_y, -1)
    group = lax.dynamic_index_in_dim(group, at_a, 0, keepdims=False)
    group = lax.dynamic_index_in_dim(group, at_b, 1, keepdims=False)
    group = jnp.where(at_y == 1, group[:, 0, 1], group[:, 0, 0])
    group = group.reshape(2, 2, 2)
    for dim, step in enumerate((4, 2, 1)):
        group = jnp.where(at_t // step % 2 == 1, jnp.flip(group, dim), group)
    slot_lengths = jnp.round(group.reshape(-1)).astype(jnp.int32)
    gain_row = all_vectors[0]
    bias = all_vectors[2:5].reshape(3 * n_a, n_t, head_cols)
    bias = lax.dynamic_index_in_dim(bias, at_t, 1, keepdims=False).reshape(1, -1)

    top = n_a // 2
    upper = at_a // top % 2
    other_half = jnp.stack([1 - upper, at_y])
    own_half = jnp.stack([upper, at_y])
    lower_bits = r_bits[1:]

    def over_rest(value, parts_shape):
        summed = value.reshape(parts_shape + (value.shape[-1],))
        for name, step in lower_bits:
            dim = 0 if name == "a" else 2
            at = at_a if name == "a" else at_b
            size = summed.shape[dim] // 2
            low_half = lax.slice_in_dim(summed, 0, size, axis=dim)
            high_half = lax.slice_in_dim(summed, size, 2 * size, axis=dim)
            is_upper = (at // step) % 2 == 1
            keep = jnp.where(is_upper, high_half, low_half)
            send = jnp.where(is_upper, low_half, high_half)
            summed = keep + swap(send.astype(BF16), name, step).astype(F32)
        return summed.reshape(summed.shape[1], summed.shape[3], summed.shape[4])

    def first_sums(got, kept):
        shape = (2, 2, row_count, width)
        both = got.reshape(shape).astype(F32) + kept.reshape(shape).astype(F32)
        left, right = both[..., :half_width], both[..., half_width:]
        return [v.astype(BF16) for v in (left[0], left[1], right[:, 0], right[:, 1])]

    def second_sums(left_kept, left_got, right_kept, right_got):
        sums = []
        for kept, got in ((left_kept, left_got), (right_kept, right_got)):
            both = (kept.astype(F32) + got.astype(F32)).astype(BF16)
            sums += [both[0], both[1]]
        return sums

    def third_sums(left_kept, left_got, right_kept, right_got):
        left = left_kept.astype(F32) + left_got.astype(F32)
        return jnp.concatenate([left, right_kept.astype(F32) + right_got.astype(F32)], axis=1)

    half_width = width // 2
    shape_w = (top, n_t, n_b, w_rows)
    normed, dy, hidden, d_joined = mlp(
        after(here, qkv_own),
        masks,
        (x_even, x_odd, dy_even, dy_odd),
        all_vectors[:2],
        gu_parts,
        down_parts,
        sizes,
        unit,
    )
    qkv_parts, qkv_other, out_parts, out_other, normed, dy, hidden, d_joined = barrier(
        (
            spread_top(qkv_own),
            over_y(qkv_own),
            spread_top(out_own),
            over_y(out_own),
            normed,
            dy,
            hidden,
            d_joined,
        )
    )

    qkv_far, out_far = over_y_rest(qkv_parts), over_y_rest(out_parts)
    down_far_sent, down_far_kept, down_sent, down_kept = grads_rows(
        other_half, hidden, dy, "grads_down"
    )
    gu_far_sent, gu_far_kept = grads_cols(
        after(other_half, down_kept), normed, d_joined, "grads_gate_up_far"
    )
    down_far_got = over_y(down_far_sent)
    gu_sent, gu_kept = grads_cols(
        after(own_half, gu_far_kept), normed, d_joined, "grads_gate_up_near"
    )
    qkv_far, out_far, down_far_got, gu_far_sent, down_sent, gu_sent, gu_kept = barrier(
        (qkv_far, out_far, down_far_got, gu_far_sent, down_sent, gu_sent, gu_kept)
    )
    qkv_parts = qkv_parts + [qkv_other] + qkv_far
    out_parts = out_parts + [out_other] + out_far

    down_far = barrier(summed(down_far_kept, down_far_got).astype(BF16))
    attended, d_qkv, bias_sums = attention(
        after(here, down_far),
        masks,
        slot_lengths,
        normed,
        dy,
        bias,
        qkv_parts,
        out_parts,
        sizes,
    )
    gu_rows = gu_sent.shape[0] // 2
    down_far_got, gu_far_got, down_sent, gu_sent, attended, d_qkv = barrier(
        (
            over_top(down_far),
            over_y(gu_far_sent),
            down_sent,
            (gu_sent[:gu_rows], gu_sent[gu_rows:]),
            attended,
            d_qkv,
        )
    )

    def quarters(value):
        value = value.reshape(value.shape[0] // (n_b * w_rows), n_b * w_rows, -1)
        part = value.shape[1] // 4
        return [value[:, n * part : (n + 1) * part] for n in range(4)]

    gu_far = [summed(k, g).astype(BF16) for k, g in zip(quarters(gu_far_kept), quarters(gu_far_got))]
    gu_far = barrier(gu_far)
    qo_sent, qo_kept = grads_attention(after(other_half, *gu_far), normed, d_qkv, attended, dy)
    gu_far_one, gu_got, gu_far, qo_far_sent, qo_sent = barrier(
        (
            over_top(gu_far[0]),
            over_y(gu_sent[0]),
            gu_far,
            (qo_sent[0, :2], qo_sent[0, 2:]),
            qo_sent[1],
        )
    )

    branch_rows = functools.partial(
        row_blocks,
        functools.partial(branch_kernel, masks),
        "branch_rows",
        inputs=(attended, hidden),
        parts=out_parts + down_parts,
        scratch=[
            pltpu.VMEM((n_a, 1, n_b, w_rows, width), BF16),
            pltpu.VMEM((n_a, 1, n_b, unit, width), BF16),
        ],
        slot=row_count,
        width=width,
        n_t=n_t,
    )
    branch_sent = branch_rows(after(here, *qo_far_sent), False)
    gu_far_two, qo_far_got, branch_sent, gu_far, qo_far_sent = barrier(
        (over_top(gu_far[1]), over_y(qo_far_sent[0]), branch_sent, gu_far, qo_far_sent[1])
    )
    branch_kept = branch_rows(after(here, branch_sent), True)
    gu_far_three, branch_got, qo_far_more, branch_kept, gu_far = barrier(
        (
            over_top(gu_far[2]),
            swap(branch_sent, "t", 1),
            over_y(qo_far_sent),
            branch_kept,
            gu_far,
        )
    )

    branch = barrier(first_sums(branch_got, branch_kept))
    normal_rows = functools.partial(
        row_blocks,
        functools.partial(normal_kernel, masks),
        "normal_rows",
        inputs=(d_qkv, d_joined),
        parts=qkv_parts + gu_parts,
        scratch=[
            pltpu.VMEM((n_a, n_t, n_b, w_rows, d_qkv.shape[1]), BF16),
            pltpu.VMEM((n_y, n_a, n_t, n_b, w_rows, n_a * n_b * unit), BF16),
        ],
        slot=row_count,
        width=width,
        n_t=n_t,
    )
    normal_sent = normal_rows(after(here, *branch), False)
    branch_got = [swap(branch[1], "t", 2), swap(branch[3], "t", 4)]
    qo_far_got = jnp.concatenate([qo_far_got, qo_far_more], axis=0)
    qo_far = summed(qo_kept[0], qo_far_got).astype(BF16)
    qo_far = (qo_far[:2], qo_far[2:])
    gu_far_four, gu_got_more, branch_got, normal_sent, qo_far, qo_sent, down_sent = barrier(
        (
            over_top(gu_far[3]),
            over_y(gu_sent[1]),
            branch_got,
            normal_sent,
            qo_far,
            qo_sent,
            down_sent,
        )
    )
    gu_got = jnp.concatenate([gu_got, gu_got_more], axis=0)
    gu_far_got = jnp.concatenate([gu_far_one, gu_far_two, gu_far_three, gu_far_four], axis=1)
    g_gu = summed(gu_kept, gu_got, gu_far_got.reshape(gu_kept.shape))
    g_gu = over_rest(g_gu, shape_w).astype(BF16)
    g_gu, qo_far = barrier((g_gu, qo_far))
    normal_kept = normal_rows(after(here, normal_sent, g_gu), True)
    qo_far_got, down_sent, normal_got, g_gu, normal_kept, qo_far, qo_got = barrier(
        (
            over_top(qo_far[0]),
            down_sent,
            swap(normal_sent, "t", 1),
            exchange(g_gu),
            normal_kept,
            qo_far[1],
            over_y(qo_sent),
        )
    )

    qo_far_more, down_got = over_top(qo_far), over_y(down_sent)
    normal = barrier(first_sums(normal_got, normal_kept))
    normal_got = [swap(normal[1], "t", 2), swap(normal[3], "t", 4)]
    branch = second_sums(branch[0], branch_got[0], branch[2], branch_got[1])
    branch = [after(part, *normal) for part in branch]
    new_gu, moment_gu, square_gu = finish(
        functools.partial(finish_gu_kernel, sizes, d_rows, unit),
        "finish_gate_up",
        after(g_gu, *branch),
        w_gate_up,
        first_gate_up,
        second_gate_up,
    )
    normal_got, qo_far_more, down_got, branch, new_gu = barrier(
        (normal_got, qo_far_more, down_got, branch, new_gu)
    )

    normal = barrier(second_sums(normal[0], normal_got[0], normal[2], normal_got[1]))
    normal_got = [swap(normal[1], "t", 4), swap(normal[3], "t", 2)]
    branch = barrier([after(part, *normal) for part in branch])
    branch_got = [swap(branch[1], "t", 4), swap(branch[3], "t", 2)]
    qo_far_got = jnp.concatenate([qo_far_got, qo_far_more], axis=0)
    qo = after(summed(qo_kept[1], qo_got, qo_far_got), *normal)
    g_qkv = over_rest(qo[:-1].transpose(1, 0, 2).reshape(qo.shape[1], -1), shape_w)
    g_out = qo[-1].reshape(half_width // LANES, -1, LANES).transpose(1, 0, 2)
    g_out = over_rest(g_out.reshape(-1, half_width), (top, 1, n_b, w_rows))
    g_qkv = g_qkv.astype(BF16).reshape(n_t, w_rows, -1, LANES).transpose(0, 2, 1, 3)
    g_qkv = barrier(g_qkv)
    g_down = summed(down_kept, down_got, down_far_got)
    g_down = over_rest(after(g_down, g_qkv), (top, 1, n_b, unit))
    new_down, moment_down, square_down = adam(w_down, g_down[0, :d_rows], first_down, second_down)
    g_qkv, normal_got, g_out, branch_got, new_down = barrier(
        (exchange(g_qkv), normal_got, g_out, branch_got, new_down)
    )
    normal_own = third_sums(normal[0], normal_got[0], normal[2], normal_got[1])
    _, scaled_own, inv_own = normalize(tokens.astype(F32), gain_row, all_vectors[1])
    d_scaled = normal_own * gain_row
    input_grad = cotangent.astype(F32) + inv_own * (
        d_scaled
        - jnp.mean(d_scaled, axis=-1, keepdims=True)
        - scaled_own * jnp.mean(d_scaled * scaled_own, axis=-1, keepdims=True)
    )
    g_bias = jnp.sum(bias_sums, axis=0).reshape(3 * n_a, 1, head_cols)
    is_here = (jnp.arange(n_t) == at_t)[None, :, None]
    g_bias = jnp.where(is_here, g_bias, 0.0).reshape(3, width)
    vector_part = jnp.concatenate(
        [
            jnp.sum(normal_own * scaled_own, axis=0)[None],
            jnp.sum(normal_own, axis=0)[None],
            g_bias,
        ],
        axis=0,
    )
    vector_part = vector_part.reshape(5, total, -1).transpose(1, 0, 2).reshape(total, 1, -1)
    vector_part = jnp.pad(vector_part, ((0, 0), (0, 0), (0, -vector_part.shape[2] % 128)))
    vector_part = lax.all_to_all(vector_part, AXES, split_axis=0, concat_axis=0, tiled=True)
    vector_grad = jnp.sum(vector_part, axis=0)[0, : vectors.size].reshape(vectors.shape)
    branch_own = third_sums(branch[0], branch_got[0], branch[2], branch_got[1])
    output = (tokens.astype(F32) + after(branch_own, vector_part)).astype(BF16)
    new_out, moment_out, square_out = adam(w_out, g_out[0], first_out, second_out)
    new_qkv, moment_qkv, square_qkv = finish(
        functools.partial(finish_qkv_kernel, sizes, head_cols),
        "finish_qkv",
        g_qkv,
        w_qkv,
        first_qkv,
        second_qkv,
    )
    new_vec, moment_vec, square_vec = adam_update(
        vectors, vector_grad, first_vectors, second_vectors, rate_vector, 0.0
    )
    return (
        output,
        input_grad.astype(BF16),
        new_qkv,
        new_out,
        new_gu,
        new_down,
        new_vec,
        moment_qkv,
        moment_out,
        moment_gu,
        moment_down,
        moment_vec,
        square_qkv,
        square_out,
        square_gu,
        square_down,
        square_vec,
    )


def solution(mesh):
    n_dp, n_y = mesh.shape["dp"], mesh.shape["branch"]
    n_b = max(1, HEAD * n_dp // (HEADS * HEAD))
    n_t = min(SLICES, n_dp // n_b)
    sizes = (n_dp // (n_t * n_b), n_t, n_b, n_y)
    split = Mesh(mesh.devices.reshape(sizes), AXES)
    dp = ("a", "t", "b")
    rows = P(AXES, None)
    matrix = P(dp, "y")
    vector = P(None, AXES)
    weights = (matrix, matrix, matrix, matrix, vector)
    return jax.shard_map(
        functools.partial(per_device, sizes),
        mesh=split,
        in_specs=(rows, rows, P(dp, None)) + weights * 3,
        out_specs=(rows, rows) + weights * 3,
        check_vma=False,
    )
```

```python
import functools

import jax
import jax.numpy as jnp
from jax import lax
from jax.experimental import pallas as pl
from jax.experimental.pallas import tpu as pltpu
from jax.sharding import Mesh, PartitionSpec as P

HEADS = 32
HEAD = 64
ROT = 16
MB = 2
STEP = 10
SLICES = 8
LANES = 128

theta_base = 10000.0
norm_eps = 1e-05
beta_one = 0.9
beta_two = 0.95
adam_eps = 1e-08
decay_rate = 0.1
rate_matrix = 0.05
rate_vector = 1.0

AXES = ("a", "t", "b", "y")
F32 = jnp.float32
BF16 = jnp.bfloat16


def dot(left, right):
    return jnp.dot(left, right, preferred_element_type=F32)


def dot_nt(left, right):
    return lax.dot_general(left, right, (((1,), (1,)), ((), ())), preferred_element_type=F32)


def dot_tn(left, right):
    return lax.dot_general(left, right, (((0,), (0,)), ((), ())), preferred_element_type=F32)


def rotary_lanes(row_count):
    half_rot = ROT // 2
    freqs = theta_base ** (-2.0 * jnp.arange(half_rot, dtype=F32) / ROT)
    angles = jnp.arange(row_count, dtype=F32)[:, None] * freqs[None, :]
    cosine, sine = jnp.cos(angles), jnp.sin(angles)
    rest = HEAD - ROT
    one, zero, gap = (
        jnp.ones((row_count, rest), F32),
        jnp.zeros((row_count, half_rot), F32),
        jnp.zeros((row_count, rest), F32),
    )
    cos_head = jnp.concatenate([cosine, cosine, one], axis=1)
    up_head = jnp.concatenate([sine, zero, gap], axis=1)
    down_head = jnp.concatenate([zero, sine, gap], axis=1)
    return tuple(jnp.concatenate([x, x], axis=1) for x in (cos_head, up_head, down_head))


def normalize(block_rows, gain_row, shift_row):
    row_mean = jnp.mean(block_rows, axis=-1, keepdims=True)
    centered = block_rows - row_mean
    inv_std = lax.rsqrt(jnp.mean(centered * centered, axis=-1, keepdims=True) + norm_eps)
    scaled = centered * inv_std
    return (scaled * gain_row + shift_row, scaled, inv_std)


def adam_update(weight, gradient, first_moment, second_moment, step_rate, decay):
    moment_new = beta_one * first_moment + (1.0 - beta_one) * gradient
    square_new = beta_two * second_moment + (1.0 - beta_two) * gradient * gradient
    moment_hat = moment_new / (1.0 - beta_one**STEP)
    square_hat = square_new / (1.0 - beta_two**STEP)
    weight_new = weight - step_rate * (
        moment_hat / (jnp.sqrt(square_hat) + adam_eps) + decay * weight
    )
    return (weight_new, moment_new, square_new)


def bits(count):
    found = []
    step = 1
    while step < count:
        found.append(step)
        step *= 2
    return found


def params(count):
    return pltpu.CompilerParams(
        dimension_semantics=("arbitrary",) * count, vmem_limit_bytes=56 * 2**20
    )


def cost(flops, bytes_moved, transcendentals=0):
    return pl.CostEstimate(
        flops=int(flops), bytes_accessed=int(bytes_moved), transcendentals=int(transcendentals)
    )


def place(here, parts, masks, target, sems, first_sem):
    copies = []
    for n, (part, (ma, mb, my)) in enumerate(zip(parts, masks)):
        copy = pltpu.make_async_copy(
            part, target(here[0] ^ ma, here[2] ^ mb, here[3] ^ my), sems.at[first_sem + n]
        )
        copy.start()
        copies.append(copy)
    return copies


def by_rows(ref, first, count):
    return lambda a, b, y: ref.at[y, a, pl.ds(first, count), b]


def place_gu(here, parts, masks, ref, sems, first_sem):
    count = len(masks)
    copies = []
    for n in range(2):
        cut = parts[n * count].shape[0]
        target = by_rows(ref, n * (ref.shape[2] - cut), cut)
        copies += place(
            here, parts[n * count : (n + 1) * count], masks, target, sems, first_sem + n * count
        )
    return copies


def by_columns(ref, width):
    return lambda a, b, y: ref.at[a, :, b, :, pl.ds(pl.multiple_of(y * width, 128), width)]


def prep_kernel(sizes, n_blocks, head_cols, d_rows, unit, qkv, gu, qkv_out, gu_out):
    n_a, n_t, n_b, _ = sizes
    ff_cols = n_b * d_rows
    for t in range(n_t):
        for block in range(n_blocks):
            at = (block * n_t + t) * head_cols
            qkv_out[t, :, block * head_cols : (block + 1) * head_cols] = qkv[
                :, at : at + head_cols
            ].astype(BF16)
        pieces = []
        gap = jnp.zeros((gu.shape[0], unit - d_rows), F32)
        for a in range(n_a):
            for b in range(n_b):
                at = (a * n_t + t) * ff_cols + b * d_rows
                pieces += [gu[:, at : at + d_rows], gap]
        gu_out[t] = jnp.concatenate(pieces, axis=1).astype(BF16)


def prep(sizes, unit, w_qkv, w_gu, d_rows):
    n_a, n_t, n_b, _ = sizes
    rows = w_qkv.shape[0]
    head_cols = n_b * rows
    n_blocks = w_qkv.shape[1] // (n_t * head_cols)
    tile = 16
    wide_q, wide_g = n_blocks * head_cols, n_a * n_b * unit
    return pl.pallas_call(
        functools.partial(prep_kernel, sizes, n_blocks, head_cols, d_rows, unit),
        grid=(rows // tile,),
        in_specs=[
            pl.BlockSpec((tile, w_qkv.shape[1]), lambda i: (i, 0)),
            pl.BlockSpec((tile, w_gu.shape[1]), lambda i: (i, 0)),
        ],
        out_specs=[
            pl.BlockSpec((n_t, tile, wide_q), lambda i: (0, i, 0)),
            pl.BlockSpec((n_t, tile, wide_g), lambda i: (0, i, 0)),
        ],
        out_shape=[
            jax.ShapeDtypeStruct((n_t, rows, wide_q), BF16),
            jax.ShapeDtypeStruct((n_t, rows, wide_g), BF16),
        ],
        compiler_params=params(1),
        cost_estimate=cost(0, 20 * w_gu.size),
        name="prep",
    )(w_qkv, w_gu)


def adam(weight, gradient, first_moment, second_moment):
    return adam_update(weight, gradient, first_moment, second_moment, rate_matrix, decay_rate)


def finish_gu_kernel(sizes, d_rows, unit, g, w, m, v, w_out, m_out, v_out):
    n_a, n_t, n_b, _ = sizes
    pieces = []
    for a in range(n_a):
        for t in range(n_t):
            for b in range(n_b):
                at = (a * n_b + b) * unit
                pieces.append(g[t, :, at : at + d_rows].astype(F32))
    grad = jnp.concatenate(pieces, axis=1)
    w_out[...], m_out[...], v_out[...] = adam(w[...], grad, m[...], v[...])


def finish_qkv_kernel(sizes, head_cols, g, w, m, v, w_out, m_out, v_out):
    n_t = sizes[1]
    for block in range(w.shape[1] // (n_t * head_cols)):
        for t in range(n_t):
            at = (block * n_t + t) * head_cols
            cols = slice(at, at + head_cols)
            tile, lane = block * head_cols // LANES, block * head_cols % LANES
            grad = g[t, tile, :, lane : lane + head_cols].astype(F32)
            w_out[:, cols], m_out[:, cols], v_out[:, cols] = adam(
                w[:, cols], grad, m[:, cols], v[:, cols]
            )


def finish(kernel, name, gradient, weight, first, second):
    tile = 16
    rows, cols = weight.shape
    matrix = pl.BlockSpec((tile, cols), lambda i: (i, 0))
    lead, lanes = gradient.shape[:-2], gradient.shape[-1]
    gradient_block = pl.BlockSpec(
        lead + (tile, lanes), lambda i: (0,) * len(lead) + (i, 0)
    )
    return pl.pallas_call(
        kernel,
        grid=(rows // tile,),
        in_specs=[
            gradient_block,
            matrix,
            matrix,
            matrix,
        ],
        out_specs=[matrix] * 3,
        out_shape=[jax.ShapeDtypeStruct(weight.shape, F32)] * 3,
        compiler_params=params(1),
        cost_estimate=cost(20 * weight.size, 26 * weight.size),
        name=name,
    )(gradient, weight, first, second)


ANYWHERE = pl.BlockSpec(memory_space=pl.ANY)


def mlp_kernel(masks, steps, here, vec, x_even, x_odd, dy_even, dy_odd, *rest):
    count = len(masks)
    gu_parts, down_parts = rest[: 2 * count], rest[2 * count : 3 * count]
    normed, grads_out, hidden, d_joined, gu, down, rows, sems, row_sems = rest[-9:]
    step = pl.program_id(0)
    slot = normed.shape[0]

    def fetch(n):
        spot = pl.ds(n // 2 * slot, slot)
        sources = (x_odd, dy_odd) if n % 2 else (x_even, dy_even)
        return [
            pltpu.make_async_copy(
                source.at[spot], rows.at[n % 2, pl.ds(m * slot, slot)], row_sems.at[n % 2, m]
            )
            for m, source in enumerate(sources)
        ]

    @pl.when(step == 0)
    def _():
        for copy in fetch(0):
            copy.start()
        copies = place_gu(here, gu_parts, masks, gu, sems, 0)
        target = by_columns(down, down.shape[4] // 2)
        copies += place(here, down_parts, masks, target, sems, 2 * count)
        for copy in copies:
            copy.wait()

    for n in range(steps):

        @pl.when(step == n)
        def _(n=n):
            if n + 1 < steps:
                for copy in fetch(n + 1):
                    copy.start()
            for copy in fetch(n):
                copy.wait()

    now = step % 2
    low = normalize(rows[now, :slot].astype(F32), vec[0:1], vec[1:2])[0].astype(BF16)
    dy = rows[now, slot:]
    normed[...] = low
    grads_out[...] = dy
    wide = gu.shape[5]
    gate = dot(low, gu[0].reshape(-1, wide))
    up = dot(low, gu[1].reshape(-1, wide))
    d_hidden = dot_nt(dy, down[...].reshape(wide, -1))
    sig = jax.nn.sigmoid(gate)
    act = gate * sig
    hidden[...] = (act * up).astype(BF16)
    d_joined[0] = (d_hidden * up * sig * (1.0 + gate * (1.0 - sig))).astype(BF16)
    d_joined[1] = (d_hidden * act).astype(BF16)


def mlp(here, masks, held, vec, gu_parts, down_parts, sizes, unit):
    n_a, n_t, n_b, n_y = sizes
    width = held[0].shape[1]
    slot = held[0].shape[0] * 2 // n_t
    wide = n_a * n_b * unit
    rows = n_t * slot
    w_rows = gu_parts[0].shape[1]
    return pl.pallas_call(
        functools.partial(mlp_kernel, masks, n_t),
        grid_spec=pltpu.PrefetchScalarGridSpec(
            num_scalar_prefetch=1,
            grid=(n_t,),
            in_specs=[pl.BlockSpec(vec.shape, lambda i, h: (0, 0))]
            + [ANYWHERE] * (3 * len(masks) + 4),
            out_specs=[
                pl.BlockSpec((slot, width), lambda i, h: (i, 0)),
                pl.BlockSpec((slot, width), lambda i, h: (i, 0)),
                pl.BlockSpec((slot, wide), lambda i, h: (i, 0)),
                pl.BlockSpec((2, slot, wide), lambda i, h: (0, i, 0)),
            ],
            scratch_shapes=[
                pltpu.VMEM((n_y, n_a, n_t, n_b, w_rows, wide), BF16),
                pltpu.VMEM((n_a, 1, n_b, unit, width), BF16),
                pltpu.VMEM((2, 2 * slot, width), BF16),
                pltpu.SemaphoreType.DMA((3 * len(masks),)),
                pltpu.SemaphoreType.DMA((2, 2)),
            ],
        ),
        out_shape=[
            jax.ShapeDtypeStruct((rows, width), BF16),
            jax.ShapeDtypeStruct((rows, width), BF16),
            jax.ShapeDtypeStruct((rows, wide), BF16),
            jax.ShapeDtypeStruct((2, rows, wide), BF16),
        ],
        compiler_params=params(1),
        name="mlp",
    )(here, vec, *held, *gu_parts, *down_parts)


def attention_kernel(
    masks, here, lengths, normed, dy, bias, cos_ref, up_ref, down_ref, *rest
):
    count = len(masks)
    qkv_parts, out_parts = rest[:count], rest[count : 2 * count]
    o_ref, dqkv_ref, bias_ref, w_qkv, w_out, sems = rest[2 * count :]

    @pl.when(pl.program_id(0) == 0)
    def _():
        copies = place(here, qkv_parts, masks, by_columns(w_qkv, w_qkv.shape[4] // 2), sems, 0)
        copies += place(here, out_parts, masks, by_columns(w_out, w_out.shape[4] // 2), sems, count)
        for copy in copies:
            copy.wait()

    rows = normed.shape[0]
    wide = w_qkv.shape[4]
    width = wide // 3
    qkv = dot(normed[...], w_qkv[...].reshape(-1, wide)) + bias[...]
    dpo = dot_nt(dy[...], w_out[...].reshape(width, -1)).astype(BF16)
    length = lengths[pl.program_id(0)]
    cosine, sine_up, sine_down = cos_ref[...], up_ref[...], down_ref[...]
    query_at = lax.broadcasted_iota(jnp.int32, (rows, rows), 0)
    key_at = lax.broadcasted_iota(jnp.int32, (rows, rows), 1)
    allowed = (key_at <= query_at) & (key_at < length)
    lane = lax.broadcasted_iota(jnp.int32, (rows, 2 * HEAD), 1)
    lower = lane < HEAD
    half = ROT // 2
    scale = HEAD ** (-0.5)

    def turn(x, sign):
        ahead = pltpu.roll(x, 2 * HEAD - half, 1)
        behind = pltpu.roll(x, half, 1)
        return x * cosine + sign * (behind * sine_down - ahead * sine_up)

    for pair in range(width // (2 * HEAD)):
        at = pair * 2 * HEAD
        cols = slice(at, at + 2 * HEAD)
        k_cols = slice(width + at, width + at + 2 * HEAD)
        v_cols = slice(2 * width + at, 2 * width + at + 2 * HEAD)
        q_rot = turn(qkv[:, cols], 1.0).astype(BF16)
        k_rot = turn(qkv[:, k_cols], 1.0).astype(BF16)
        values = qkv[:, v_cols].astype(BF16)
        grad = dpo[:, cols]
        results = []
        for side in range(2):
            mine = lower if side == 0 else ~lower
            scores = dot_nt(jnp.where(mine, q_rot, 0.0).astype(BF16), k_rot) * scale
            masked = jnp.where(allowed, scores, -1e30)
            raised = jnp.exp(masked - jnp.max(masked, axis=1, keepdims=True))
            probs = raised * (1.0 / jnp.sum(raised, axis=1, keepdims=True))
            probs_low = probs.astype(BF16)
            out = dot(probs_low, values)
            d_probs = dot_nt(jnp.where(mine, grad, 0.0).astype(BF16), values)
            d_values = dot_tn(probs_low, grad)
            inner = jnp.sum(probs * d_probs, axis=1, keepdims=True)
            d_scores = (probs * (d_probs - inner)).astype(BF16)
            d_query = dot(d_scores, k_rot) * scale
            d_keys = dot_tn(d_scores, q_rot) * scale
            results.append((out, d_query, d_keys, d_values))
        out, d_query, d_keys, d_values = (
            jnp.where(lower, first, second) for first, second in zip(*results)
        )
        o_ref[:, cols] = out.astype(BF16)
        for spot, value in (
            (cols, turn(d_query, -1.0)),
            (k_cols, turn(d_keys, -1.0)),
            (v_cols, d_values),
        ):
            low = value.astype(BF16)
            dqkv_ref[:, spot] = low
            bias_ref[0, :, spot] = jnp.sum(low.astype(F32), axis=0, keepdims=True)


def attention(here, masks, lengths, tables, normed, dy, bias, qkv_parts, out_parts, sizes):
    n_a, n_t, n_b, _ = sizes
    slots = lengths.shape[0]
    slot, width = dy.shape[0] // slots, dy.shape[1]
    wide = bias.shape[1]
    table = pl.BlockSpec((slot, 2 * HEAD), lambda i, h, lens: (0, 0))
    w_rows = qkv_parts[0].shape[1]
    return pl.pallas_call(
        functools.partial(attention_kernel, masks),
        grid_spec=pltpu.PrefetchScalarGridSpec(
            num_scalar_prefetch=2,
            grid=(n_t,),
            in_specs=[
                pl.BlockSpec((slot, width), lambda i, h, lens: (i, 0)),
                pl.BlockSpec((slot, width), lambda i, h, lens: (i, 0)),
                pl.BlockSpec((1, wide), lambda i, h, lens: (0, 0)),
                table,
                table,
                table,
            ]
            + [ANYWHERE] * (2 * len(masks)),
            out_specs=[
                pl.BlockSpec((slot, wide // 3), lambda i, h, lens: (i, 0)),
                pl.BlockSpec((slot, wide), lambda i, h, lens: (i, 0)),
                pl.BlockSpec((1, 1, wide), lambda i, h, lens: (i, 0, 0)),
            ],
            scratch_shapes=[
                pltpu.VMEM((n_a, n_t, n_b, w_rows, wide), BF16),
                pltpu.VMEM((n_a, 1, n_b, w_rows, width), BF16),
                pltpu.SemaphoreType.DMA((2 * len(masks),)),
            ],
        ),
        out_shape=[
            jax.ShapeDtypeStruct((n_t * slot, wide // 3), BF16),
            jax.ShapeDtypeStruct((n_t * slot, wide), BF16),
            jax.ShapeDtypeStruct((n_t, 1, wide), F32),
        ],
        compiler_params=params(1),
        cost_estimate=cost(
            4 * n_t * slot * width * wide, 5 * n_t * slot * width * 2, n_t * slot * slot * 8
        ),
        name="attention",
    )(here, lengths, normed, dy, bias, *tables, *qkv_parts, *out_parts)


def grads_cols_kernel(where, left, d_sent, d_kept, *outs):
    tall = left[...]
    sent = dot_tn(tall, d_sent[0]).astype(BF16)
    kept = dot_tn(tall, d_kept[0])
    far = pl.program_id(0) < pl.num_programs(0) // 2

    @pl.when(far)
    def _():
        outs[0][...] = sent
        outs[1][...] = kept

    @pl.when(jnp.logical_not(far))
    def _():
        outs[2][...] = sent
        outs[3][...] = kept


def grads_cols(where, normed, d_cols, name):
    rows, width = normed.shape
    wide = d_cols.shape[2]
    half_rows = width // 2
    steps = 4
    tile = half_rows // steps

    def tall(i, w):
        return (0, jnp.where(i < steps, w[0], 1 - w[0]) * steps + i % steps)

    def far(i, w):
        return (jnp.minimum(i, steps - 1), 0)

    def near(i, w):
        return (jnp.maximum(i - steps, 0), 0)

    return pl.pallas_call(
        grads_cols_kernel,
        grid_spec=pltpu.PrefetchScalarGridSpec(
            num_scalar_prefetch=1,
            grid=(2 * steps,),
            in_specs=[
                pl.BlockSpec((rows, tile), tall),
                pl.BlockSpec((1, rows, wide), lambda i, w: (1 - w[1], 0, 0)),
                pl.BlockSpec((1, rows, wide), lambda i, w: (w[1], 0, 0)),
            ],
            out_specs=[pl.BlockSpec((tile, wide), at) for at in (far, far, near, near)],
        ),
        out_shape=[jax.ShapeDtypeStruct((half_rows, wide), t) for t in (BF16, F32, BF16, F32)],
        compiler_params=params(1),
        name=name,
    )(where, normed, d_cols, d_cols)


def grads_rows_kernel(where, far, near, dy_sent, dy_kept, *outs):
    sent, kept = dy_sent[...], dy_kept[...]
    outs[0][...] = dot_tn(far[...], sent).astype(BF16)
    outs[1][...] = dot_tn(far[...], kept)
    outs[2][...] = dot_tn(near[...], sent).astype(BF16)
    outs[3][...] = dot_tn(near[...], kept)


def grads_rows(where, left, dy, name):
    rows, wide = left.shape
    width = dy.shape[1]
    half, dy_half = wide // 2, width // 2
    steps = 4
    tile = dy_half // steps
    block = (rows, tile)
    return pl.pallas_call(
        grads_rows_kernel,
        grid_spec=pltpu.PrefetchScalarGridSpec(
            num_scalar_prefetch=1,
            grid=(steps,),
            in_specs=[
                pl.BlockSpec((rows, half), lambda i, w: (0, w[0])),
                pl.BlockSpec((rows, half), lambda i, w: (0, 1 - w[0])),
                pl.BlockSpec(block, lambda i, w: (0, (1 - w[1]) * steps + i)),
                pl.BlockSpec(block, lambda i, w: (0, w[1] * steps + i)),
            ],
            out_specs=[pl.BlockSpec((half, tile), lambda i, w: (0, i))] * 4,
        ),
        out_shape=[jax.ShapeDtypeStruct((half, dy_half), t) for t in (BF16, F32, BF16, F32)],
        compiler_params=params(1),
        cost_estimate=cost(2 * rows * width * wide, 2 * rows * (width + wide) + 3 * wide * width),
        name=name,
    )(where, left, left, dy, dy)


def grads_attention_kernel(where, tall, d_qkv, left, dy_sent, dy_kept, sent, kept):
    step, steps = pl.program_id(0), pl.num_programs(0)
    tile, half = tall.shape[1], left.shape[1] // 2
    tiles = sent.shape[1] - 1
    part, first = step // (steps // 2), step % (steps // 2) * tile
    result = dot_tn(tall[...], d_qkv[...])
    low, high = result[:, : tiles * LANES], result[:, tiles * LANES :]
    upper = where[1] == 1
    for out, d_cols, dy in (
        (sent, jnp.where(upper, low, high), dy_sent),
        (kept, jnp.where(upper, high, low), dy_kept),
    ):
        d_cols = d_cols.astype(out.dtype)
        spot = pl.ds(pl.multiple_of(first, tile), tile)
        for n in range(tiles):
            out[part, n, spot, :] = d_cols[:, n * LANES : (n + 1) * LANES]
        columns = dot_tn(left[...], dy[...]).astype(out.dtype)
        spot = pl.ds(pl.multiple_of(step * half, half), half)
        out[where[0], tiles, spot, :] = columns[:half]
        out[1 - where[0], tiles, spot, :] = columns[half:]


def grads_attention(where, normed, d_qkv, attended, dy):
    rows, width = normed.shape
    d_half, half, dy_half = d_qkv.shape[1] // 2, attended.shape[1] // 2, width // 2
    steps = dy_half // LANES
    tile = width // steps
    block = (rows, LANES)
    shape = (2, d_half // LANES + 1, steps * half, LANES)
    assert shape[2] == width // 2

    def tall(i, w):
        return (0, jnp.where(i < steps // 2, w[0], 1 - w[0]) * (steps // 2) + i % (steps // 2))

    return pl.pallas_call(
        grads_attention_kernel,
        grid_spec=pltpu.PrefetchScalarGridSpec(
            num_scalar_prefetch=1,
            grid=(steps,),
            in_specs=[
                pl.BlockSpec((rows, tile), tall),
                pl.BlockSpec((rows, 2 * d_half), lambda i, w: (0, 0)),
                pl.BlockSpec((rows, 2 * half), lambda i, w: (0, 0)),
                pl.BlockSpec(block, lambda i, w: (0, (1 - w[1]) * steps + i)),
                pl.BlockSpec(block, lambda i, w: (0, w[1] * steps + i)),
            ],
            out_specs=[pl.BlockSpec(shape, lambda i, w: (0, 0, 0, 0))] * 2,
        ),
        out_shape=[jax.ShapeDtypeStruct(shape, t) for t in (BF16, F32)],
        compiler_params=params(1),
        name="grads_attention",
    )(where, normed, d_qkv, attended, dy, dy)


def row_blocks(kernel, name, here, kept, inputs, parts, scratch, slot, width, n_t):
    def slot_of(i, h):
        lowest = (i < n_t // 2).astype(jnp.int32) if kept is None else 1 - kept
        return i % 2 * 4 + i // 2 % 2 * 2 + lowest

    half = n_t // 2
    blocks = [lambda i, h: (i, 0)]
    if kept is None:
        blocks = [
            lambda i, h: (jnp.minimum(i, half - 1), 0),
            lambda i, h: (jnp.maximum(i - half, 0), 0),
        ]

    in_specs = []
    for value in inputs:
        block = (slot, value.shape[-1])
        if value.ndim == 3:
            block = (value.shape[0],) + block
            in_specs.append(pl.BlockSpec(block, lambda i, h: (0, slot_of(i, h), 0)))
        else:
            in_specs.append(pl.BlockSpec(block, lambda i, h: (slot_of(i, h), 0)))
    return pl.pallas_call(
        kernel,
        grid_spec=pltpu.PrefetchScalarGridSpec(
            num_scalar_prefetch=1,
            grid=(half * len(blocks),),
            in_specs=in_specs + [ANYWHERE] * len(parts),
            out_specs=[pl.BlockSpec((slot, width), block) for block in blocks],
            scratch_shapes=scratch + [pltpu.SemaphoreType.DMA((len(parts),))],
        ),
        out_shape=[jax.ShapeDtypeStruct((half * slot, width), BF16)] * len(blocks),
        compiler_params=params(1),
        name=name if kept is None else name + ("_kept" if kept else "_sent"),
    )(here, *inputs, *parts)


def branch_kernel(masks, here, o, hidden, *rest):
    count = len(masks)
    out_parts, down_parts = rest[:count], rest[count : 2 * count]
    *outs, w_out, down, sems = rest[2 * count :]

    @pl.when(pl.program_id(0) == 0)
    def _():
        copies = place(here, out_parts, masks, by_columns(w_out, w_out.shape[4] // 2), sems, 0)
        copies += place(here, down_parts, masks, by_columns(down, down.shape[4] // 2), sems, count)
        for copy in copies:
            copy.wait()

    width = w_out.shape[4]
    branch = dot(o[...], w_out[...].reshape(-1, width))
    branch += dot(hidden[...], down[...].reshape(-1, width))
    branch, step, half = branch.astype(BF16), pl.program_id(0), pl.num_programs(0) // 2

    @pl.when(step < half)
    def _():
        outs[0][...] = branch

    @pl.when(step >= half)
    def _():
        outs[1][...] = branch


def normal_kernel(masks, here, d_qkv, d_joined, *rest):
    count = len(masks)
    qkv_parts, gu_parts = rest[:count], rest[count : 3 * count]
    out, w_qkv, gu, sems = rest[3 * count :]

    @pl.when(pl.program_id(0) == 0)
    def _():
        copies = place(here, qkv_parts, masks, by_columns(w_qkv, w_qkv.shape[4] // 2), sems, 0)
        copies += place_gu(here, gu_parts, masks, gu, sems, count)
        for copy in copies:
            copy.wait()

    wide = w_qkv.shape[4]
    width = w_qkv.size // wide
    normal = dot_nt(d_qkv[...], w_qkv[...].reshape(width, -1))
    normal += dot_nt(d_joined[0], gu[0].reshape(width, -1))
    normal += dot_nt(d_joined[1], gu[1].reshape(width, -1))
    out[...] = normal.astype(BF16)


def after(value, *others):
    return lax.optimization_barrier((value,) + others)[0]


def per_device(
    sizes,
    tokens,
    cotangent,
    lengths,
    w_qkv,
    w_out,
    w_gate_up,
    w_down,
    vectors,
    first_qkv,
    first_out,
    first_gate_up,
    first_down,
    first_vectors,
    second_qkv,
    second_out,
    second_gate_up,
    second_down,
    second_vectors,
):
    barrier = lax.optimization_barrier
    n_a, n_t, n_b, n_y = sizes
    total = n_a * n_t * n_b * n_y
    at_a, at_t, at_b, at_y = (lax.axis_index(name).astype(jnp.int32) for name in AXES)
    here = jnp.stack([at_a, at_t, at_b, at_y])
    row_count, width = tokens.shape
    w_rows = w_qkv.shape[0]
    d_rows = w_down.shape[0]
    head_cols = n_b * w_rows
    unit = d_rows
    while unit % 16 or n_a * n_b * unit % 128:
        unit += 1

    def swap(value, name, step):
        mask = {"y": 1, "b": n_y, "t": n_y * n_b, "a": n_y * n_b * n_t}[name] * step
        return lax.ppermute(value, AXES, [(i, i ^ mask) for i in range(total)])

    def exchange(value):
        return lax.all_to_all(value, "t", split_axis=0, concat_axis=0, tiled=True)

    r_bits = [("a", s) for s in reversed(bits(n_a))] + [("b", s) for s in bits(n_b)]
    masks = [(0, 0, 0)]
    for name, step in r_bits:
        masks = masks + [
            (m[0] + step * (name == "a"), m[1] + step * (name == "b"), 0) for m in masks
        ]
    masks = tuple(masks + [(m[0], m[1], 1) for m in masks])

    small = 5 * vectors.shape[1] + lengths.shape[1]
    padded = -(-small // 128) * 128
    packed = jnp.concatenate(
        [
            vectors.reshape(1, 1, -1),
            lengths.astype(F32).reshape(1, 1, -1),
            jnp.zeros((1, 1, padded - small), F32),
        ],
        axis=2,
    )
    packed = jnp.broadcast_to(packed, (total, 1, padded))
    packed = lax.all_to_all(packed, AXES, split_axis=0, concat_axis=0, tiled=True)
    packed = packed.reshape(total, padded)

    def spread_top(part):
        parts = [part]
        for name, step in r_bits:
            parts = parts + [swap(p, name, step) for p in parts]
        return parts

    def over_y(value):
        return swap(value, "y", 1)

    def over_y_rest(parts):
        return [over_y(part) for part in parts[1:]]

    def over_top(value):
        return swap(value.astype(BF16), "a", top)

    def summed(kept, *got):
        return functools.reduce(lambda one, two: one.astype(F32) + two.astype(F32), got, kept)

    top = n_a // 2
    down_own = jnp.pad(w_down.astype(BF16), ((0, unit - d_rows), (0, 0)))[None]
    out_own = w_out.astype(BF16)[None]
    qkv_own, gu_own = prep(sizes, unit, w_qkv, w_gate_up, d_rows)
    x_top, x_middle, down_parts, down_other, qkv_own, gu_own, out_own, packed = barrier(
        (
            swap(tokens, "t", n_t // 2),
            swap(tokens, "t", n_t // 4),
            spread_top(down_own),
            over_y(down_own),
            qkv_own,
            gu_own,
            out_own,
            packed,
        )
    )
    all_vectors = packed[:, : 5 * vectors.shape[1]].reshape(total, 5, -1)
    all_vectors = all_vectors.transpose(1, 0, 2).reshape(5, width)
    group = packed[:, 5 * vectors.shape[1] : small].reshape(n_a, n_t, n_b, n_y, -1)
    group = lax.dynamic_index_in_dim(group, at_a, 0, keepdims=False)
    group = lax.dynamic_index_in_dim(group, at_b, 1, keepdims=False)
    group = jnp.where(at_y == 1, group[:, 0, 1], group[:, 0, 0])
    group = group.reshape(2, 2, 2)
    for dim, step in enumerate((4, 2, 1)):
        group = jnp.where(at_t // step % 2 == 1, jnp.flip(group, dim), group)
    slot_lengths = jnp.round(group.reshape(-1)).astype(jnp.int32)
    bias = all_vectors[2:5].reshape(3 * n_a, n_t, head_cols)
    bias = lax.dynamic_index_in_dim(bias, at_t, 1, keepdims=False).reshape(1, -1)
    vec = all_vectors[:2]
    tables = rotary_lanes(row_count)

    gu_own, down_far, out_parts, out_other, cotangent, vec, bias, slot_lengths, tables = barrier(
        (
            exchange(gu_own),
            over_y_rest(down_parts),
            spread_top(out_own),
            over_y(out_own),
            cotangent,
            vec,
            bias,
            slot_lengths,
            tables,
        )
    )
    down_parts = down_parts + [down_other] + down_far
    cut = n_t // 2
    gu_first, gu_second = barrier((gu_own[:cut], gu_own[cut:]))
    gu_parts, gu_other, out_far, dy_top, dy_middle, gu_second, qkv_own, x_top = barrier(
        (
            spread_top(gu_first),
            over_y(gu_first),
            over_y_rest(out_parts),
            swap(cotangent, "t", n_t // 2),
            swap(cotangent, "t", n_t // 4),
            gu_second,
            qkv_own,
            x_top,
        )
    )
    out_parts = out_parts + [out_other] + out_far
    gu_two, gu_two_other, gu_far, x_far, dy_far, qkv_own = barrier(
        (
            spread_top(gu_second),
            over_y(gu_second),
            over_y_rest(gu_parts),
            swap(x_top, "t", n_t // 4),
            swap(dy_top, "t", n_t // 4),
            qkv_own,
        )
    )
    x_even = jnp.concatenate([tokens, x_middle, x_top, x_far], axis=0)
    dy_even = jnp.concatenate([cotangent, dy_middle, dy_top, dy_far], axis=0)
    gu_two_far, qkv_own, x_odd, dy_odd = barrier(
        (
            over_y_rest(gu_two),
            exchange(qkv_own),
            swap(x_even, "t", 1),
            swap(dy_even, "t", 1),
        )
    )
    gu_parts = gu_parts + [gu_other] + gu_far + gu_two + [gu_two_other] + gu_two_far


    top = n_a // 2
    upper = at_a // top % 2
    other_half = jnp.stack([1 - upper, at_y])
    lower_bits = r_bits[1:]

    def over_rest(value, parts_shape):
        summed = value.reshape(parts_shape + (value.shape[-1],))
        for name, step in lower_bits:
            dim = 0 if name == "a" else 2
            at = at_a if name == "a" else at_b
            size = summed.shape[dim] // 2
            low_half = lax.slice_in_dim(summed, 0, size, axis=dim)
            high_half = lax.slice_in_dim(summed, size, 2 * size, axis=dim)
            is_upper = (at // step) % 2 == 1
            keep = jnp.where(is_upper, high_half, low_half)
            send = jnp.where(is_upper, low_half, high_half)
            summed = keep + swap(send.astype(BF16), name, step).astype(F32)
        return summed.reshape(summed.shape[1], summed.shape[3], summed.shape[4])

    def piece(raw, middle_bit, top_bit, left):
        columns = slice(0, half_width) if left else slice(half_width, width)
        got, kept = (part.reshape(2, 2, row_count, width) for part in raw)
        spot = (middle_bit, top_bit, slice(None), columns)
        return got[spot].astype(F32) + kept[spot].astype(F32)

    every = slice(None)

    def first_sends(raw):
        return piece(raw, 1, every, True).astype(BF16), piece(raw, every, 1, False).astype(BF16)

    def first_swaps(sends):
        return swap(sends[0], "t", n_t // 4), swap(sends[1], "t", n_t // 2)

    def second_sends(raw, got):
        left = piece(raw, 0, 1, True) + got[0][1].astype(F32)
        right = piece(raw, 1, 0, False) + got[1][1].astype(F32)
        return left.astype(BF16), right.astype(BF16)

    def second_swaps(sends):
        return swap(sends[0], "t", n_t // 2), swap(sends[1], "t", n_t // 4)

    def whole_rows(raw, got, last):
        left = piece(raw, 0, 0, True) + got[0][0].astype(F32) + last[0].astype(F32)
        right = piece(raw, 0, 0, False) + got[1][0].astype(F32) + last[1].astype(F32)
        return jnp.concatenate([left, right], axis=1)

    half_width = width // 2
    shape_w = (top, n_t, n_b, w_rows)
    normed, dy, hidden, d_joined = mlp(
        after(here, qkv_own),
        masks,
        (x_even, x_odd, dy_even, dy_odd),
        vec,
        gu_parts,
        down_parts,
        sizes,
        unit,
    )
    qkv_parts, qkv_other, normed, dy, hidden, d_joined = barrier(
        (
            spread_top(qkv_own),
            over_y(qkv_own),
            normed,
            dy,
            hidden,
            d_joined,
        )
    )

    qkv_far = over_y_rest(qkv_parts)
    down_far_sent, down_far_kept, down_sent, down_kept = grads_rows(
        other_half, hidden, dy, "grads_down"
    )
    qkv_far, down_far_sent, down_sent, down_kept = barrier(
        (qkv_far, down_far_sent, down_sent, down_kept)
    )
    down_far_got = over_y(down_far_sent)
    gu_far_sent, gu_far_kept, gu_sent, gu_kept = grads_cols(
        after(other_half, down_kept), normed, d_joined, "grads_gate_up"
    )
    down_far_got, gu_far_sent, down_sent, gu_sent, gu_kept = barrier(
        (down_far_got, gu_far_sent, down_sent, gu_sent, gu_kept)
    )
    qkv_parts = qkv_parts + [qkv_other] + qkv_far

    down_far = barrier(summed(down_far_kept, down_far_got).astype(BF16))
    attended, d_qkv, bias_sums = attention(
        after(here, down_far),
        masks,
        slot_lengths,
        tables,
        normed,
        dy,
        bias,
        qkv_parts,
        out_parts,
        sizes,
    )
    gu_rows = gu_sent.shape[0] // 2
    down_far_got, gu_far_got, down_sent, gu_sent, attended, d_qkv = barrier(
        (
            over_top(down_far),
            over_y(gu_far_sent),
            down_sent,
            (gu_sent[:gu_rows], gu_sent[gu_rows:]),
            attended,
            d_qkv,
        )
    )

    def thirds(value):
        value = value.reshape(value.shape[0] // (n_b * w_rows), n_b * w_rows, -1)
        cuts = [n * value.shape[1] // 8 for n in (0, 3, 6, 8)]
        return [value[:, low:high] for low, high in zip(cuts, cuts[1:])]

    gu_far = [summed(k, g).astype(BF16) for k, g in zip(thirds(gu_far_kept), thirds(gu_far_got))]
    gu_far = barrier(gu_far)
    branch_sent, branch_kept = row_blocks(
        functools.partial(branch_kernel, masks),
        "branch_rows",
        after(here, *gu_far),
        None,
        inputs=(attended, hidden),
        parts=out_parts + down_parts,
        scratch=[
            pltpu.VMEM((n_a, 1, n_b, w_rows, width), BF16),
            pltpu.VMEM((n_a, 1, n_b, unit, width), BF16),
        ],
        slot=row_count,
        width=width,
        n_t=n_t,
    )
    gu_far_one, gu_got, gu_far, branch_sent, branch_kept, gu_sent = barrier(
        (
            over_top(gu_far[0]),
            over_y(gu_sent[0]),
            gu_far,
            branch_sent,
            branch_kept,
            gu_sent[1],
        )
    )

    qo_sent, qo_kept = grads_attention(
        after(other_half, branch_sent), normed, d_qkv, attended, dy
    )
    gu_far_two, branch_got, gu_got_more, gu_far, qo_far_sent, qo_sent = barrier(
        (
            over_top(gu_far[1]),
            swap(branch_sent, "t", 1),
            over_y(gu_sent),
            gu_far,
            qo_sent[0],
            qo_sent[1],
        )
    )

    normal_rows = functools.partial(
        row_blocks,
        functools.partial(normal_kernel, masks),
        "normal_rows",
        inputs=(d_qkv, d_joined),
        parts=qkv_parts + gu_parts,
        scratch=[
            pltpu.VMEM((n_a, n_t, n_b, w_rows, d_qkv.shape[1]), BF16),
            pltpu.VMEM((n_y, n_a, n_t, n_b, w_rows, n_a * n_b * unit), BF16),
        ],
        slot=row_count,
        width=width,
        n_t=n_t,
    )
    branch = (branch_got, branch_kept)
    branch_sends = barrier(first_sends(branch))
    (normal_sent,) = normal_rows(after(here, qo_far_sent, *branch_sends), 0)
    gu_far_three, qo_far_got, branch_got, normal_sent, qo_sent, down_sent = barrier(
        (
            over_top(gu_far[2]),
            over_y(qo_far_sent),
            first_swaps(branch_sends),
            normal_sent,
            qo_sent,
            down_sent,
        )
    )
    qo_far = summed(qo_kept[0], qo_far_got).astype(BF16)
    gu_got = jnp.concatenate([gu_got, gu_got_more], axis=0)
    gu_far_got = jnp.concatenate([gu_far_one, gu_far_two, gu_far_three], axis=1)
    g_gu = summed(gu_kept, gu_got, gu_far_got.reshape(gu_kept.shape))
    g_gu = over_rest(g_gu, shape_w).astype(BF16)
    qo_far_one, qo_far_two, g_gu = barrier((qo_far[:1], qo_far[1:], g_gu))
    (normal_kept,) = normal_rows(after(here, normal_sent, g_gu), 1)
    qo_far_one, normal_got, qo_got, g_gu, normal_kept, qo_far_two, down_sent, branch_got = barrier(
        (
            over_top(qo_far_one),
            swap(normal_sent, "t", 1),
            over_y(qo_sent),
            exchange(g_gu),
            normal_kept,
            qo_far_two,
            down_sent,
            branch_got,
        )
    )

    qo_far_two, down_got = over_top(qo_far_two), over_y(down_sent)
    normal = (normal_got, normal_kept)
    normal_sends = barrier(first_sends(normal))
    new_gu, moment_gu, square_gu = finish(
        functools.partial(finish_gu_kernel, sizes, d_rows, unit),
        "finish_gate_up",
        after(g_gu, *normal_sends),
        w_gate_up,
        first_gate_up,
        second_gate_up,
    )
    branch_sends = second_sends(branch, [after(got, *normal_sends) for got in branch_got])
    normal_got, qo_far_two, down_got, branch_sends, new_gu = barrier(
        (first_swaps(normal_sends), qo_far_two, down_got, branch_sends, new_gu)
    )

    normal_sends = barrier(second_sends(normal, normal_got))
    qo_far_got = jnp.concatenate([qo_far_one, qo_far_two], axis=0)
    qo = after(summed(qo_kept[1], qo_got, qo_far_got), *normal_sends)
    g_qkv = over_rest(qo[:-1].transpose(1, 0, 2).reshape(qo.shape[1], -1), shape_w)
    g_out = qo[-1].reshape(half_width // LANES, -1, LANES).transpose(1, 0, 2)
    g_out = over_rest(g_out.reshape(-1, half_width), (top, 1, n_b, w_rows))
    g_qkv = g_qkv.astype(BF16).reshape(n_t, w_rows, -1, LANES).transpose(0, 2, 1, 3)
    g_qkv = barrier(g_qkv)
    g_down = summed(down_kept, down_got, down_far_got)
    g_down = over_rest(after(g_down, g_qkv), (top, 1, n_b, unit))
    new_down, moment_down, square_down = adam(w_down, g_down[0, :d_rows], first_down, second_down)
    g_qkv, normal_last, g_out, branch_sends, new_down = barrier(
        (exchange(g_qkv), second_swaps(normal_sends), g_out, branch_sends, new_down)
    )
    branch_last = second_swaps(branch_sends)
    normal_own = whole_rows(normal, normal_got, normal_last)
    _, scaled_own, inv_own = normalize(tokens.astype(F32), vec[0], vec[1])
    d_scaled = normal_own * vec[0]
    input_grad = cotangent.astype(F32) + inv_own * (
        d_scaled
        - jnp.mean(d_scaled, axis=-1, keepdims=True)
        - scaled_own * jnp.mean(d_scaled * scaled_own, axis=-1, keepdims=True)
    )
    g_bias = jnp.sum(bias_sums, axis=0).reshape(3 * n_a, 1, head_cols)
    is_here = (jnp.arange(n_t) == at_t)[None, :, None]
    g_bias = jnp.where(is_here, g_bias, 0.0).reshape(3, width)
    vector_part = jnp.concatenate(
        [
            jnp.sum(normal_own * scaled_own, axis=0)[None],
            jnp.sum(normal_own, axis=0)[None],
            g_bias,
        ],
        axis=0,
    )
    vector_part = vector_part.reshape(5, total, -1).transpose(1, 0, 2).reshape(total, 1, -1)
    vector_part = jnp.pad(vector_part, ((0, 0), (0, 0), (0, -vector_part.shape[2] % 128)))
    vector_part = lax.all_to_all(vector_part, AXES, split_axis=0, concat_axis=0, tiled=True)
    vector_grad = jnp.sum(vector_part, axis=0)[0, : vectors.size].reshape(vectors.shape)
    branch_own = whole_rows(branch, branch_got, branch_last)
    output = (tokens.astype(F32) + after(branch_own, vector_part)).astype(BF16)
    new_out, moment_out, square_out = adam(w_out, g_out[0], first_out, second_out)
    new_qkv, moment_qkv, square_qkv = finish(
        functools.partial(finish_qkv_kernel, sizes, head_cols),
        "finish_qkv",
        g_qkv,
        w_qkv,
        first_qkv,
        second_qkv,
    )
    new_vec, moment_vec, square_vec = adam_update(
        vectors, vector_grad, first_vectors, second_vectors, rate_vector, 0.0
    )
    return (
        output,
        input_grad.astype(BF16),
        new_qkv,
        new_out,
        new_gu,
        new_down,
        new_vec,
        moment_qkv,
        moment_out,
        moment_gu,
        moment_down,
        moment_vec,
        square_qkv,
        square_out,
        square_gu,
        square_down,
        square_vec,
    )


def solution(mesh):
    n_dp, n_y = mesh.shape["dp"], mesh.shape["branch"]
    n_b = max(1, HEAD * n_dp // (HEADS * HEAD))
    n_t = min(SLICES, n_dp // n_b)
    sizes = (n_dp // (n_t * n_b), n_t, n_b, n_y)
    split = Mesh(mesh.devices.reshape(sizes), AXES)
    dp = ("a", "t", "b")
    rows = P(AXES, None)
    matrix = P(dp, "y")
    vector = P(None, AXES)
    weights = (matrix, matrix, matrix, matrix, vector)
    return jax.shard_map(
        functools.partial(per_device, sizes),
        mesh=split,
        in_specs=(rows, rows, P(dp, None)) + weights * 3,
        out_specs=(rows, rows) + weights * 3,
        check_vma=False,
    )
```

```python
import functools

import jax
import jax.numpy as jnp
from jax import lax
from jax.experimental import pallas as pl
from jax.experimental.pallas import tpu as pltpu
from jax.sharding import Mesh, PartitionSpec as P

HEADS = 32
HEAD = 64
ROT = 16
MB = 2
STEP = 10
SLICES = 8
LANES = 128

theta_base = 10000.0
norm_eps = 1e-05
beta_one = 0.9
beta_two = 0.95
adam_eps = 1e-08
decay_rate = 0.1
rate_matrix = 0.05
rate_vector = 1.0

AXES = ("a", "t", "b", "y")
F32 = jnp.float32
BF16 = jnp.bfloat16


def dot(left, right):
    return jnp.dot(left, right, preferred_element_type=F32)


def dot_nt(left, right):
    return lax.dot_general(left, right, (((1,), (1,)), ((), ())), preferred_element_type=F32)


def dot_tn(left, right):
    return lax.dot_general(left, right, (((0,), (0,)), ((), ())), preferred_element_type=F32)


def rotary_lanes(row_count):
    half_rot = ROT // 2
    freqs = theta_base ** (-2.0 * jnp.arange(half_rot, dtype=F32) / ROT)
    angles = jnp.arange(row_count, dtype=F32)[:, None] * freqs[None, :]
    cosine, sine = jnp.cos(angles), jnp.sin(angles)
    rest = HEAD - ROT
    one, zero, gap = (
        jnp.ones((row_count, rest), F32),
        jnp.zeros((row_count, half_rot), F32),
        jnp.zeros((row_count, rest), F32),
    )
    cos_head = jnp.concatenate([cosine, cosine, one], axis=1)
    up_head = jnp.concatenate([sine, zero, gap], axis=1)
    down_head = jnp.concatenate([zero, sine, gap], axis=1)
    return tuple(jnp.concatenate([x, x], axis=1) for x in (cos_head, up_head, down_head))


def normalize(block_rows, gain_row, shift_row):
    row_mean = jnp.mean(block_rows, axis=-1, keepdims=True)
    centered = block_rows - row_mean
    inv_std = lax.rsqrt(jnp.mean(centered * centered, axis=-1, keepdims=True) + norm_eps)
    scaled = centered * inv_std
    return (scaled * gain_row + shift_row, scaled, inv_std)


def adam_update(weight, gradient, first_moment, second_moment, step_rate, decay):
    moment_new = beta_one * first_moment + (1.0 - beta_one) * gradient
    square_new = beta_two * second_moment + (1.0 - beta_two) * gradient * gradient
    moment_hat = moment_new / (1.0 - beta_one**STEP)
    square_hat = square_new / (1.0 - beta_two**STEP)
    weight_new = weight - step_rate * (
        moment_hat / (jnp.sqrt(square_hat) + adam_eps) + decay * weight
    )
    return (weight_new, moment_new, square_new)


def bits(count):
    found = []
    step = 1
    while step < count:
        found.append(step)
        step *= 2
    return found


def params(count):
    return pltpu.CompilerParams(
        dimension_semantics=("arbitrary",) * count, vmem_limit_bytes=56 * 2**20
    )


def cost(flops, bytes_moved, transcendentals=0):
    return pl.CostEstimate(
        flops=int(flops), bytes_accessed=int(bytes_moved), transcendentals=int(transcendentals)
    )


def place(here, parts, masks, target, sems, first_sem):
    copies = []
    for n, (part, (ma, mb, my)) in enumerate(zip(parts, masks)):
        copy = pltpu.make_async_copy(
            part, target(here[0] ^ ma, here[2] ^ mb, here[3] ^ my), sems.at[first_sem + n]
        )
        copy.start()
        copies.append(copy)
    return copies


def by_rows(ref, first, count):
    return lambda a, b, y: ref.at[y, a, pl.ds(first, count), b]


def place_gu(here, parts, masks, ref, sems, first_sem):
    count = len(masks)
    copies = []
    for n in range(2):
        cut = parts[n * count].shape[0]
        target = by_rows(ref, n * (ref.shape[2] - cut), cut)
        copies += place(
            here, parts[n * count : (n + 1) * count], masks, target, sems, first_sem + n * count
        )
    return copies


def by_columns(ref, width):
    return lambda a, b, y: ref.at[a, :, b, :, pl.ds(pl.multiple_of(y * width, 128), width)]


def prep_kernel(sizes, n_blocks, head_cols, d_rows, unit, qkv, gu, qkv_out, gu_out):
    n_a, n_t, n_b, _ = sizes
    ff_cols = n_b * d_rows
    for t in range(n_t):
        for block in range(n_blocks):
            at = (block * n_t + t) * head_cols
            qkv_out[t, :, block * head_cols : (block + 1) * head_cols] = qkv[
                :, at : at + head_cols
            ].astype(BF16)
        pieces = []
        gap = jnp.zeros((gu.shape[0], unit - d_rows), F32)
        for a in range(n_a):
            for b in range(n_b):
                at = (a * n_t + t) * ff_cols + b * d_rows
                pieces += [gu[:, at : at + d_rows], gap]
        gu_out[t] = jnp.concatenate(pieces, axis=1).astype(BF16)


def prep(sizes, unit, w_qkv, w_gu, d_rows):
    n_a, n_t, n_b, _ = sizes
    rows = w_qkv.shape[0]
    head_cols = n_b * rows
    n_blocks = w_qkv.shape[1] // (n_t * head_cols)
    tile = 16
    wide_q, wide_g = n_blocks * head_cols, n_a * n_b * unit
    return pl.pallas_call(
        functools.partial(prep_kernel, sizes, n_blocks, head_cols, d_rows, unit),
        grid=(rows // tile,),
        in_specs=[
            pl.BlockSpec((tile, w_qkv.shape[1]), lambda i: (i, 0)),
            pl.BlockSpec((tile, w_gu.shape[1]), lambda i: (i, 0)),
        ],
        out_specs=[
            pl.BlockSpec((n_t, tile, wide_q), lambda i: (0, i, 0)),
            pl.BlockSpec((n_t, tile, wide_g), lambda i: (0, i, 0)),
        ],
        out_shape=[
            jax.ShapeDtypeStruct((n_t, rows, wide_q), BF16),
            jax.ShapeDtypeStruct((n_t, rows, wide_g), BF16),
        ],
        compiler_params=params(1),
        cost_estimate=cost(0, 20 * w_gu.size),
        name="prep",
    )(w_qkv, w_gu)


def adam(weight, gradient, first_moment, second_moment):
    return adam_update(weight, gradient, first_moment, second_moment, rate_matrix, decay_rate)


def finish_gu_kernel(sizes, d_rows, unit, g, w, m, v, w_out, m_out, v_out):
    n_a, n_t, n_b, _ = sizes
    pieces = []
    for a in range(n_a):
        for t in range(n_t):
            for b in range(n_b):
                at = (a * n_b + b) * unit
                pieces.append(g[t, :, at : at + d_rows].astype(F32))
    grad = jnp.concatenate(pieces, axis=1)
    w_out[...], m_out[...], v_out[...] = adam(w[...], grad, m[...], v[...])


def finish_qkv_kernel(sizes, head_cols, g, w, m, v, w_out, m_out, v_out):
    n_t = sizes[1]
    for block in range(w.shape[1] // (n_t * head_cols)):
        for t in range(n_t):
            at = (block * n_t + t) * head_cols
            cols = slice(at, at + head_cols)
            tile, lane = block * head_cols // LANES, block * head_cols % LANES
            grad = g[t, tile, :, lane : lane + head_cols].astype(F32)
            w_out[:, cols], m_out[:, cols], v_out[:, cols] = adam(
                w[:, cols], grad, m[:, cols], v[:, cols]
            )


def finish(kernel, name, gradient, weight, first, second):
    tile = 16
    rows, cols = weight.shape
    matrix = pl.BlockSpec((tile, cols), lambda i: (i, 0))
    lead, lanes = gradient.shape[:-2], gradient.shape[-1]
    gradient_block = pl.BlockSpec(
        lead + (tile, lanes), lambda i: (0,) * len(lead) + (i, 0)
    )
    return pl.pallas_call(
        kernel,
        grid=(rows // tile,),
        in_specs=[
            gradient_block,
            matrix,
            matrix,
            matrix,
        ],
        out_specs=[matrix] * 3,
        out_shape=[jax.ShapeDtypeStruct(weight.shape, F32)] * 3,
        compiler_params=params(1),
        cost_estimate=cost(20 * weight.size, 26 * weight.size),
        name=name,
    )(gradient, weight, first, second)


ANYWHERE = pl.BlockSpec(memory_space=pl.ANY)


def mlp_kernel(masks, steps, here, vec, x_even, x_odd, dy_even, dy_odd, *rest):
    count = len(masks)
    gu_parts, down_parts = rest[: 2 * count], rest[2 * count : 3 * count]
    normed, grads_out, hidden, d_joined, gu, down, rows, sems, row_sems = rest[-9:]
    step = pl.program_id(0)
    slot = normed.shape[0]

    def fetch(n):
        spot = pl.ds(n // 2 * slot, slot)
        sources = (x_odd, dy_odd) if n % 2 else (x_even, dy_even)
        return [
            pltpu.make_async_copy(
                source.at[spot], rows.at[n % 2, pl.ds(m * slot, slot)], row_sems.at[n % 2, m]
            )
            for m, source in enumerate(sources)
        ]

    @pl.when(step == 0)
    def _():
        for copy in fetch(0):
            copy.start()
        copies = place_gu(here, gu_parts, masks, gu, sems, 0)
        target = by_columns(down, down.shape[4] // 2)
        copies += place(here, down_parts, masks, target, sems, 2 * count)
        for copy in copies:
            copy.wait()

    for n in range(steps):

        @pl.when(step == n)
        def _(n=n):
            if n + 1 < steps:
                for copy in fetch(n + 1):
                    copy.start()
            for copy in fetch(n):
                copy.wait()

    now = step % 2
    low = normalize(rows[now, :slot].astype(F32), vec[0:1], vec[1:2])[0].astype(BF16)
    dy = rows[now, slot:]
    normed[...] = low
    grads_out[...] = dy
    wide = gu.shape[5]
    gate = dot(low, gu[0].reshape(-1, wide))
    up = dot(low, gu[1].reshape(-1, wide))
    d_hidden = dot_nt(dy, down[...].reshape(wide, -1))
    sig = jax.nn.sigmoid(gate)
    act = gate * sig
    hidden[...] = (act * up).astype(BF16)
    d_joined[0] = (d_hidden * up * sig * (1.0 + gate * (1.0 - sig))).astype(BF16)
    d_joined[1] = (d_hidden * act).astype(BF16)


def mlp(here, masks, held, vec, gu_parts, down_parts, sizes, unit):
    n_a, n_t, n_b, n_y = sizes
    width = held[0].shape[1]
    slot = held[0].shape[0] * 2 // n_t
    wide = n_a * n_b * unit
    rows = n_t * slot
    w_rows = gu_parts[0].shape[1]
    return pl.pallas_call(
        functools.partial(mlp_kernel, masks, n_t),
        grid_spec=pltpu.PrefetchScalarGridSpec(
            num_scalar_prefetch=1,
            grid=(n_t,),
            in_specs=[pl.BlockSpec(vec.shape, lambda i, h: (0, 0))]
            + [ANYWHERE] * (3 * len(masks) + 4),
            out_specs=[
                pl.BlockSpec((slot, width), lambda i, h: (i, 0)),
                pl.BlockSpec((slot, width), lambda i, h: (i, 0)),
                pl.BlockSpec((slot, wide), lambda i, h: (i, 0)),
                pl.BlockSpec((2, slot, wide), lambda i, h: (0, i, 0)),
            ],
            scratch_shapes=[
                pltpu.VMEM((n_y, n_a, n_t, n_b, w_rows, wide), BF16),
                pltpu.VMEM((n_a, 1, n_b, unit, width), BF16),
                pltpu.VMEM((2, 2 * slot, width), BF16),
                pltpu.SemaphoreType.DMA((3 * len(masks),)),
                pltpu.SemaphoreType.DMA((2, 2)),
            ],
        ),
        out_shape=[
            jax.ShapeDtypeStruct((rows, width), BF16),
            jax.ShapeDtypeStruct((rows, width), BF16),
            jax.ShapeDtypeStruct((rows, wide), BF16),
            jax.ShapeDtypeStruct((2, rows, wide), BF16),
        ],
        compiler_params=params(1),
        name="mlp",
    )(here, vec, *held, *gu_parts, *down_parts)


def attention_kernel(
    masks, here, lengths, normed, dy, bias, cos_ref, up_ref, down_ref, *rest
):
    count = len(masks)
    qkv_parts, out_parts = rest[:count], rest[count : 2 * count]
    o_ref, dqkv_ref, bias_ref, w_qkv, w_out, sems = rest[2 * count :]

    @pl.when(pl.program_id(0) == 0)
    def _():
        copies = place(here, qkv_parts, masks, by_columns(w_qkv, w_qkv.shape[4] // 2), sems, 0)
        copies += place(here, out_parts, masks, by_columns(w_out, w_out.shape[4] // 2), sems, count)
        for copy in copies:
            copy.wait()

    rows = normed.shape[0]
    wide = w_qkv.shape[4]
    width = wide // 3
    qkv = dot(normed[...], w_qkv[...].reshape(-1, wide)) + bias[...]
    dpo = dot_nt(dy[...], w_out[...].reshape(width, -1)).astype(BF16)
    length = lengths[pl.program_id(0)]
    cosine, sine_up, sine_down = cos_ref[...], up_ref[...], down_ref[...]
    query_at = lax.broadcasted_iota(jnp.int32, (rows, rows), 0)
    key_at = lax.broadcasted_iota(jnp.int32, (rows, rows), 1)
    allowed = (key_at <= query_at) & (key_at < length)
    lane = lax.broadcasted_iota(jnp.int32, (rows, 2 * HEAD), 1)
    lower = lane < HEAD
    half = ROT // 2
    scale = HEAD ** (-0.5)

    def turn(x, sign):
        ahead = pltpu.roll(x, 2 * HEAD - half, 1)
        behind = pltpu.roll(x, half, 1)
        return x * cosine + sign * (behind * sine_down - ahead * sine_up)

    for pair in range(width // (2 * HEAD)):
        at = pair * 2 * HEAD
        cols = slice(at, at + 2 * HEAD)
        k_cols = slice(width + at, width + at + 2 * HEAD)
        v_cols = slice(2 * width + at, 2 * width + at + 2 * HEAD)
        q_rot = turn(qkv[:, cols], 1.0).astype(BF16)
        k_rot = turn(qkv[:, k_cols], 1.0).astype(BF16)
        values = qkv[:, v_cols].astype(BF16)
        grad = dpo[:, cols]
        results = []
        for side in range(2):
            mine = lower if side == 0 else ~lower
            scores = dot_nt(jnp.where(mine, q_rot, 0.0).astype(BF16), k_rot) * scale
            masked = jnp.where(allowed, scores, -1e30)
            raised = jnp.exp(masked - jnp.max(masked, axis=1, keepdims=True))
            probs = raised * (1.0 / jnp.sum(raised, axis=1, keepdims=True))
            probs_low = probs.astype(BF16)
            out = dot(probs_low, values)
            d_probs = dot_nt(jnp.where(mine, grad, 0.0).astype(BF16), values)
            d_values = dot_tn(probs_low, grad)
            inner = jnp.sum(probs * d_probs, axis=1, keepdims=True)
            d_scores = (probs * (d_probs - inner)).astype(BF16)
            d_query = dot(d_scores, k_rot) * scale
            d_keys = dot_tn(d_scores, q_rot) * scale
            results.append((out, d_query, d_keys, d_values))
        out, d_query, d_keys, d_values = (
            jnp.where(lower, first, second) for first, second in zip(*results)
        )
        o_ref[:, cols] = out.astype(BF16)
        for spot, value in (
            (cols, turn(d_query, -1.0)),
            (k_cols, turn(d_keys, -1.0)),
            (v_cols, d_values),
        ):
            low = value.astype(BF16)
            dqkv_ref[:, spot] = low
            bias_ref[0, :, spot] = jnp.sum(low.astype(F32), axis=0, keepdims=True)


def attention(here, masks, lengths, tables, normed, dy, bias, qkv_parts, out_parts, sizes):
    n_a, n_t, n_b, _ = sizes
    slots = lengths.shape[0]
    slot, width = dy.shape[0] // slots, dy.shape[1]
    wide = bias.shape[1]
    table = pl.BlockSpec((slot, 2 * HEAD), lambda i, h, lens: (0, 0))
    w_rows = qkv_parts[0].shape[1]
    return pl.pallas_call(
        functools.partial(attention_kernel, masks),
        grid_spec=pltpu.PrefetchScalarGridSpec(
            num_scalar_prefetch=2,
            grid=(n_t,),
            in_specs=[
                pl.BlockSpec((slot, width), lambda i, h, lens: (i, 0)),
                pl.BlockSpec((slot, width), lambda i, h, lens: (i, 0)),
                pl.BlockSpec((1, wide), lambda i, h, lens: (0, 0)),
                table,
                table,
                table,
            ]
            + [ANYWHERE] * (2 * len(masks)),
            out_specs=[
                pl.BlockSpec((slot, wide // 3), lambda i, h, lens: (i, 0)),
                pl.BlockSpec((slot, wide), lambda i, h, lens: (i, 0)),
                pl.BlockSpec((1, 1, wide), lambda i, h, lens: (i, 0, 0)),
            ],
            scratch_shapes=[
                pltpu.VMEM((n_a, n_t, n_b, w_rows, wide), BF16),
                pltpu.VMEM((n_a, 1, n_b, w_rows, width), BF16),
                pltpu.SemaphoreType.DMA((2 * len(masks),)),
            ],
        ),
        out_shape=[
            jax.ShapeDtypeStruct((n_t * slot, wide // 3), BF16),
            jax.ShapeDtypeStruct((n_t * slot, wide), BF16),
            jax.ShapeDtypeStruct((n_t, 1, wide), F32),
        ],
        compiler_params=params(1),
        cost_estimate=cost(
            4 * n_t * slot * width * wide, 5 * n_t * slot * width * 2, n_t * slot * slot * 8
        ),
        name="attention",
    )(here, lengths, normed, dy, bias, *tables, *qkv_parts, *out_parts)


def grads_cols_kernel(where, left, d_sent, d_kept, *outs):
    tall = left[...]
    sent = dot_tn(tall, d_sent[0]).astype(BF16)
    kept = dot_tn(tall, d_kept[0])
    far = pl.program_id(0) < pl.num_programs(0) // 2

    @pl.when(far)
    def _():
        outs[0][...] = sent
        outs[1][...] = kept

    @pl.when(jnp.logical_not(far))
    def _():
        outs[2][...] = sent
        outs[3][...] = kept


def grads_cols(where, normed, d_cols, name):
    rows, width = normed.shape
    wide = d_cols.shape[2]
    half_rows = width // 2
    steps = 4
    tile = half_rows // steps

    def tall(i, w):
        return (0, jnp.where(i < steps, w[0], 1 - w[0]) * steps + i % steps)

    def far(i, w):
        return (jnp.minimum(i, steps - 1), 0)

    def near(i, w):
        return (jnp.maximum(i - steps, 0), 0)

    return pl.pallas_call(
        grads_cols_kernel,
        grid_spec=pltpu.PrefetchScalarGridSpec(
            num_scalar_prefetch=1,
            grid=(2 * steps,),
            in_specs=[
                pl.BlockSpec((rows, tile), tall),
                pl.BlockSpec((1, rows, wide), lambda i, w: (1 - w[1], 0, 0)),
                pl.BlockSpec((1, rows, wide), lambda i, w: (w[1], 0, 0)),
            ],
            out_specs=[pl.BlockSpec((tile, wide), at) for at in (far, far, near, near)],
        ),
        out_shape=[jax.ShapeDtypeStruct((half_rows, wide), t) for t in (BF16, F32, BF16, F32)],
        compiler_params=params(1),
        name=name,
    )(where, normed, d_cols, d_cols)


def grads_rows_kernel(where, far, near, dy_sent, dy_kept, *outs):
    sent, kept = dy_sent[...], dy_kept[...]
    outs[0][...] = dot_tn(far[...], sent).astype(BF16)
    outs[1][...] = dot_tn(far[...], kept)
    outs[2][...] = dot_tn(near[...], sent).astype(BF16)
    outs[3][...] = dot_tn(near[...], kept)


def grads_rows(where, left, dy, name):
    rows, wide = left.shape
    width = dy.shape[1]
    half, dy_half = wide // 2, width // 2
    steps = 4
    tile = dy_half // steps
    block = (rows, tile)
    return pl.pallas_call(
        grads_rows_kernel,
        grid_spec=pltpu.PrefetchScalarGridSpec(
            num_scalar_prefetch=1,
            grid=(steps,),
            in_specs=[
                pl.BlockSpec((rows, half), lambda i, w: (0, w[0])),
                pl.BlockSpec((rows, half), lambda i, w: (0, 1 - w[0])),
                pl.BlockSpec(block, lambda i, w: (0, (1 - w[1]) * steps + i)),
                pl.BlockSpec(block, lambda i, w: (0, w[1] * steps + i)),
            ],
            out_specs=[pl.BlockSpec((half, tile), lambda i, w: (0, i))] * 4,
        ),
        out_shape=[jax.ShapeDtypeStruct((half, dy_half), t) for t in (BF16, F32, BF16, F32)],
        compiler_params=params(1),
        cost_estimate=cost(2 * rows * width * wide, 2 * rows * (width + wide) + 3 * wide * width),
        name=name,
    )(where, left, left, dy, dy)


def grads_attention_kernel(where, tall, d_qkv, left, dy_sent, dy_kept, sent, kept):
    step, steps = pl.program_id(0), pl.num_programs(0)
    tile, half = tall.shape[1], left.shape[1] // 2
    tiles = sent.shape[1] - 1
    part, first = step // (steps // 2), step % (steps // 2) * tile
    result = dot_tn(tall[...], d_qkv[...])
    low, high = result[:, : tiles * LANES], result[:, tiles * LANES :]
    upper = where[1] == 1
    for out, d_cols, dy in (
        (sent, jnp.where(upper, low, high), dy_sent),
        (kept, jnp.where(upper, high, low), dy_kept),
    ):
        d_cols = d_cols.astype(out.dtype)
        spot = pl.ds(pl.multiple_of(first, tile), tile)
        for n in range(tiles):
            out[part, n, spot, :] = d_cols[:, n * LANES : (n + 1) * LANES]
        columns = dot_tn(left[...], dy[...]).astype(out.dtype)
        spot = pl.ds(pl.multiple_of(step * half, half), half)
        out[where[0], tiles, spot, :] = columns[:half]
        out[1 - where[0], tiles, spot, :] = columns[half:]


def grads_attention(where, normed, d_qkv, attended, dy):
    rows, width = normed.shape
    d_half, half, dy_half = d_qkv.shape[1] // 2, attended.shape[1] // 2, width // 2
    steps = dy_half // LANES
    tile = width // steps
    block = (rows, LANES)
    shape = (2, d_half // LANES + 1, steps * half, LANES)
    assert shape[2] == width // 2

    def tall(i, w):
        return (0, jnp.where(i < steps // 2, w[0], 1 - w[0]) * (steps // 2) + i % (steps // 2))

    return pl.pallas_call(
        grads_attention_kernel,
        grid_spec=pltpu.PrefetchScalarGridSpec(
            num_scalar_prefetch=1,
            grid=(steps,),
            in_specs=[
                pl.BlockSpec((rows, tile), tall),
                pl.BlockSpec((rows, 2 * d_half), lambda i, w: (0, 0)),
                pl.BlockSpec((rows, 2 * half), lambda i, w: (0, 0)),
                pl.BlockSpec(block, lambda i, w: (0, (1 - w[1]) * steps + i)),
                pl.BlockSpec(block, lambda i, w: (0, w[1] * steps + i)),
            ],
            out_specs=[pl.BlockSpec(shape, lambda i, w: (0, 0, 0, 0))] * 2,
        ),
        out_shape=[jax.ShapeDtypeStruct(shape, t) for t in (BF16, F32)],
        compiler_params=params(1),
        name="grads_attention",
    )(where, normed, d_qkv, attended, dy, dy)


def row_blocks(kernel, name, here, kept, inputs, parts, scratch, slot, width, n_t):
    def slot_of(i, h):
        lowest = (i < n_t // 2).astype(jnp.int32) if kept is None else 1 - kept
        return i % 2 * 4 + i // 2 % 2 * 2 + lowest

    half = n_t // 2
    blocks = [lambda i, h: (i, 0)]
    if kept is None:
        blocks = [
            lambda i, h: (jnp.minimum(i, half - 1), 0),
            lambda i, h: (jnp.maximum(i - half, 0), 0),
        ]

    in_specs = []
    for value in inputs:
        block = (slot, value.shape[-1])
        if value.ndim == 3:
            block = (value.shape[0],) + block
            in_specs.append(pl.BlockSpec(block, lambda i, h: (0, slot_of(i, h), 0)))
        else:
            in_specs.append(pl.BlockSpec(block, lambda i, h: (slot_of(i, h), 0)))
    return pl.pallas_call(
        kernel,
        grid_spec=pltpu.PrefetchScalarGridSpec(
            num_scalar_prefetch=1,
            grid=(half * len(blocks),),
            in_specs=in_specs + [ANYWHERE] * len(parts),
            out_specs=[pl.BlockSpec((slot, width), block) for block in blocks],
            scratch_shapes=scratch + [pltpu.SemaphoreType.DMA((len(parts),))],
        ),
        out_shape=[jax.ShapeDtypeStruct((half * slot, width), BF16)] * len(blocks),
        compiler_params=params(1),
        name=name if kept is None else name + ("_kept" if kept else "_sent"),
    )(here, *inputs, *parts)


def branch_kernel(masks, here, o, hidden, *rest):
    count = len(masks)
    out_parts, down_parts = rest[:count], rest[count : 2 * count]
    *outs, w_out, down, sems = rest[2 * count :]

    @pl.when(pl.program_id(0) == 0)
    def _():
        copies = place(here, out_parts, masks, by_columns(w_out, w_out.shape[4] // 2), sems, 0)
        copies += place(here, down_parts, masks, by_columns(down, down.shape[4] // 2), sems, count)
        for copy in copies:
            copy.wait()

    width = w_out.shape[4]
    branch = dot(o[...], w_out[...].reshape(-1, width))
    branch += dot(hidden[...], down[...].reshape(-1, width))
    branch, step, half = branch.astype(BF16), pl.program_id(0), pl.num_programs(0) // 2

    @pl.when(step < half)
    def _():
        outs[0][...] = branch

    @pl.when(step >= half)
    def _():
        outs[1][...] = branch


def normal_kernel(masks, here, d_qkv, d_joined, *rest):
    count = len(masks)
    qkv_parts, gu_parts = rest[:count], rest[count : 3 * count]
    out, w_qkv, gu, sems = rest[3 * count :]

    @pl.when(pl.program_id(0) == 0)
    def _():
        copies = place(here, qkv_parts, masks, by_columns(w_qkv, w_qkv.shape[4] // 2), sems, 0)
        copies += place_gu(here, gu_parts, masks, gu, sems, count)
        for copy in copies:
            copy.wait()

    wide = w_qkv.shape[4]
    width = w_qkv.size // wide
    normal = dot_nt(d_qkv[...], w_qkv[...].reshape(width, -1))
    normal += dot_nt(d_joined[0], gu[0].reshape(width, -1))
    normal += dot_nt(d_joined[1], gu[1].reshape(width, -1))
    out[...] = normal.astype(BF16)


def after(value, *others):
    return lax.optimization_barrier((value,) + others)[0]


def per_device(
    sizes,
    tokens,
    cotangent,
    lengths,
    w_qkv,
    w_out,
    w_gate_up,
    w_down,
    vectors,
    first_qkv,
    first_out,
    first_gate_up,
    first_down,
    first_vectors,
    second_qkv,
    second_out,
    second_gate_up,
    second_down,
    second_vectors,
):
    barrier = lax.optimization_barrier
    n_a, n_t, n_b, n_y = sizes
    total = n_a * n_t * n_b * n_y
    at_a, at_t, at_b, at_y = (lax.axis_index(name).astype(jnp.int32) for name in AXES)
    here = jnp.stack([at_a, at_t, at_b, at_y])
    row_count, width = tokens.shape
    w_rows = w_qkv.shape[0]
    d_rows = w_down.shape[0]
    head_cols = n_b * w_rows
    unit = d_rows
    while unit % 16 or n_a * n_b * unit % 128:
        unit += 1

    def swap(value, name, step):
        mask = {"y": 1, "b": n_y, "t": n_y * n_b, "a": n_y * n_b * n_t}[name] * step
        return lax.ppermute(value, AXES, [(i, i ^ mask) for i in range(total)])

    def exchange(value):
        return lax.all_to_all(value, "t", split_axis=0, concat_axis=0, tiled=True)

    r_bits = [("a", s) for s in reversed(bits(n_a))] + [("b", s) for s in bits(n_b)]
    masks = [(0, 0, 0)]
    for name, step in r_bits:
        masks = masks + [
            (m[0] + step * (name == "a"), m[1] + step * (name == "b"), 0) for m in masks
        ]
    masks = tuple(masks + [(m[0], m[1], 1) for m in masks])

    small = 5 * vectors.shape[1] + lengths.shape[1]
    padded = -(-small // 128) * 128
    packed = jnp.concatenate(
        [
            vectors.reshape(1, 1, -1),
            lengths.astype(F32).reshape(1, 1, -1),
            jnp.zeros((1, 1, padded - small), F32),
        ],
        axis=2,
    )
    packed = jnp.broadcast_to(packed, (total, 1, padded))
    packed = lax.all_to_all(packed, AXES, split_axis=0, concat_axis=0, tiled=True)
    packed = packed.reshape(total, padded)

    def spread_top(part):
        parts = [part]
        for name, step in r_bits:
            parts = parts + [swap(p, name, step) for p in parts]
        return parts

    def over_y(value):
        return swap(value, "y", 1)

    def over_y_rest(parts):
        return [over_y(part) for part in parts[1:]]

    def over_top(value):
        return swap(value.astype(BF16), "a", top)

    def summed(kept, *got):
        return functools.reduce(lambda one, two: one.astype(F32) + two.astype(F32), got, kept)

    top = n_a // 2
    down_own = jnp.pad(w_down.astype(BF16), ((0, unit - d_rows), (0, 0)))[None]
    out_own = w_out.astype(BF16)[None]
    qkv_own, gu_own = prep(sizes, unit, w_qkv, w_gate_up, d_rows)
    x_top, x_middle, down_parts, down_other, qkv_own, gu_own, out_own, packed = barrier(
        (
            swap(tokens, "t", n_t // 2),
            swap(tokens, "t", n_t // 4),
            spread_top(down_own),
            over_y(down_own),
            qkv_own,
            gu_own,
            out_own,
            packed,
        )
    )
    all_vectors = packed[:, : 5 * vectors.shape[1]].reshape(total, 5, -1)
    all_vectors = all_vectors.transpose(1, 0, 2).reshape(5, width)
    group = packed[:, 5 * vectors.shape[1] : small].reshape(n_a, n_t, n_b, n_y, -1)
    group = lax.dynamic_index_in_dim(group, at_a, 0, keepdims=False)
    group = lax.dynamic_index_in_dim(group, at_b, 1, keepdims=False)
    group = jnp.where(at_y == 1, group[:, 0, 1], group[:, 0, 0])
    group = group.reshape(2, 2, 2)
    for dim, step in enumerate((4, 2, 1)):
        group = jnp.where(at_t // step % 2 == 1, jnp.flip(group, dim), group)
    slot_lengths = jnp.round(group.reshape(-1)).astype(jnp.int32)
    bias = all_vectors[2:5].reshape(3 * n_a, n_t, head_cols)
    bias = lax.dynamic_index_in_dim(bias, at_t, 1, keepdims=False).reshape(1, -1)
    vec = all_vectors[:2]
    tables = rotary_lanes(row_count)

    gu_own, out_parts, out_other, cotangent, vec, bias, slot_lengths, tables = barrier(
        (
            exchange(gu_own),
            spread_top(out_own),
            over_y(out_own),
            cotangent,
            vec,
            bias,
            slot_lengths,
            tables,
        )
    )
    cut = n_t * 5 // 8
    gu_first, gu_second = barrier((gu_own[:cut], gu_own[cut:]))
    gu_parts, gu_other, down_far, dy_top, dy_middle, gu_second, qkv_own, x_top = barrier(
        (
            spread_top(gu_first),
            over_y(gu_first),
            over_y_rest(down_parts),
            swap(cotangent, "t", n_t // 2),
            swap(cotangent, "t", n_t // 4),
            gu_second,
            qkv_own,
            x_top,
        )
    )
    down_parts = down_parts + [down_other] + down_far
    gu_two, gu_two_other, gu_far, x_far, dy_far, qkv_own = barrier(
        (
            spread_top(gu_second),
            over_y(gu_second),
            over_y_rest(gu_parts),
            swap(x_top, "t", n_t // 4),
            swap(dy_top, "t", n_t // 4),
            qkv_own,
        )
    )
    x_even = jnp.concatenate([tokens, x_middle, x_top, x_far], axis=0)
    dy_even = jnp.concatenate([cotangent, dy_middle, dy_top, dy_far], axis=0)
    gu_two_far, qkv_own, x_odd, dy_odd = barrier(
        (
            over_y_rest(gu_two),
            exchange(qkv_own),
            swap(x_even, "t", 1),
            swap(dy_even, "t", 1),
        )
    )
    gu_parts = gu_parts + [gu_other] + gu_far + gu_two + [gu_two_other] + gu_two_far


    top = n_a // 2
    upper = at_a // top % 2
    other_half = jnp.stack([1 - upper, at_y])
    lower_bits = r_bits[1:]

    def over_rest(value, parts_shape):
        summed = value.reshape(parts_shape + (value.shape[-1],))
        for name, step in lower_bits:
            dim = 0 if name == "a" else 2
            at = at_a if name == "a" else at_b
            size = summed.shape[dim] // 2
            low_half = lax.slice_in_dim(summed, 0, size, axis=dim)
            high_half = lax.slice_in_dim(summed, size, 2 * size, axis=dim)
            is_upper = (at // step) % 2 == 1
            keep = jnp.where(is_upper, high_half, low_half)
            send = jnp.where(is_upper, low_half, high_half)
            summed = keep + swap(send.astype(BF16), name, step).astype(F32)
        return summed.reshape(summed.shape[1], summed.shape[3], summed.shape[4])

    def piece(raw, middle_bit, top_bit, left):
        columns = slice(0, split) if left else slice(split, width)
        got, kept = (part.reshape(2, 2, row_count, width) for part in raw)
        spot = (middle_bit, top_bit, slice(None), columns)
        return got[spot].astype(F32) + kept[spot].astype(F32)

    split = width * 5 // 8
    every = slice(None)

    def first_sends(raw):
        return piece(raw, 1, every, True).astype(BF16), piece(raw, every, 1, False).astype(BF16)

    def first_swaps(sends):
        return swap(sends[0], "t", n_t // 4), swap(sends[1], "t", n_t // 2)

    def second_sends(raw, got):
        left = piece(raw, 0, 1, True) + got[0][1].astype(F32)
        right = piece(raw, 1, 0, False) + got[1][1].astype(F32)
        return left.astype(BF16), right.astype(BF16)

    def second_swaps(sends):
        return swap(sends[0], "t", n_t // 2), swap(sends[1], "t", n_t // 4)

    def whole_rows(raw, got, last):
        left = piece(raw, 0, 0, True) + got[0][0].astype(F32) + last[0].astype(F32)
        right = piece(raw, 0, 0, False) + got[1][0].astype(F32) + last[1].astype(F32)
        return jnp.concatenate([left, right], axis=1)

    half_width = width // 2
    shape_w = (top, n_t, n_b, w_rows)
    normed, dy, hidden, d_joined = mlp(
        after(here, qkv_own),
        masks,
        (x_even, x_odd, dy_even, dy_odd),
        vec,
        gu_parts,
        down_parts,
        sizes,
        unit,
    )
    qkv_parts, qkv_other, out_far, normed, dy, hidden, d_joined = barrier(
        (
            spread_top(qkv_own),
            over_y(qkv_own),
            over_y_rest(out_parts),
            normed,
            dy,
            hidden,
            d_joined,
        )
    )

    out_parts = out_parts + [out_other] + out_far
    qkv_far = over_y_rest(qkv_parts)
    down_far_sent, down_far_kept, down_sent, down_kept = grads_rows(
        other_half, hidden, dy, "grads_down"
    )
    qkv_far, down_far_sent, down_sent, down_kept = barrier(
        (qkv_far, down_far_sent, down_sent, down_kept)
    )
    down_far_got = over_y(down_far_sent)
    gu_far_sent, gu_far_kept, gu_sent, gu_kept = grads_cols(
        after(other_half, down_kept), normed, d_joined, "grads_gate_up"
    )
    down_far_got, gu_far_sent, down_sent, gu_sent, gu_kept = barrier(
        (down_far_got, gu_far_sent, down_sent, gu_sent, gu_kept)
    )
    qkv_parts = qkv_parts + [qkv_other] + qkv_far

    down_far = barrier(summed(down_far_kept, down_far_got).astype(BF16))
    attended, d_qkv, bias_sums = attention(
        after(here, down_far),
        masks,
        slot_lengths,
        tables,
        normed,
        dy,
        bias,
        qkv_parts,
        out_parts,
        sizes,
    )
    gu_rows = gu_sent.shape[0] // 2
    down_far_got, gu_far_got, down_sent, gu_sent, attended, d_qkv = barrier(
        (
            over_top(down_far),
            over_y(gu_far_sent),
            down_sent,
            (gu_sent[:gu_rows], gu_sent[gu_rows:]),
            attended,
            d_qkv,
        )
    )

    def thirds(value):
        value = value.reshape(value.shape[0] // (n_b * w_rows), n_b * w_rows, -1)
        cuts = [n * value.shape[1] // 8 for n in (0, 2, 5, 8)]
        return [value[:, low:high] for low, high in zip(cuts, cuts[1:])]

    gu_far = [summed(k, g).astype(BF16) for k, g in zip(thirds(gu_far_kept), thirds(gu_far_got))]
    gu_far = barrier(gu_far)
    branch_sent, branch_kept = row_blocks(
        functools.partial(branch_kernel, masks),
        "branch_rows",
        after(here, *gu_far),
        None,
        inputs=(attended, hidden),
        parts=out_parts + down_parts,
        scratch=[
            pltpu.VMEM((n_a, 1, n_b, w_rows, width), BF16),
            pltpu.VMEM((n_a, 1, n_b, unit, width), BF16),
        ],
        slot=row_count,
        width=width,
        n_t=n_t,
    )
    gu_far_one, gu_got, gu_far, branch_sent, branch_kept, gu_sent = barrier(
        (
            over_top(gu_far[0]),
            over_y(gu_sent[0]),
            gu_far,
            branch_sent,
            branch_kept,
            gu_sent[1],
        )
    )

    qo_sent, qo_kept = grads_attention(
        after(other_half, branch_sent), normed, d_qkv, attended, dy
    )
    gu_far_two, branch_got, gu_got_more, gu_far, qo_far_sent, qo_sent = barrier(
        (
            over_top(gu_far[1]),
            swap(branch_sent, "t", 1),
            over_y(gu_sent),
            gu_far,
            qo_sent[0],
            qo_sent[1],
        )
    )

    normal_rows = functools.partial(
        row_blocks,
        functools.partial(normal_kernel, masks),
        "normal_rows",
        inputs=(d_qkv, d_joined),
        parts=qkv_parts + gu_parts,
        scratch=[
            pltpu.VMEM((n_a, n_t, n_b, w_rows, d_qkv.shape[1]), BF16),
            pltpu.VMEM((n_y, n_a, n_t, n_b, w_rows, n_a * n_b * unit), BF16),
        ],
        slot=row_count,
        width=width,
        n_t=n_t,
    )
    branch = (branch_got, branch_kept)
    branch_sends = barrier(first_sends(branch))
    (normal_sent,) = normal_rows(after(here, qo_far_sent, *branch_sends), 0)
    gu_far_three, qo_far_got, branch_got, normal_sent, qo_sent, down_sent = barrier(
        (
            over_top(gu_far[2]),
            over_y(qo_far_sent),
            first_swaps(branch_sends),
            normal_sent,
            qo_sent,
            down_sent,
        )
    )
    qo_far = summed(qo_kept[0], qo_far_got).astype(BF16)
    gu_got = jnp.concatenate([gu_got, gu_got_more], axis=0)
    gu_far_got = jnp.concatenate([gu_far_one, gu_far_two, gu_far_three], axis=1)
    g_gu = summed(gu_kept, gu_got, gu_far_got.reshape(gu_kept.shape))
    g_gu = over_rest(g_gu, shape_w).astype(BF16)
    qo_far_one, qo_far_two, g_gu = barrier((qo_far[:1], qo_far[1:], g_gu))
    (normal_kept,) = normal_rows(after(here, normal_sent, g_gu), 1)
    qo_far_one, normal_got, qo_got, g_gu, normal_kept, qo_far_two, down_sent, branch_got = barrier(
        (
            over_top(qo_far_one),
            swap(normal_sent, "t", 1),
            over_y(qo_sent),
            exchange(g_gu),
            normal_kept,
            qo_far_two,
            down_sent,
            branch_got,
        )
    )

    qo_far_two, down_got = over_top(qo_far_two), over_y(down_sent)
    normal = (normal_got, normal_kept)
    normal_sends = barrier(first_sends(normal))
    new_gu, moment_gu, square_gu = finish(
        functools.partial(finish_gu_kernel, sizes, d_rows, unit),
        "finish_gate_up",
        after(g_gu, *normal_sends),
        w_gate_up,
        first_gate_up,
        second_gate_up,
    )
    branch_sends = second_sends(branch, [after(got, *normal_sends) for got in branch_got])
    normal_got, qo_far_two, down_got, branch_sends, new_gu = barrier(
        (first_swaps(normal_sends), qo_far_two, down_got, branch_sends, new_gu)
    )

    normal_sends = barrier(second_sends(normal, normal_got))
    qo_far_got = jnp.concatenate([qo_far_one, qo_far_two], axis=0)
    qo = after(summed(qo_kept[1], qo_got, qo_far_got), *normal_sends)
    g_qkv = over_rest(qo[:-1].transpose(1, 0, 2).reshape(qo.shape[1], -1), shape_w)
    g_out = qo[-1].reshape(half_width // LANES, -1, LANES).transpose(1, 0, 2)
    g_out = over_rest(g_out.reshape(-1, half_width), (top, 1, n_b, w_rows))
    g_qkv = g_qkv.astype(BF16).reshape(n_t, w_rows, -1, LANES).transpose(0, 2, 1, 3)
    g_qkv = barrier(g_qkv)
    g_down = summed(down_kept, down_got, down_far_got)
    g_down = over_rest(after(g_down, g_qkv), (top, 1, n_b, unit))
    new_down, moment_down, square_down = adam(w_down, g_down[0, :d_rows], first_down, second_down)
    g_qkv, normal_last, g_out, branch_sends, new_down = barrier(
        (g_qkv, second_swaps(normal_sends), g_out, branch_sends, new_down)
    )
    g_qkv = exchange(g_qkv)
    branch_last = second_swaps(branch_sends)
    normal_own = whole_rows(normal, normal_got, normal_last)
    _, scaled_own, inv_own = normalize(tokens.astype(F32), vec[0], vec[1])
    d_scaled = normal_own * vec[0]
    input_grad = cotangent.astype(F32) + inv_own * (
        d_scaled
        - jnp.mean(d_scaled, axis=-1, keepdims=True)
        - scaled_own * jnp.mean(d_scaled * scaled_own, axis=-1, keepdims=True)
    )
    g_bias = jnp.sum(bias_sums, axis=0).reshape(3 * n_a, 1, head_cols)
    is_here = (jnp.arange(n_t) == at_t)[None, :, None]
    g_bias = jnp.where(is_here, g_bias, 0.0).reshape(3, width)
    vector_part = jnp.concatenate(
        [
            jnp.sum(normal_own * scaled_own, axis=0)[None],
            jnp.sum(normal_own, axis=0)[None],
            g_bias,
        ],
        axis=0,
    )
    vector_part = vector_part.reshape(5, total, -1).transpose(1, 0, 2).reshape(total, 1, -1)
    vector_part = jnp.pad(vector_part, ((0, 0), (0, 0), (0, -vector_part.shape[2] % 128)))
    vector_part = lax.all_to_all(vector_part, AXES, split_axis=0, concat_axis=0, tiled=True)
    vector_grad = jnp.sum(vector_part, axis=0)[0, : vectors.size].reshape(vectors.shape)
    branch_own = whole_rows(branch, branch_got, branch_last)
    output = (tokens.astype(F32) + after(branch_own, vector_part)).astype(BF16)
    new_out, moment_out, square_out = adam(w_out, g_out[0], first_out, second_out)
    new_qkv, moment_qkv, square_qkv = finish(
        functools.partial(finish_qkv_kernel, sizes, head_cols),
        "finish_qkv",
        g_qkv,
        w_qkv,
        first_qkv,
        second_qkv,
    )
    new_vec, moment_vec, square_vec = adam_update(
        vectors, vector_grad, first_vectors, second_vectors, rate_vector, 0.0
    )
    return (
        output,
        input_grad.astype(BF16),
        new_qkv,
        new_out,
        new_gu,
        new_down,
        new_vec,
        moment_qkv,
        moment_out,
        moment_gu,
        moment_down,
        moment_vec,
        square_qkv,
        square_out,
        square_gu,
        square_down,
        square_vec,
    )


def solution(mesh):
    n_dp, n_y = mesh.shape["dp"], mesh.shape["branch"]
    n_b = max(1, HEAD * n_dp // (HEADS * HEAD))
    n_t = min(SLICES, n_dp // n_b)
    sizes = (n_dp // (n_t * n_b), n_t, n_b, n_y)
    split = Mesh(mesh.devices.reshape(sizes), AXES)
    dp = ("a", "t", "b")
    rows = P(AXES, None)
    matrix = P(dp, "y")
    vector = P(None, AXES)
    weights = (matrix, matrix, matrix, matrix, vector)
    return jax.shard_map(
        functools.partial(per_device, sizes),
        mesh=split,
        in_specs=(rows, rows, P(dp, None)) + weights * 3,
        out_specs=(rows, rows) + weights * 3,
        check_vma=False,
    )
```

```python
import functools

import jax
import jax.numpy as jnp
from jax import lax
from jax.experimental import pallas as pl
from jax.experimental.pallas import tpu as pltpu
from jax.sharding import Mesh, PartitionSpec as P

HEADS = 32
HEAD = 64
ROT = 16
MB = 2
STEP = 10
SLICES = 8
LANES = 128

theta_base = 10000.0
norm_eps = 1e-05
beta_one = 0.9
beta_two = 0.95
adam_eps = 1e-08
decay_rate = 0.1
rate_matrix = 0.05
rate_vector = 1.0

AXES = ("a", "t", "b", "y")
F32 = jnp.float32
BF16 = jnp.bfloat16


def dot(left, right):
    return jnp.dot(left, right, preferred_element_type=F32)


def dot_nt(left, right):
    return lax.dot_general(left, right, (((1,), (1,)), ((), ())), preferred_element_type=F32)


def dot_tn(left, right):
    return lax.dot_general(left, right, (((0,), (0,)), ((), ())), preferred_element_type=F32)


def rotary_lanes(row_count):
    half_rot = ROT // 2
    freqs = theta_base ** (-2.0 * jnp.arange(half_rot, dtype=F32) / ROT)
    angles = jnp.arange(row_count, dtype=F32)[:, None] * freqs[None, :]
    cosine, sine = jnp.cos(angles), jnp.sin(angles)
    rest = HEAD - ROT
    one, zero, gap = (
        jnp.ones((row_count, rest), F32),
        jnp.zeros((row_count, half_rot), F32),
        jnp.zeros((row_count, rest), F32),
    )
    cos_head = jnp.concatenate([cosine, cosine, one], axis=1)
    up_head = jnp.concatenate([sine, zero, gap], axis=1)
    down_head = jnp.concatenate([zero, sine, gap], axis=1)
    return tuple(jnp.concatenate([x, x], axis=1) for x in (cos_head, up_head, down_head))


def normalize(block_rows, gain_row, shift_row):
    row_mean = jnp.mean(block_rows, axis=-1, keepdims=True)
    centered = block_rows - row_mean
    inv_std = lax.rsqrt(jnp.mean(centered * centered, axis=-1, keepdims=True) + norm_eps)
    scaled = centered * inv_std
    return (scaled * gain_row + shift_row, scaled, inv_std)


def adam_update(weight, gradient, first_moment, second_moment, step_rate, decay):
    moment_new = beta_one * first_moment + (1.0 - beta_one) * gradient
    square_new = beta_two * second_moment + (1.0 - beta_two) * gradient * gradient
    moment_hat = moment_new / (1.0 - beta_one**STEP)
    square_hat = square_new / (1.0 - beta_two**STEP)
    weight_new = weight - step_rate * (
        moment_hat / (jnp.sqrt(square_hat) + adam_eps) + decay * weight
    )
    return (weight_new, moment_new, square_new)


def bits(count):
    found = []
    step = 1
    while step < count:
        found.append(step)
        step *= 2
    return found


def params(count):
    return pltpu.CompilerParams(
        dimension_semantics=("arbitrary",) * count, vmem_limit_bytes=56 * 2**20
    )


def cost(flops, bytes_moved, transcendentals=0):
    return pl.CostEstimate(
        flops=int(flops), bytes_accessed=int(bytes_moved), transcendentals=int(transcendentals)
    )


def place(here, parts, masks, target, sems, first_sem):
    copies = []
    for n, (part, (ma, mb, my)) in enumerate(zip(parts, masks)):
        copy = pltpu.make_async_copy(
            part, target(here[0] ^ ma, here[2] ^ mb, here[3] ^ my), sems.at[first_sem + n]
        )
        copy.start()
        copies.append(copy)
    return copies


def by_rows(ref, first, count):
    return lambda a, b, y: ref.at[y, a, pl.ds(first, count), b]


def place_gu(here, parts, masks, ref, sems, first_sem):
    count = len(masks)
    copies = []
    for n in range(2):
        cut = parts[n * count].shape[0]
        target = by_rows(ref, n * (ref.shape[2] - cut), cut)
        copies += place(
            here, parts[n * count : (n + 1) * count], masks, target, sems, first_sem + n * count
        )
    return copies


def by_columns(ref, width):
    return lambda a, b, y: ref.at[a, :, b, :, pl.ds(pl.multiple_of(y * width, 128), width)]


def prep_kernel(sizes, n_blocks, head_cols, d_rows, unit, qkv, gu, qkv_out, gu_out):
    n_a, n_t, n_b, _ = sizes
    ff_cols = n_b * d_rows
    for t in range(n_t):
        for block in range(n_blocks):
            at = (block * n_t + t) * head_cols
            qkv_out[t, :, block * head_cols : (block + 1) * head_cols] = qkv[
                :, at : at + head_cols
            ].astype(BF16)
        pieces = []
        gap = jnp.zeros((gu.shape[0], unit - d_rows), F32)
        for a in range(n_a):
            for b in range(n_b):
                at = (a * n_t + t) * ff_cols + b * d_rows
                pieces += [gu[:, at : at + d_rows], gap]
        gu_out[t] = jnp.concatenate(pieces, axis=1).astype(BF16)


def prep(sizes, unit, w_qkv, w_gu, d_rows):
    n_a, n_t, n_b, _ = sizes
    rows = w_qkv.shape[0]
    head_cols = n_b * rows
    n_blocks = w_qkv.shape[1] // (n_t * head_cols)
    tile = 16
    wide_q, wide_g = n_blocks * head_cols, n_a * n_b * unit
    return pl.pallas_call(
        functools.partial(prep_kernel, sizes, n_blocks, head_cols, d_rows, unit),
        grid=(rows // tile,),
        in_specs=[
            pl.BlockSpec((tile, w_qkv.shape[1]), lambda i: (i, 0)),
            pl.BlockSpec((tile, w_gu.shape[1]), lambda i: (i, 0)),
        ],
        out_specs=[
            pl.BlockSpec((n_t, tile, wide_q), lambda i: (0, i, 0)),
            pl.BlockSpec((n_t, tile, wide_g), lambda i: (0, i, 0)),
        ],
        out_shape=[
            jax.ShapeDtypeStruct((n_t, rows, wide_q), BF16),
            jax.ShapeDtypeStruct((n_t, rows, wide_g), BF16),
        ],
        compiler_params=params(1),
        cost_estimate=cost(0, 20 * w_gu.size),
        name="prep",
    )(w_qkv, w_gu)


def adam(weight, gradient, first_moment, second_moment):
    return adam_update(weight, gradient, first_moment, second_moment, rate_matrix, decay_rate)


def finish_gu_kernel(sizes, d_rows, unit, g, w, m, v, w_out, m_out, v_out):
    n_a, n_t, n_b, _ = sizes
    pieces = []
    for a in range(n_a):
        for t in range(n_t):
            for b in range(n_b):
                at = (a * n_b + b) * unit
                pieces.append(g[t, :, at : at + d_rows].astype(F32))
    grad = jnp.concatenate(pieces, axis=1)
    w_out[...], m_out[...], v_out[...] = adam(w[...], grad, m[...], v[...])


def finish_qkv_kernel(sizes, head_cols, g, w, m, v, w_out, m_out, v_out):
    n_t = sizes[1]
    for block in range(w.shape[1] // (n_t * head_cols)):
        for t in range(n_t):
            at = (block * n_t + t) * head_cols
            cols = slice(at, at + head_cols)
            tile, lane = block * head_cols // LANES, block * head_cols % LANES
            grad = g[t, tile, :, lane : lane + head_cols].astype(F32)
            w_out[:, cols], m_out[:, cols], v_out[:, cols] = adam(
                w[:, cols], grad, m[:, cols], v[:, cols]
            )


def finish(kernel, name, gradient, weight, first, second):
    tile = 16
    rows, cols = weight.shape
    matrix = pl.BlockSpec((tile, cols), lambda i: (i, 0))
    lead, lanes = gradient.shape[:-2], gradient.shape[-1]
    gradient_block = pl.BlockSpec(
        lead + (tile, lanes), lambda i: (0,) * len(lead) + (i, 0)
    )
    return pl.pallas_call(
        kernel,
        grid=(rows // tile,),
        in_specs=[
            gradient_block,
            matrix,
            matrix,
            matrix,
        ],
        out_specs=[matrix] * 3,
        out_shape=[jax.ShapeDtypeStruct(weight.shape, F32)] * 3,
        compiler_params=params(1),
        cost_estimate=cost(20 * weight.size, 26 * weight.size),
        name=name,
    )(gradient, weight, first, second)


ANYWHERE = pl.BlockSpec(memory_space=pl.ANY)


def mlp_kernel(masks, steps, here, vec, x_even, x_odd, dy_even, dy_odd, *rest):
    count = len(masks)
    gu_parts, down_parts = rest[: 2 * count], rest[2 * count : 3 * count]
    normed, grads_out, hidden, d_joined, gu, down, rows, sems, row_sems = rest[-9:]
    step = pl.program_id(0)
    slot = normed.shape[0]

    def fetch(n):
        spot = pl.ds(n // 2 * slot, slot)
        sources = (x_odd, dy_odd) if n % 2 else (x_even, dy_even)
        return [
            pltpu.make_async_copy(
                source.at[spot], rows.at[n % 2, pl.ds(m * slot, slot)], row_sems.at[n % 2, m]
            )
            for m, source in enumerate(sources)
        ]

    @pl.when(step == 0)
    def _():
        for copy in fetch(0):
            copy.start()
        copies = place_gu(here, gu_parts, masks, gu, sems, 0)
        target = by_columns(down, down.shape[4] // 2)
        copies += place(here, down_parts, masks, target, sems, 2 * count)
        for copy in copies:
            copy.wait()

    for n in range(steps):

        @pl.when(step == n)
        def _(n=n):
            if n + 1 < steps:
                for copy in fetch(n + 1):
                    copy.start()
            for copy in fetch(n):
                copy.wait()

    now = step % 2
    low = normalize(rows[now, :slot].astype(F32), vec[0:1], vec[1:2])[0].astype(BF16)
    dy = rows[now, slot:]
    normed[...] = low
    grads_out[...] = dy
    wide = gu.shape[5]
    gate = dot(low, gu[0].reshape(-1, wide))
    up = dot(low, gu[1].reshape(-1, wide))
    d_hidden = dot_nt(dy, down[...].reshape(wide, -1))
    sig = jax.nn.sigmoid(gate)
    act = gate * sig
    hidden[...] = (act * up).astype(BF16)
    d_joined[0] = (d_hidden * up * sig * (1.0 + gate * (1.0 - sig))).astype(BF16)
    d_joined[1] = (d_hidden * act).astype(BF16)


def mlp(here, masks, held, vec, gu_parts, down_parts, sizes, unit):
    n_a, n_t, n_b, n_y = sizes
    width = held[0].shape[1]
    slot = held[0].shape[0] * 2 // n_t
    wide = n_a * n_b * unit
    rows = n_t * slot
    w_rows = gu_parts[0].shape[1]
    return pl.pallas_call(
        functools.partial(mlp_kernel, masks, n_t),
        grid_spec=pltpu.PrefetchScalarGridSpec(
            num_scalar_prefetch=1,
            grid=(n_t,),
            in_specs=[pl.BlockSpec(vec.shape, lambda i, h: (0, 0))]
            + [ANYWHERE] * (3 * len(masks) + 4),
            out_specs=[
                pl.BlockSpec((slot, width), lambda i, h: (i, 0)),
                pl.BlockSpec((slot, width), lambda i, h: (i, 0)),
                pl.BlockSpec((slot, wide), lambda i, h: (i, 0)),
                pl.BlockSpec((2, slot, wide), lambda i, h: (0, i, 0)),
            ],
            scratch_shapes=[
                pltpu.VMEM((n_y, n_a, n_t, n_b, w_rows, wide), BF16),
                pltpu.VMEM((n_a, 1, n_b, unit, width), BF16),
                pltpu.VMEM((2, 2 * slot, width), BF16),
                pltpu.SemaphoreType.DMA((3 * len(masks),)),
                pltpu.SemaphoreType.DMA((2, 2)),
            ],
        ),
        out_shape=[
            jax.ShapeDtypeStruct((rows, width), BF16),
            jax.ShapeDtypeStruct((rows, width), BF16),
            jax.ShapeDtypeStruct((rows, wide), BF16),
            jax.ShapeDtypeStruct((2, rows, wide), BF16),
        ],
        compiler_params=params(1),
        name="mlp",
    )(here, vec, *held, *gu_parts, *down_parts)


def attention_kernel(
    masks, here, lengths, normed, dy, bias, cos_ref, up_ref, down_ref, *rest
):
    count = len(masks)
    qkv_parts, out_parts = rest[:count], rest[count : 2 * count]
    o_ref, dqkv_ref, bias_ref, w_qkv, w_out, sems = rest[2 * count :]

    @pl.when(pl.program_id(0) == 0)
    def _():
        copies = place(here, qkv_parts, masks, by_columns(w_qkv, w_qkv.shape[4] // 2), sems, 0)
        copies += place(here, out_parts, masks, by_columns(w_out, w_out.shape[4] // 2), sems, count)
        for copy in copies:
            copy.wait()

    rows = normed.shape[0]
    wide = w_qkv.shape[4]
    width = wide // 3
    qkv = dot(normed[...], w_qkv[...].reshape(-1, wide)) + bias[...]
    dpo = dot_nt(dy[...], w_out[...].reshape(width, -1)).astype(BF16)
    length = lengths[pl.program_id(0)]
    cosine, sine_up, sine_down = cos_ref[...], up_ref[...], down_ref[...]
    query_at = lax.broadcasted_iota(jnp.int32, (rows, rows), 0)
    key_at = lax.broadcasted_iota(jnp.int32, (rows, rows), 1)
    allowed = (key_at <= query_at) & (key_at < length)
    lane = lax.broadcasted_iota(jnp.int32, (rows, 2 * HEAD), 1)
    lower = lane < HEAD
    half = ROT // 2
    scale = HEAD ** (-0.5)

    def turn(x, sign):
        ahead = pltpu.roll(x, 2 * HEAD - half, 1)
        behind = pltpu.roll(x, half, 1)
        return x * cosine + sign * (behind * sine_down - ahead * sine_up)

    for pair in range(width // (2 * HEAD)):
        at = pair * 2 * HEAD
        cols = slice(at, at + 2 * HEAD)
        k_cols = slice(width + at, width + at + 2 * HEAD)
        v_cols = slice(2 * width + at, 2 * width + at + 2 * HEAD)
        q_rot = turn(qkv[:, cols], 1.0).astype(BF16)
        k_rot = turn(qkv[:, k_cols], 1.0).astype(BF16)
        values = qkv[:, v_cols].astype(BF16)
        grad = dpo[:, cols]
        results = []
        for side in range(2):
            mine = lower if side == 0 else ~lower
            scores = dot_nt(jnp.where(mine, q_rot, 0.0).astype(BF16), k_rot) * scale
            masked = jnp.where(allowed, scores, -1e30)
            raised = jnp.exp(masked - jnp.max(masked, axis=1, keepdims=True))
            probs = raised * (1.0 / jnp.sum(raised, axis=1, keepdims=True))
            probs_low = probs.astype(BF16)
            out = dot(probs_low, values)
            d_probs = dot_nt(jnp.where(mine, grad, 0.0).astype(BF16), values)
            d_values = dot_tn(probs_low, grad)
            inner = jnp.sum(probs * d_probs, axis=1, keepdims=True)
            d_scores = (probs * (d_probs - inner)).astype(BF16)
            d_query = dot(d_scores, k_rot) * scale
            d_keys = dot_tn(d_scores, q_rot) * scale
            results.append((out, d_query, d_keys, d_values))
        out, d_query, d_keys, d_values = (
            jnp.where(lower, first, second) for first, second in zip(*results)
        )
        o_ref[:, cols] = out.astype(BF16)
        for spot, value in (
            (cols, turn(d_query, -1.0)),
            (k_cols, turn(d_keys, -1.0)),
            (v_cols, d_values),
        ):
            low = value.astype(BF16)
            dqkv_ref[:, spot] = low
            bias_ref[0, :, spot] = jnp.sum(low.astype(F32), axis=0, keepdims=True)


def attention(here, masks, lengths, tables, normed, dy, bias, qkv_parts, out_parts, sizes):
    n_a, n_t, n_b, _ = sizes
    slots = lengths.shape[0]
    slot, width = dy.shape[0] // slots, dy.shape[1]
    wide = bias.shape[1]
    table = pl.BlockSpec((slot, 2 * HEAD), lambda i, h, lens: (0, 0))
    w_rows = qkv_parts[0].shape[1]
    return pl.pallas_call(
        functools.partial(attention_kernel, masks),
        grid_spec=pltpu.PrefetchScalarGridSpec(
            num_scalar_prefetch=2,
            grid=(n_t,),
            in_specs=[
                pl.BlockSpec((slot, width), lambda i, h, lens: (i, 0)),
                pl.BlockSpec((slot, width), lambda i, h, lens: (i, 0)),
                pl.BlockSpec((1, wide), lambda i, h, lens: (0, 0)),
                table,
                table,
                table,
            ]
            + [ANYWHERE] * (2 * len(masks)),
            out_specs=[
                pl.BlockSpec((slot, wide // 3), lambda i, h, lens: (i, 0)),
                pl.BlockSpec((slot, wide), lambda i, h, lens: (i, 0)),
                pl.BlockSpec((1, 1, wide), lambda i, h, lens: (i, 0, 0)),
            ],
            scratch_shapes=[
                pltpu.VMEM((n_a, n_t, n_b, w_rows, wide), BF16),
                pltpu.VMEM((n_a, 1, n_b, w_rows, width), BF16),
                pltpu.SemaphoreType.DMA((2 * len(masks),)),
            ],
        ),
        out_shape=[
            jax.ShapeDtypeStruct((n_t * slot, wide // 3), BF16),
            jax.ShapeDtypeStruct((n_t * slot, wide), BF16),
            jax.ShapeDtypeStruct((n_t, 1, wide), F32),
        ],
        compiler_params=params(1),
        cost_estimate=cost(
            4 * n_t * slot * width * wide, 5 * n_t * slot * width * 2, n_t * slot * slot * 8
        ),
        name="attention",
    )(here, lengths, normed, dy, bias, *tables, *qkv_parts, *out_parts)


def grads_cols_kernel(where, left, d_sent, d_kept, *outs):
    tall = left[...]
    sent = dot_tn(tall, d_sent[0]).astype(BF16)
    kept = dot_tn(tall, d_kept[0])
    far = pl.program_id(0) < pl.num_programs(0) // 2

    @pl.when(far)
    def _():
        outs[0][...] = sent
        outs[1][...] = kept

    @pl.when(jnp.logical_not(far))
    def _():
        outs[2][...] = sent
        outs[3][...] = kept


def grads_cols(where, normed, d_cols, name):
    rows, width = normed.shape
    wide = d_cols.shape[2]
    half_rows = width // 2
    steps = 4
    tile = half_rows // steps

    def tall(i, w):
        return (0, jnp.where(i < steps, w[0], 1 - w[0]) * steps + i % steps)

    def far(i, w):
        return (jnp.minimum(i, steps - 1), 0)

    def near(i, w):
        return (jnp.maximum(i - steps, 0), 0)

    return pl.pallas_call(
        grads_cols_kernel,
        grid_spec=pltpu.PrefetchScalarGridSpec(
            num_scalar_prefetch=1,
            grid=(2 * steps,),
            in_specs=[
                pl.BlockSpec((rows, tile), tall),
                pl.BlockSpec((1, rows, wide), lambda i, w: (1 - w[1], 0, 0)),
                pl.BlockSpec((1, rows, wide), lambda i, w: (w[1], 0, 0)),
            ],
            out_specs=[pl.BlockSpec((tile, wide), at) for at in (far, far, near, near)],
        ),
        out_shape=[jax.ShapeDtypeStruct((half_rows, wide), t) for t in (BF16, F32, BF16, F32)],
        compiler_params=params(1),
        name=name,
    )(where, normed, d_cols, d_cols)


def grads_rows_kernel(where, far, near, dy_sent, dy_kept, *outs):
    sent, kept = dy_sent[...], dy_kept[...]
    outs[0][...] = dot_tn(far[...], sent).astype(BF16)
    outs[1][...] = dot_tn(far[...], kept)
    outs[2][...] = dot_tn(near[...], sent).astype(BF16)
    outs[3][...] = dot_tn(near[...], kept)


def grads_rows(where, left, dy, name):
    rows, wide = left.shape
    width = dy.shape[1]
    half, dy_half = wide // 2, width // 2
    steps = 4
    tile = dy_half // steps
    block = (rows, tile)
    return pl.pallas_call(
        grads_rows_kernel,
        grid_spec=pltpu.PrefetchScalarGridSpec(
            num_scalar_prefetch=1,
            grid=(steps,),
            in_specs=[
                pl.BlockSpec((rows, half), lambda i, w: (0, w[0])),
                pl.BlockSpec((rows, half), lambda i, w: (0, 1 - w[0])),
                pl.BlockSpec(block, lambda i, w: (0, (1 - w[1]) * steps + i)),
                pl.BlockSpec(block, lambda i, w: (0, w[1] * steps + i)),
            ],
            out_specs=[pl.BlockSpec((half, tile), lambda i, w: (0, i))] * 4,
        ),
        out_shape=[jax.ShapeDtypeStruct((half, dy_half), t) for t in (BF16, F32, BF16, F32)],
        compiler_params=params(1),
        cost_estimate=cost(2 * rows * width * wide, 2 * rows * (width + wide) + 3 * wide * width),
        name=name,
    )(where, left, left, dy, dy)


def grads_attention_kernel(where, tall, d_qkv, left, dy_sent, dy_kept, sent, kept):
    step, steps = pl.program_id(0), pl.num_programs(0)
    tile, half = tall.shape[1], left.shape[1] // 2
    tiles = sent.shape[1] - 1
    part, first = step // (steps // 2), step % (steps // 2) * tile
    result = dot_tn(tall[...], d_qkv[...])
    low, high = result[:, : tiles * LANES], result[:, tiles * LANES :]
    upper = where[1] == 1
    for out, d_cols, dy in (
        (sent, jnp.where(upper, low, high), dy_sent),
        (kept, jnp.where(upper, high, low), dy_kept),
    ):
        d_cols = d_cols.astype(out.dtype)
        spot = pl.ds(pl.multiple_of(first, tile), tile)
        for n in range(tiles):
            out[part, n, spot, :] = d_cols[:, n * LANES : (n + 1) * LANES]
        columns = dot_tn(left[...], dy[...]).astype(out.dtype)
        spot = pl.ds(pl.multiple_of(step * half, half), half)
        out[where[0], tiles, spot, :] = columns[:half]
        out[1 - where[0], tiles, spot, :] = columns[half:]


def grads_attention(where, normed, d_qkv, attended, dy):
    rows, width = normed.shape
    d_half, half, dy_half = d_qkv.shape[1] // 2, attended.shape[1] // 2, width // 2
    steps = dy_half // LANES
    tile = width // steps
    block = (rows, LANES)
    shape = (2, d_half // LANES + 1, steps * half, LANES)
    assert shape[2] == width // 2

    def tall(i, w):
        return (0, jnp.where(i < steps // 2, w[0], 1 - w[0]) * (steps // 2) + i % (steps // 2))

    return pl.pallas_call(
        grads_attention_kernel,
        grid_spec=pltpu.PrefetchScalarGridSpec(
            num_scalar_prefetch=1,
            grid=(steps,),
            in_specs=[
                pl.BlockSpec((rows, tile), tall),
                pl.BlockSpec((rows, 2 * d_half), lambda i, w: (0, 0)),
                pl.BlockSpec((rows, 2 * half), lambda i, w: (0, 0)),
                pl.BlockSpec(block, lambda i, w: (0, (1 - w[1]) * steps + i)),
                pl.BlockSpec(block, lambda i, w: (0, w[1] * steps + i)),
            ],
            out_specs=[pl.BlockSpec(shape, lambda i, w: (0, 0, 0, 0))] * 2,
        ),
        out_shape=[jax.ShapeDtypeStruct(shape, t) for t in (BF16, F32)],
        compiler_params=params(1),
        name="grads_attention",
    )(where, normed, d_qkv, attended, dy, dy)


def row_blocks(kernel, name, here, kept, inputs, parts, scratch, slot, width, n_t):
    def slot_of(i, h):
        lowest = (i < n_t // 2).astype(jnp.int32) if kept is None else 1 - kept
        return i % 2 * 4 + i // 2 % 2 * 2 + lowest

    half = n_t // 2
    blocks = [lambda i, h: (i, 0)]
    if kept is None:
        blocks = [
            lambda i, h: (jnp.minimum(i, half - 1), 0),
            lambda i, h: (jnp.maximum(i - half, 0), 0),
        ]

    in_specs = []
    for value in inputs:
        block = (slot, value.shape[-1])
        if value.ndim == 3:
            block = (value.shape[0],) + block
            in_specs.append(pl.BlockSpec(block, lambda i, h: (0, slot_of(i, h), 0)))
        else:
            in_specs.append(pl.BlockSpec(block, lambda i, h: (slot_of(i, h), 0)))
    return pl.pallas_call(
        kernel,
        grid_spec=pltpu.PrefetchScalarGridSpec(
            num_scalar_prefetch=1,
            grid=(half * len(blocks),),
            in_specs=in_specs + [ANYWHERE] * len(parts),
            out_specs=[pl.BlockSpec((slot, width), block) for block in blocks],
            scratch_shapes=scratch + [pltpu.SemaphoreType.DMA((len(parts),))],
        ),
        out_shape=[jax.ShapeDtypeStruct((half * slot, width), BF16)] * len(blocks),
        compiler_params=params(1),
        name=name if kept is None else name + ("_kept" if kept else "_sent"),
    )(here, *inputs, *parts)


def branch_kernel(masks, here, o, hidden, *rest):
    count = len(masks)
    out_parts, down_parts = rest[:count], rest[count : 2 * count]
    *outs, w_out, down, sems = rest[2 * count :]

    @pl.when(pl.program_id(0) == 0)
    def _():
        copies = place(here, out_parts, masks, by_columns(w_out, w_out.shape[4] // 2), sems, 0)
        copies += place(here, down_parts, masks, by_columns(down, down.shape[4] // 2), sems, count)
        for copy in copies:
            copy.wait()

    width = w_out.shape[4]
    branch = dot(o[...], w_out[...].reshape(-1, width))
    branch += dot(hidden[...], down[...].reshape(-1, width))
    branch, step, half = branch.astype(BF16), pl.program_id(0), pl.num_programs(0) // 2

    @pl.when(step < half)
    def _():
        outs[0][...] = branch

    @pl.when(step >= half)
    def _():
        outs[1][...] = branch


def normal_kernel(masks, here, d_qkv, d_joined, *rest):
    count = len(masks)
    qkv_parts, gu_parts = rest[:count], rest[count : 3 * count]
    out, w_qkv, gu, sems = rest[3 * count :]

    @pl.when(pl.program_id(0) == 0)
    def _():
        copies = place(here, qkv_parts, masks, by_columns(w_qkv, w_qkv.shape[4] // 2), sems, 0)
        copies += place_gu(here, gu_parts, masks, gu, sems, count)
        for copy in copies:
            copy.wait()

    wide = w_qkv.shape[4]
    width = w_qkv.size // wide
    normal = dot_nt(d_qkv[...], w_qkv[...].reshape(width, -1))
    normal += dot_nt(d_joined[0], gu[0].reshape(width, -1))
    normal += dot_nt(d_joined[1], gu[1].reshape(width, -1))
    out[...] = normal.astype(BF16)


def after(value, *others):
    return lax.optimization_barrier((value,) + others)[0]


def per_device(
    sizes,
    tokens,
    cotangent,
    lengths,
    w_qkv,
    w_out,
    w_gate_up,
    w_down,
    vectors,
    first_qkv,
    first_out,
    first_gate_up,
    first_down,
    first_vectors,
    second_qkv,
    second_out,
    second_gate_up,
    second_down,
    second_vectors,
):
    barrier = lax.optimization_barrier
    n_a, n_t, n_b, n_y = sizes
    total = n_a * n_t * n_b * n_y
    at_a, at_t, at_b, at_y = (lax.axis_index(name).astype(jnp.int32) for name in AXES)
    here = jnp.stack([at_a, at_t, at_b, at_y])
    row_count, width = tokens.shape
    w_rows = w_qkv.shape[0]
    d_rows = w_down.shape[0]
    head_cols = n_b * w_rows
    unit = d_rows
    while unit % 16 or n_a * n_b * unit % 128:
        unit += 1

    def swap(value, name, step):
        mask = {"y": 1, "b": n_y, "t": n_y * n_b, "a": n_y * n_b * n_t}[name] * step
        return lax.ppermute(value, AXES, [(i, i ^ mask) for i in range(total)])

    def exchange(value):
        return lax.all_to_all(value, "t", split_axis=0, concat_axis=0, tiled=True)

    r_bits = [("a", s) for s in reversed(bits(n_a))] + [("b", s) for s in bits(n_b)]
    masks = [(0, 0, 0)]
    for name, step in r_bits:
        masks = masks + [
            (m[0] + step * (name == "a"), m[1] + step * (name == "b"), 0) for m in masks
        ]
    masks = tuple(masks + [(m[0], m[1], 1) for m in masks])

    small = 5 * vectors.shape[1] + lengths.shape[1]
    padded = -(-small // 128) * 128
    packed = jnp.concatenate(
        [
            vectors.reshape(1, 1, -1),
            lengths.astype(F32).reshape(1, 1, -1),
            jnp.zeros((1, 1, padded - small), F32),
        ],
        axis=2,
    )
    packed = jnp.broadcast_to(packed, (total, 1, padded))
    packed = lax.all_to_all(packed, AXES, split_axis=0, concat_axis=0, tiled=True)
    packed = packed.reshape(total, padded)

    def spread_top(part):
        parts = [part]
        for name, step in r_bits:
            parts = parts + [swap(p, name, step) for p in parts]
        return parts

    def over_y(value):
        return swap(value, "y", 1)

    def over_y_rest(parts):
        return [over_y(part) for part in parts[1:]]

    def over_top(value):
        return swap(value.astype(BF16), "a", top)

    def summed(kept, *got):
        return functools.reduce(lambda one, two: one.astype(F32) + two.astype(F32), got, kept)

    top = n_a // 2
    down_own = jnp.pad(w_down.astype(BF16), ((0, unit - d_rows), (0, 0)))[None]
    out_own = w_out.astype(BF16)[None]
    qkv_own, gu_own = prep(sizes, unit, w_qkv, w_gate_up, d_rows)
    x_top, x_middle, down_parts, down_other, qkv_own, gu_own, out_own, packed = barrier(
        (
            swap(tokens, "t", n_t // 2),
            swap(tokens, "t", n_t // 4),
            spread_top(down_own),
            over_y(down_own),
            qkv_own,
            gu_own,
            out_own,
            packed,
        )
    )
    all_vectors = packed[:, : 5 * vectors.shape[1]].reshape(total, 5, -1)
    all_vectors = all_vectors.transpose(1, 0, 2).reshape(5, width)
    group = packed[:, 5 * vectors.shape[1] : small].reshape(n_a, n_t, n_b, n_y, -1)
    group = lax.dynamic_index_in_dim(group, at_a, 0, keepdims=False)
    group = lax.dynamic_index_in_dim(group, at_b, 1, keepdims=False)
    group = jnp.where(at_y == 1, group[:, 0, 1], group[:, 0, 0])
    group = group.reshape(2, 2, 2)
    for dim, step in enumerate((4, 2, 1)):
        group = jnp.where(at_t // step % 2 == 1, jnp.flip(group, dim), group)
    slot_lengths = jnp.round(group.reshape(-1)).astype(jnp.int32)
    bias = all_vectors[2:5].reshape(3 * n_a, n_t, head_cols)
    bias = lax.dynamic_index_in_dim(bias, at_t, 1, keepdims=False).reshape(1, -1)
    vec = all_vectors[:2]
    tables = rotary_lanes(row_count)

    gu_own, out_parts, out_other, cotangent, vec, bias, slot_lengths, tables = barrier(
        (
            exchange(gu_own),
            spread_top(out_own),
            over_y(out_own),
            cotangent,
            vec,
            bias,
            slot_lengths,
            tables,
        )
    )
    cut = n_t * 5 // 8
    gu_first, gu_second = barrier((gu_own[:cut], gu_own[cut:]))
    gu_parts, gu_other, down_far, dy_top, dy_middle, gu_second, qkv_own, x_top = barrier(
        (
            spread_top(gu_first),
            over_y(gu_first),
            over_y_rest(down_parts),
            swap(cotangent, "t", n_t // 2),
            swap(cotangent, "t", n_t // 4),
            gu_second,
            qkv_own,
            x_top,
        )
    )
    down_parts = down_parts + [down_other] + down_far
    gu_two, gu_two_other, gu_far, x_far, dy_far, qkv_own = barrier(
        (
            spread_top(gu_second),
            over_y(gu_second),
            over_y_rest(gu_parts),
            swap(x_top, "t", n_t // 4),
            swap(dy_top, "t", n_t // 4),
            qkv_own,
        )
    )
    x_even = jnp.concatenate([tokens, x_middle, x_top, x_far], axis=0)
    dy_even = jnp.concatenate([cotangent, dy_middle, dy_top, dy_far], axis=0)
    gu_two_far, qkv_own, x_odd, dy_odd = barrier(
        (
            over_y_rest(gu_two),
            exchange(qkv_own),
            swap(x_even, "t", 1),
            swap(dy_even, "t", 1),
        )
    )
    gu_parts = gu_parts + [gu_other] + gu_far + gu_two + [gu_two_other] + gu_two_far


    top = n_a // 2
    upper = at_a // top % 2
    other_half = jnp.stack([1 - upper, at_y])
    lower_bits = r_bits[1:]

    def over_rest(value, parts_shape):
        summed = value.reshape(parts_shape + (value.shape[-1],))
        for name, step in lower_bits:
            dim = 0 if name == "a" else 2
            at = at_a if name == "a" else at_b
            size = summed.shape[dim] // 2
            low_half = lax.slice_in_dim(summed, 0, size, axis=dim)
            high_half = lax.slice_in_dim(summed, size, 2 * size, axis=dim)
            is_upper = (at // step) % 2 == 1
            keep = jnp.where(is_upper, high_half, low_half)
            send = jnp.where(is_upper, low_half, high_half)
            summed = keep + swap(send.astype(BF16), name, step).astype(F32)
        return summed.reshape(summed.shape[1], summed.shape[3], summed.shape[4])

    def piece(raw, middle_bit, top_bit, left):
        columns = slice(0, split) if left else slice(split, width)
        got, kept = (part.reshape(2, 2, row_count, width) for part in raw)
        spot = (middle_bit, top_bit, slice(None), columns)
        return got[spot].astype(F32) + kept[spot].astype(F32)

    split = width * 5 // 8
    every = slice(None)

    def first_sends(raw):
        return piece(raw, 1, every, True).astype(BF16), piece(raw, every, 1, False).astype(BF16)

    def first_swaps(sends):
        return swap(sends[0], "t", n_t // 4), swap(sends[1], "t", n_t // 2)

    def second_sends(raw, got):
        left = piece(raw, 0, 1, True) + got[0][1].astype(F32)
        right = piece(raw, 1, 0, False) + got[1][1].astype(F32)
        return left.astype(BF16), right.astype(BF16)

    def second_swaps(sends):
        return swap(sends[0], "t", n_t // 2), swap(sends[1], "t", n_t // 4)

    def whole_rows(raw, got, last):
        left = piece(raw, 0, 0, True) + got[0][0].astype(F32) + last[0].astype(F32)
        right = piece(raw, 0, 0, False) + got[1][0].astype(F32) + last[1].astype(F32)
        return jnp.concatenate([left, right], axis=1)

    half_width = width // 2
    shape_w = (top, n_t, n_b, w_rows)
    normed, dy, hidden, d_joined = mlp(
        after(here, qkv_own),
        masks,
        (x_even, x_odd, dy_even, dy_odd),
        vec,
        gu_parts,
        down_parts,
        sizes,
        unit,
    )
    qkv_parts, qkv_other, out_far, normed, dy, hidden, d_joined = barrier(
        (
            spread_top(qkv_own),
            over_y(qkv_own),
            over_y_rest(out_parts),
            normed,
            dy,
            hidden,
            d_joined,
        )
    )

    out_parts = out_parts + [out_other] + out_far
    qkv_far = over_y_rest(qkv_parts)
    down_far_sent, down_far_kept, down_sent, down_kept = grads_rows(
        other_half, hidden, dy, "grads_down"
    )
    qkv_far, down_far_sent, down_sent, down_kept = barrier(
        (qkv_far, down_far_sent, down_sent, down_kept)
    )
    down_far_got = over_y(down_far_sent)
    gu_far_sent, gu_far_kept, gu_sent, gu_kept = grads_cols(
        after(other_half, down_kept), normed, d_joined, "grads_gate_up"
    )
    down_far_got, gu_far_sent, down_sent, gu_sent, gu_kept = barrier(
        (down_far_got, gu_far_sent, down_sent, gu_sent, gu_kept)
    )
    qkv_parts = qkv_parts + [qkv_other] + qkv_far

    down_far = barrier(summed(down_far_kept, down_far_got).astype(BF16))
    attended, d_qkv, bias_sums = attention(
        after(here, down_far),
        masks,
        slot_lengths,
        tables,
        normed,
        dy,
        bias,
        qkv_parts,
        out_parts,
        sizes,
    )
    gu_rows = gu_sent.shape[0] // 2
    down_far_got, gu_far_got, down_sent, gu_sent, attended, d_qkv = barrier(
        (
            over_top(down_far),
            over_y(gu_far_sent),
            down_sent,
            (gu_sent[:gu_rows], gu_sent[gu_rows:]),
            attended,
            d_qkv,
        )
    )

    def thirds(value):
        value = value.reshape(value.shape[0] // (n_b * w_rows), n_b * w_rows, -1)
        cuts = [n * value.shape[1] // 8 for n in (0, 2, 5, 8)]
        return [value[:, low:high] for low, high in zip(cuts, cuts[1:])]

    gu_far = [summed(k, g).astype(BF16) for k, g in zip(thirds(gu_far_kept), thirds(gu_far_got))]
    gu_far = barrier(gu_far)
    branch_sent, branch_kept = row_blocks(
        functools.partial(branch_kernel, masks),
        "branch_rows",
        after(here, *gu_far),
        None,
        inputs=(attended, hidden),
        parts=out_parts + down_parts,
        scratch=[
            pltpu.VMEM((n_a, 1, n_b, w_rows, width), BF16),
            pltpu.VMEM((n_a, 1, n_b, unit, width), BF16),
        ],
        slot=row_count,
        width=width,
        n_t=n_t,
    )
    gu_far_one, gu_got, gu_far, branch_sent, branch_kept, gu_sent = barrier(
        (
            over_top(gu_far[0]),
            over_y(gu_sent[0]),
            gu_far,
            branch_sent,
            branch_kept,
            gu_sent[1],
        )
    )

    qo_sent, qo_kept = grads_attention(
        after(other_half, branch_sent), normed, d_qkv, attended, dy
    )
    gu_far_two, branch_got, gu_got_more, gu_far, qo_far_sent, qo_sent = barrier(
        (
            over_top(gu_far[1]),
            swap(branch_sent, "t", 1),
            over_y(gu_sent),
            gu_far,
            qo_sent[0],
            qo_sent[1],
        )
    )

    normal_rows = functools.partial(
        row_blocks,
        functools.partial(normal_kernel, masks),
        "normal_rows",
        inputs=(d_qkv, d_joined),
        parts=qkv_parts + gu_parts,
        scratch=[
            pltpu.VMEM((n_a, n_t, n_b, w_rows, d_qkv.shape[1]), BF16),
            pltpu.VMEM((n_y, n_a, n_t, n_b, w_rows, n_a * n_b * unit), BF16),
        ],
        slot=row_count,
        width=width,
        n_t=n_t,
    )
    branch = (branch_got, branch_kept)
    branch_sends = barrier(first_sends(branch))
    (normal_sent,) = normal_rows(after(here, qo_far_sent, *branch_sends), 0)
    gu_far_three, qo_far_got, branch_got, normal_sent, qo_sent, down_sent = barrier(
        (
            over_top(gu_far[2]),
            over_y(qo_far_sent),
            first_swaps(branch_sends),
            normal_sent,
            qo_sent,
            down_sent,
        )
    )
    qo_far = summed(qo_kept[0], qo_far_got).astype(BF16)
    gu_got = jnp.concatenate([gu_got, gu_got_more], axis=0)
    gu_far_got = jnp.concatenate([gu_far_one, gu_far_two, gu_far_three], axis=1)
    g_gu = summed(gu_kept, gu_got, gu_far_got.reshape(gu_kept.shape))
    g_gu = over_rest(g_gu, shape_w).astype(BF16)
    qo_far_one, qo_far_two, g_gu = barrier((qo_far[:1], qo_far[1:], g_gu))
    (normal_kept,) = normal_rows(after(here, normal_sent, g_gu), 1)
    qo_far_one, normal_got, qo_got, g_gu, normal_kept, qo_far_two, down_sent, branch_got = barrier(
        (
            over_top(qo_far_one),
            swap(normal_sent, "t", 1),
            over_y(qo_sent),
            exchange(g_gu),
            normal_kept,
            qo_far_two,
            down_sent,
            branch_got,
        )
    )

    qo_far_two, down_got = over_top(qo_far_two), over_y(down_sent)
    normal = (normal_got, normal_kept)
    normal_sends = barrier(first_sends(normal))
    new_gu, moment_gu, square_gu = finish(
        functools.partial(finish_gu_kernel, sizes, d_rows, unit),
        "finish_gate_up",
        after(g_gu, *normal_sends),
        w_gate_up,
        first_gate_up,
        second_gate_up,
    )
    branch_sends = second_sends(branch, [after(got, *normal_sends) for got in branch_got])
    normal_got, qo_far_two, down_got, branch_sends, new_gu = barrier(
        (first_swaps(normal_sends), qo_far_two, down_got, branch_sends, new_gu)
    )

    normal_sends = barrier(second_sends(normal, normal_got))
    qo_far_got = jnp.concatenate([qo_far_one, qo_far_two], axis=0)
    qo = after(summed(qo_kept[1], qo_got, qo_far_got), *normal_sends)
    g_qkv = over_rest(qo[:-1].transpose(1, 0, 2).reshape(qo.shape[1], -1), shape_w)
    g_out = qo[-1].reshape(half_width // LANES, -1, LANES).transpose(1, 0, 2)
    g_out = over_rest(g_out.reshape(-1, half_width), (top, 1, n_b, w_rows))
    g_qkv = g_qkv.astype(BF16).reshape(n_t, w_rows, -1, LANES).transpose(0, 2, 1, 3)
    g_qkv = barrier(g_qkv)
    g_down = summed(down_kept, down_got, down_far_got)
    g_down = over_rest(after(g_down, g_qkv), (top, 1, n_b, unit))
    new_down, moment_down, square_down = adam(w_down, g_down[0, :d_rows], first_down, second_down)
    g_qkv, normal_last, g_out, branch_sends, new_down = barrier(
        (g_qkv, second_swaps(normal_sends), g_out, branch_sends, new_down)
    )
    g_qkv = exchange(g_qkv)
    branch_last = second_swaps([after(part, g_qkv) for part in branch_sends])
    normal_own = whole_rows(normal, normal_got, normal_last)
    _, scaled_own, inv_own = normalize(tokens.astype(F32), vec[0], vec[1])
    d_scaled = normal_own * vec[0]
    input_grad = cotangent.astype(F32) + inv_own * (
        d_scaled
        - jnp.mean(d_scaled, axis=-1, keepdims=True)
        - scaled_own * jnp.mean(d_scaled * scaled_own, axis=-1, keepdims=True)
    )
    g_bias = jnp.sum(bias_sums, axis=0).reshape(3 * n_a, 1, head_cols)
    is_here = (jnp.arange(n_t) == at_t)[None, :, None]
    g_bias = jnp.where(is_here, g_bias, 0.0).reshape(3, width)
    vector_part = jnp.concatenate(
        [
            jnp.sum(normal_own * scaled_own, axis=0)[None],
            jnp.sum(normal_own, axis=0)[None],
            g_bias,
        ],
        axis=0,
    )
    vector_part = vector_part.reshape(5, total, -1).transpose(1, 0, 2).reshape(total, 1, -1)
    vector_part = jnp.pad(vector_part, ((0, 0), (0, 0), (0, -vector_part.shape[2] % 128)))
    vector_part = lax.all_to_all(vector_part, AXES, split_axis=0, concat_axis=0, tiled=True)
    vector_grad = jnp.sum(vector_part, axis=0)[0, : vectors.size].reshape(vectors.shape)
    branch_own = whole_rows(branch, branch_got, branch_last)
    output = (tokens.astype(F32) + after(branch_own, vector_part)).astype(BF16)
    new_out, moment_out, square_out = adam(w_out, g_out[0], first_out, second_out)
    new_qkv, moment_qkv, square_qkv = finish(
        functools.partial(finish_qkv_kernel, sizes, head_cols),
        "finish_qkv",
        g_qkv,
        w_qkv,
        first_qkv,
        second_qkv,
    )
    new_vec, moment_vec, square_vec = adam_update(
        vectors, vector_grad, first_vectors, second_vectors, rate_vector, 0.0
    )
    return (
        output,
        input_grad.astype(BF16),
        new_qkv,
        new_out,
        new_gu,
        new_down,
        new_vec,
        moment_qkv,
        moment_out,
        moment_gu,
        moment_down,
        moment_vec,
        square_qkv,
        square_out,
        square_gu,
        square_down,
        square_vec,
    )


def solution(mesh):
    n_dp, n_y = mesh.shape["dp"], mesh.shape["branch"]
    n_b = max(1, HEAD * n_dp // (HEADS * HEAD))
    n_t = min(SLICES, n_dp // n_b)
    sizes = (n_dp // (n_t * n_b), n_t, n_b, n_y)
    split = Mesh(mesh.devices.reshape(sizes), AXES)
    dp = ("a", "t", "b")
    rows = P(AXES, None)
    matrix = P(dp, "y")
    vector = P(None, AXES)
    weights = (matrix, matrix, matrix, matrix, vector)
    return jax.shard_map(
        functools.partial(per_device, sizes),
        mesh=split,
        in_specs=(rows, rows, P(dp, None)) + weights * 3,
        out_specs=(rows, rows) + weights * 3,
        check_vma=False,
    )
```

```python
import functools

import jax
import jax.numpy as jnp
from jax import lax
from jax.experimental import pallas as pl
from jax.experimental.pallas import tpu as pltpu
from jax.sharding import Mesh, PartitionSpec as P

HEADS = 32
HEAD = 64
ROT = 16
MB = 2
STEP = 10
SLICES = 8
LANES = 128

theta_base = 10000.0
norm_eps = 1e-05
beta_one = 0.9
beta_two = 0.95
adam_eps = 1e-08
decay_rate = 0.1
rate_matrix = 0.05
rate_vector = 1.0

AXES = ("a", "t", "b", "y")
F32 = jnp.float32
BF16 = jnp.bfloat16


def dot(left, right):
    return jnp.dot(left, right, preferred_element_type=F32)


def dot_nt(left, right):
    return lax.dot_general(left, right, (((1,), (1,)), ((), ())), preferred_element_type=F32)


def dot_tn(left, right):
    return lax.dot_general(left, right, (((0,), (0,)), ((), ())), preferred_element_type=F32)


def rotary_lanes(row_count):
    half_rot = ROT // 2
    freqs = theta_base ** (-2.0 * jnp.arange(half_rot, dtype=F32) / ROT)
    angles = jnp.arange(row_count, dtype=F32)[:, None] * freqs[None, :]
    cosine, sine = jnp.cos(angles), jnp.sin(angles)
    rest = HEAD - ROT
    one, zero, gap = (
        jnp.ones((row_count, rest), F32),
        jnp.zeros((row_count, half_rot), F32),
        jnp.zeros((row_count, rest), F32),
    )
    cos_head = jnp.concatenate([cosine, cosine, one], axis=1)
    up_head = jnp.concatenate([sine, zero, gap], axis=1)
    down_head = jnp.concatenate([zero, sine, gap], axis=1)
    return tuple(jnp.concatenate([x, x], axis=1) for x in (cos_head, up_head, down_head))


def normalize(block_rows, gain_row, shift_row):
    row_mean = jnp.mean(block_rows, axis=-1, keepdims=True)
    centered = block_rows - row_mean
    inv_std = lax.rsqrt(jnp.mean(centered * centered, axis=-1, keepdims=True) + norm_eps)
    scaled = centered * inv_std
    return (scaled * gain_row + shift_row, scaled, inv_std)


def adam_update(weight, gradient, first_moment, second_moment, step_rate, decay):
    moment_new = beta_one * first_moment + (1.0 - beta_one) * gradient
    square_new = beta_two * second_moment + (1.0 - beta_two) * gradient * gradient
    moment_hat = moment_new / (1.0 - beta_one**STEP)
    square_hat = square_new / (1.0 - beta_two**STEP)
    weight_new = weight - step_rate * (
        moment_hat / (jnp.sqrt(square_hat) + adam_eps) + decay * weight
    )
    return (weight_new, moment_new, square_new)


def bits(count):
    found = []
    step = 1
    while step < count:
        found.append(step)
        step *= 2
    return found


def params(count):
    return pltpu.CompilerParams(
        dimension_semantics=("arbitrary",) * count, vmem_limit_bytes=56 * 2**20
    )


def cost(flops, bytes_moved, transcendentals=0):
    return pl.CostEstimate(
        flops=int(flops), bytes_accessed=int(bytes_moved), transcendentals=int(transcendentals)
    )


def place(here, parts, masks, target, sems, first_sem):
    copies = []
    for n, (part, (ma, mb, my)) in enumerate(zip(parts, masks)):
        copy = pltpu.make_async_copy(
            part, target(here[0] ^ ma, here[2] ^ mb, here[3] ^ my), sems.at[first_sem + n]
        )
        copy.start()
        copies.append(copy)
    return copies


def by_rows(ref, first, count):
    return lambda a, b, y: ref.at[y, a, pl.ds(first, count), b]


def place_gu(here, parts, masks, ref, sems, first_sem):
    count = len(masks)
    copies = []
    for n in range(2):
        cut = parts[n * count].shape[0]
        target = by_rows(ref, n * (ref.shape[2] - cut), cut)
        copies += place(
            here, parts[n * count : (n + 1) * count], masks, target, sems, first_sem + n * count
        )
    return copies


def by_columns(ref, width):
    return lambda a, b, y: ref.at[a, :, b, :, pl.ds(pl.multiple_of(y * width, 128), width)]


def prep_kernel(sizes, n_blocks, head_cols, d_rows, unit, qkv, gu, qkv_out, gu_out):
    n_a, n_t, n_b, _ = sizes
    ff_cols = n_b * d_rows
    for t in range(n_t):
        for block in range(n_blocks):
            at = (block * n_t + t) * head_cols
            qkv_out[t, :, block * head_cols : (block + 1) * head_cols] = qkv[
                :, at : at + head_cols
            ].astype(BF16)
        pieces = []
        gap = jnp.zeros((gu.shape[0], unit - d_rows), F32)
        for a in range(n_a):
            for b in range(n_b):
                at = (a * n_t + t) * ff_cols + b * d_rows
                pieces += [gu[:, at : at + d_rows], gap]
        gu_out[t] = jnp.concatenate(pieces, axis=1).astype(BF16)


def prep(sizes, unit, w_qkv, w_gu, d_rows):
    n_a, n_t, n_b, _ = sizes
    rows = w_qkv.shape[0]
    head_cols = n_b * rows
    n_blocks = w_qkv.shape[1] // (n_t * head_cols)
    tile = 16
    wide_q, wide_g = n_blocks * head_cols, n_a * n_b * unit
    return pl.pallas_call(
        functools.partial(prep_kernel, sizes, n_blocks, head_cols, d_rows, unit),
        grid=(rows // tile,),
        in_specs=[
            pl.BlockSpec((tile, w_qkv.shape[1]), lambda i: (i, 0)),
            pl.BlockSpec((tile, w_gu.shape[1]), lambda i: (i, 0)),
        ],
        out_specs=[
            pl.BlockSpec((n_t, tile, wide_q), lambda i: (0, i, 0)),
            pl.BlockSpec((n_t, tile, wide_g), lambda i: (0, i, 0)),
        ],
        out_shape=[
            jax.ShapeDtypeStruct((n_t, rows, wide_q), BF16),
            jax.ShapeDtypeStruct((n_t, rows, wide_g), BF16),
        ],
        compiler_params=params(1),
        cost_estimate=cost(0, 20 * w_gu.size),
        name="prep",
    )(w_qkv, w_gu)


def adam(weight, gradient, first_moment, second_moment):
    return adam_update(weight, gradient, first_moment, second_moment, rate_matrix, decay_rate)


def finish_gu_kernel(sizes, d_rows, unit, g, w, m, v, w_out, m_out, v_out):
    n_a, n_t, n_b, _ = sizes
    pieces = []
    for a in range(n_a):
        for t in range(n_t):
            for b in range(n_b):
                at = (a * n_b + b) * unit
                pieces.append(g[t, :, at : at + d_rows].astype(F32))
    grad = jnp.concatenate(pieces, axis=1)
    w_out[...], m_out[...], v_out[...] = adam(w[...], grad, m[...], v[...])


def finish_qkv_kernel(sizes, head_cols, g, w, m, v, w_out, m_out, v_out):
    n_t = sizes[1]
    for block in range(w.shape[1] // (n_t * head_cols)):
        for t in range(n_t):
            at = (block * n_t + t) * head_cols
            cols = slice(at, at + head_cols)
            tile, lane = block * head_cols // LANES, block * head_cols % LANES
            grad = g[t, tile, :, lane : lane + head_cols].astype(F32)
            w_out[:, cols], m_out[:, cols], v_out[:, cols] = adam(
                w[:, cols], grad, m[:, cols], v[:, cols]
            )


def finish(kernel, name, gradient, weight, first, second):
    tile = 16
    rows, cols = weight.shape
    matrix = pl.BlockSpec((tile, cols), lambda i: (i, 0))
    lead, lanes = gradient.shape[:-2], gradient.shape[-1]
    gradient_block = pl.BlockSpec(
        lead + (tile, lanes), lambda i: (0,) * len(lead) + (i, 0)
    )
    return pl.pallas_call(
        kernel,
        grid=(rows // tile,),
        in_specs=[
            gradient_block,
            matrix,
            matrix,
            matrix,
        ],
        out_specs=[matrix] * 3,
        out_shape=[jax.ShapeDtypeStruct(weight.shape, F32)] * 3,
        compiler_params=params(1),
        cost_estimate=cost(20 * weight.size, 26 * weight.size),
        name=name,
    )(gradient, weight, first, second)


ANYWHERE = pl.BlockSpec(memory_space=pl.ANY)


def mlp_kernel(masks, steps, here, vec, x_even, x_odd, dy_even, dy_odd, *rest):
    count = len(masks)
    gu_parts, down_parts = rest[: 2 * count], rest[2 * count : 3 * count]
    normed, grads_out, hidden, d_joined, gu, down, rows, lows, sems, row_sems = rest[-10:]
    step = pl.program_id(0)
    slot = normed.shape[0]

    def fetch(n):
        spot = pl.ds(n // 2 * slot, slot)
        sources = (x_odd, dy_odd) if n % 2 else (x_even, dy_even)
        return [
            pltpu.make_async_copy(
                source.at[spot], rows.at[n % 3, pl.ds(m * slot, slot)], row_sems.at[n % 3, m]
            )
            for m, source in enumerate(sources)
        ]

    def prepared(n):
        return normalize(rows[n, :slot].astype(F32), vec[0:1], vec[1:2])[0].astype(BF16)

    @pl.when(step == 0)
    def _():
        for copy in fetch(0) + fetch(1):
            copy.start()
        copies = place_gu(here, gu_parts, masks, gu, sems, 0)
        target = by_columns(down, down.shape[4] // 2)
        copies += place(here, down_parts, masks, target, sems, 2 * count)
        for copy in copies + fetch(0):
            copy.wait()
        lows[0] = prepared(0)

    for n in range(steps):

        @pl.when(step == n)
        def _(n=n):
            if n + 2 < steps:
                for copy in fetch(n + 2):
                    copy.start()
            if n + 1 < steps:
                for copy in fetch(n + 1):
                    copy.wait()

    low = lows[step % 2]
    dy = rows[step % 3, slot:]
    lows[(step + 1) % 2] = prepared((step + 1) % 3)
    normed[...] = low
    grads_out[...] = dy
    wide = gu.shape[5]
    gate = dot(low, gu[0].reshape(-1, wide))
    up = dot(low, gu[1].reshape(-1, wide))
    d_hidden = dot_nt(dy, down[...].reshape(wide, -1))
    sig = jax.nn.sigmoid(gate)
    act = gate * sig
    hidden[...] = (act * up).astype(BF16)
    d_joined[0] = (d_hidden * up * sig * (1.0 + gate * (1.0 - sig))).astype(BF16)
    d_joined[1] = (d_hidden * act).astype(BF16)


def mlp(here, masks, held, vec, gu_parts, down_parts, sizes, unit):
    n_a, n_t, n_b, n_y = sizes
    width = held[0].shape[1]
    slot = held[0].shape[0] * 2 // n_t
    wide = n_a * n_b * unit
    rows = n_t * slot
    w_rows = gu_parts[0].shape[1]
    return pl.pallas_call(
        functools.partial(mlp_kernel, masks, n_t),
        grid_spec=pltpu.PrefetchScalarGridSpec(
            num_scalar_prefetch=1,
            grid=(n_t,),
            in_specs=[pl.BlockSpec(vec.shape, lambda i, h: (0, 0))]
            + [ANYWHERE] * (3 * len(masks) + 4),
            out_specs=[
                pl.BlockSpec((slot, width), lambda i, h: (i, 0)),
                pl.BlockSpec((slot, width), lambda i, h: (i, 0)),
                pl.BlockSpec((slot, wide), lambda i, h: (i, 0)),
                pl.BlockSpec((2, slot, wide), lambda i, h: (0, i, 0)),
            ],
            scratch_shapes=[
                pltpu.VMEM((n_y, n_a, n_t, n_b, w_rows, wide), BF16),
                pltpu.VMEM((n_a, 1, n_b, unit, width), BF16),
                pltpu.VMEM((3, 2 * slot, width), BF16),
                pltpu.VMEM((2, slot, width), BF16),
                pltpu.SemaphoreType.DMA((3 * len(masks),)),
                pltpu.SemaphoreType.DMA((3, 2)),
            ],
        ),
        out_shape=[
            jax.ShapeDtypeStruct((rows, width), BF16),
            jax.ShapeDtypeStruct((rows, width), BF16),
            jax.ShapeDtypeStruct((rows, wide), BF16),
            jax.ShapeDtypeStruct((2, rows, wide), BF16),
        ],
        compiler_params=params(1),
        name="mlp",
    )(here, vec, *held, *gu_parts, *down_parts)


def attention_kernel(
    masks, here, lengths, normed, dy, bias, cos_ref, up_ref, down_ref, *rest
):
    count = len(masks)
    qkv_parts, out_parts = rest[:count], rest[count : 2 * count]
    o_ref, dqkv_ref, bias_ref, w_qkv, w_out, sems = rest[2 * count :]

    @pl.when(pl.program_id(0) == 0)
    def _():
        copies = place(here, qkv_parts, masks, by_columns(w_qkv, w_qkv.shape[4] // 2), sems, 0)
        copies += place(here, out_parts, masks, by_columns(w_out, w_out.shape[4] // 2), sems, count)
        for copy in copies:
            copy.wait()

    rows = normed.shape[0]
    wide = w_qkv.shape[4]
    width = wide // 3
    qkv = dot(normed[...], w_qkv[...].reshape(-1, wide)) + bias[...]
    dpo = dot_nt(dy[...], w_out[...].reshape(width, -1)).astype(BF16)
    length = lengths[pl.program_id(0)]
    cosine, sine_up, sine_down = cos_ref[...], up_ref[...], down_ref[...]
    query_at = lax.broadcasted_iota(jnp.int32, (rows, rows), 0)
    key_at = lax.broadcasted_iota(jnp.int32, (rows, rows), 1)
    allowed = (key_at <= query_at) & (key_at < length)
    lane = lax.broadcasted_iota(jnp.int32, (rows, 2 * HEAD), 1)
    lower = lane < HEAD
    half = ROT // 2
    scale = HEAD ** (-0.5)

    def turn(x, sign):
        ahead = pltpu.roll(x, 2 * HEAD - half, 1)
        behind = pltpu.roll(x, half, 1)
        return x * cosine + sign * (behind * sine_down - ahead * sine_up)

    for pair in range(width // (2 * HEAD)):
        at = pair * 2 * HEAD
        cols = slice(at, at + 2 * HEAD)
        k_cols = slice(width + at, width + at + 2 * HEAD)
        v_cols = slice(2 * width + at, 2 * width + at + 2 * HEAD)
        q_rot = turn(qkv[:, cols], 1.0).astype(BF16)
        k_rot = turn(qkv[:, k_cols], 1.0).astype(BF16)
        values = qkv[:, v_cols].astype(BF16)
        grad = dpo[:, cols]
        results = []
        for side in range(2):
            mine = lower if side == 0 else ~lower
            scores = dot_nt(jnp.where(mine, q_rot, 0.0).astype(BF16), k_rot) * scale
            masked = jnp.where(allowed, scores, -1e30)
            raised = jnp.exp(masked - jnp.max(masked, axis=1, keepdims=True))
            probs = raised * (1.0 / jnp.sum(raised, axis=1, keepdims=True))
            probs_low = probs.astype(BF16)
            out = dot(probs_low, values)
            d_probs = dot_nt(jnp.where(mine, grad, 0.0).astype(BF16), values)
            d_values = dot_tn(probs_low, grad)
            inner = jnp.sum(probs * d_probs, axis=1, keepdims=True)
            d_scores = (probs * (d_probs - inner)).astype(BF16)
            d_query = dot(d_scores, k_rot) * scale
            d_keys = dot_tn(d_scores, q_rot) * scale
            results.append((out, d_query, d_keys, d_values))
        out, d_query, d_keys, d_values = (
            jnp.where(lower, first, second) for first, second in zip(*results)
        )
        o_ref[:, cols] = out.astype(BF16)
        for spot, value in (
            (cols, turn(d_query, -1.0)),
            (k_cols, turn(d_keys, -1.0)),
            (v_cols, d_values),
        ):
            low = value.astype(BF16)
            dqkv_ref[:, spot] = low
            bias_ref[0, :, spot] = jnp.sum(low.astype(F32), axis=0, keepdims=True)


def attention(here, masks, lengths, tables, normed, dy, bias, qkv_parts, out_parts, sizes):
    n_a, n_t, n_b, _ = sizes
    slots = lengths.shape[0]
    slot, width = dy.shape[0] // slots, dy.shape[1]
    wide = bias.shape[1]
    table = pl.BlockSpec((slot, 2 * HEAD), lambda i, h, lens: (0, 0))
    w_rows = qkv_parts[0].shape[1]
    return pl.pallas_call(
        functools.partial(attention_kernel, masks),
        grid_spec=pltpu.PrefetchScalarGridSpec(
            num_scalar_prefetch=2,
            grid=(n_t,),
            in_specs=[
                pl.BlockSpec((slot, width), lambda i, h, lens: (i, 0)),
                pl.BlockSpec((slot, width), lambda i, h, lens: (i, 0)),
                pl.BlockSpec((1, wide), lambda i, h, lens: (0, 0)),
                table,
                table,
                table,
            ]
            + [ANYWHERE] * (2 * len(masks)),
            out_specs=[
                pl.BlockSpec((slot, wide // 3), lambda i, h, lens: (i, 0)),
                pl.BlockSpec((slot, wide), lambda i, h, lens: (i, 0)),
                pl.BlockSpec((1, 1, wide), lambda i, h, lens: (i, 0, 0)),
            ],
            scratch_shapes=[
                pltpu.VMEM((n_a, n_t, n_b, w_rows, wide), BF16),
                pltpu.VMEM((n_a, 1, n_b, w_rows, width), BF16),
                pltpu.SemaphoreType.DMA((2 * len(masks),)),
            ],
        ),
        out_shape=[
            jax.ShapeDtypeStruct((n_t * slot, wide // 3), BF16),
            jax.ShapeDtypeStruct((n_t * slot, wide), BF16),
            jax.ShapeDtypeStruct((n_t, 1, wide), F32),
        ],
        compiler_params=params(1),
        cost_estimate=cost(
            4 * n_t * slot * width * wide, 5 * n_t * slot * width * 2, n_t * slot * slot * 8
        ),
        name="attention",
    )(here, lengths, normed, dy, bias, *tables, *qkv_parts, *out_parts)


def grads_cols_kernel(where, left, d_sent, d_kept, *outs):
    tall = left[...]
    sent = dot_tn(tall, d_sent[0]).astype(BF16)
    kept = dot_tn(tall, d_kept[0])
    far = pl.program_id(0) < pl.num_programs(0) // 2

    @pl.when(far)
    def _():
        outs[0][...] = sent
        outs[1][...] = kept

    @pl.when(jnp.logical_not(far))
    def _():
        outs[2][...] = sent
        outs[3][...] = kept


def grads_cols(where, normed, d_cols, name):
    rows, width = normed.shape
    wide = d_cols.shape[2]
    half_rows = width // 2
    steps = 4
    tile = half_rows // steps

    def tall(i, w):
        return (0, jnp.where(i < steps, w[0], 1 - w[0]) * steps + i % steps)

    def far(i, w):
        return (jnp.minimum(i, steps - 1), 0)

    def near(i, w):
        return (jnp.maximum(i - steps, 0), 0)

    return pl.pallas_call(
        grads_cols_kernel,
        grid_spec=pltpu.PrefetchScalarGridSpec(
            num_scalar_prefetch=1,
            grid=(2 * steps,),
            in_specs=[
                pl.BlockSpec((rows, tile), tall),
                pl.BlockSpec((1, rows, wide), lambda i, w: (1 - w[1], 0, 0)),
                pl.BlockSpec((1, rows, wide), lambda i, w: (w[1], 0, 0)),
            ],
            out_specs=[pl.BlockSpec((tile, wide), at) for at in (far, far, near, near)],
        ),
        out_shape=[jax.ShapeDtypeStruct((half_rows, wide), t) for t in (BF16, F32, BF16, F32)],
        compiler_params=params(1),
        name=name,
    )(where, normed, d_cols, d_cols)


def grads_rows_kernel(where, far, near, dy_sent, dy_kept, *outs):
    sent, kept = dy_sent[...], dy_kept[...]
    outs[0][...] = dot_tn(far[...], sent).astype(BF16)
    outs[1][...] = dot_tn(far[...], kept)
    outs[2][...] = dot_tn(near[...], sent).astype(BF16)
    outs[3][...] = dot_tn(near[...], kept)


def grads_rows(where, left, dy, name):
    rows, wide = left.shape
    width = dy.shape[1]
    half, dy_half = wide // 2, width // 2
    steps = 4
    tile = dy_half // steps
    block = (rows, tile)
    return pl.pallas_call(
        grads_rows_kernel,
        grid_spec=pltpu.PrefetchScalarGridSpec(
            num_scalar_prefetch=1,
            grid=(steps,),
            in_specs=[
                pl.BlockSpec((rows, half), lambda i, w: (0, w[0])),
                pl.BlockSpec((rows, half), lambda i, w: (0, 1 - w[0])),
                pl.BlockSpec(block, lambda i, w: (0, (1 - w[1]) * steps + i)),
                pl.BlockSpec(block, lambda i, w: (0, w[1] * steps + i)),
            ],
            out_specs=[pl.BlockSpec((half, tile), lambda i, w: (0, i))] * 4,
        ),
        out_shape=[jax.ShapeDtypeStruct((half, dy_half), t) for t in (BF16, F32, BF16, F32)],
        compiler_params=params(1),
        cost_estimate=cost(2 * rows * width * wide, 2 * rows * (width + wide) + 3 * wide * width),
        name=name,
    )(where, left, left, dy, dy)


def grads_attention_kernel(where, tall, d_qkv, left, dy_sent, dy_kept, sent, kept):
    step, steps = pl.program_id(0), pl.num_programs(0)
    tile, half = tall.shape[1], left.shape[1] // 2
    tiles = sent.shape[1] - 1
    part, first = step // (steps // 2), step % (steps // 2) * tile
    result = dot_tn(tall[...], d_qkv[...])
    low, high = result[:, : tiles * LANES], result[:, tiles * LANES :]
    upper = where[1] == 1
    for out, d_cols, dy in (
        (sent, jnp.where(upper, low, high), dy_sent),
        (kept, jnp.where(upper, high, low), dy_kept),
    ):
        d_cols = d_cols.astype(out.dtype)
        spot = pl.ds(pl.multiple_of(first, tile), tile)
        for n in range(tiles):
            out[part, n, spot, :] = d_cols[:, n * LANES : (n + 1) * LANES]
        columns = dot_tn(left[...], dy[...]).astype(out.dtype)
        spot = pl.ds(pl.multiple_of(step * half, half), half)
        out[where[0], tiles, spot, :] = columns[:half]
        out[1 - where[0], tiles, spot, :] = columns[half:]


def grads_attention(where, normed, d_qkv, attended, dy):
    rows, width = normed.shape
    d_half, half, dy_half = d_qkv.shape[1] // 2, attended.shape[1] // 2, width // 2
    steps = dy_half // LANES
    tile = width // steps
    block = (rows, LANES)
    shape = (2, d_half // LANES + 1, steps * half, LANES)
    assert shape[2] == width // 2

    def tall(i, w):
        return (0, jnp.where(i < steps // 2, w[0], 1 - w[0]) * (steps // 2) + i % (steps // 2))

    return pl.pallas_call(
        grads_attention_kernel,
        grid_spec=pltpu.PrefetchScalarGridSpec(
            num_scalar_prefetch=1,
            grid=(steps,),
            in_specs=[
                pl.BlockSpec((rows, tile), tall),
                pl.BlockSpec((rows, 2 * d_half), lambda i, w: (0, 0)),
                pl.BlockSpec((rows, 2 * half), lambda i, w: (0, 0)),
                pl.BlockSpec(block, lambda i, w: (0, (1 - w[1]) * steps + i)),
                pl.BlockSpec(block, lambda i, w: (0, w[1] * steps + i)),
            ],
            out_specs=[pl.BlockSpec(shape, lambda i, w: (0, 0, 0, 0))] * 2,
        ),
        out_shape=[jax.ShapeDtypeStruct(shape, t) for t in (BF16, F32)],
        compiler_params=params(1),
        name="grads_attention",
    )(where, normed, d_qkv, attended, dy, dy)


def row_blocks(kernel, name, here, kept, inputs, parts, scratch, slot, width, n_t):
    def slot_of(i, h):
        lowest = (i < n_t // 2).astype(jnp.int32) if kept is None else 1 - kept
        return i % 2 * 4 + i // 2 % 2 * 2 + lowest

    half = n_t // 2
    blocks = [lambda i, h: (i, 0)]
    if kept is None:
        blocks = [
            lambda i, h: (jnp.minimum(i, half - 1), 0),
            lambda i, h: (jnp.maximum(i - half, 0), 0),
        ]

    in_specs = []
    for value in inputs:
        block = (slot, value.shape[-1])
        if value.ndim == 3:
            block = (value.shape[0],) + block
            in_specs.append(pl.BlockSpec(block, lambda i, h: (0, slot_of(i, h), 0)))
        else:
            in_specs.append(pl.BlockSpec(block, lambda i, h: (slot_of(i, h), 0)))
    return pl.pallas_call(
        kernel,
        grid_spec=pltpu.PrefetchScalarGridSpec(
            num_scalar_prefetch=1,
            grid=(half * len(blocks),),
            in_specs=in_specs + [ANYWHERE] * len(parts),
            out_specs=[pl.BlockSpec((slot, width), block) for block in blocks],
            scratch_shapes=scratch + [pltpu.SemaphoreType.DMA((len(parts),))],
        ),
        out_shape=[jax.ShapeDtypeStruct((half * slot, width), BF16)] * len(blocks),
        compiler_params=params(1),
        name=name if kept is None else name + ("_kept" if kept else "_sent"),
    )(here, *inputs, *parts)


def branch_kernel(masks, here, o, hidden, *rest):
    count = len(masks)
    out_parts, down_parts = rest[:count], rest[count : 2 * count]
    *outs, w_out, down, sems = rest[2 * count :]

    @pl.when(pl.program_id(0) == 0)
    def _():
        copies = place(here, out_parts, masks, by_columns(w_out, w_out.shape[4] // 2), sems, 0)
        copies += place(here, down_parts, masks, by_columns(down, down.shape[4] // 2), sems, count)
        for copy in copies:
            copy.wait()

    width = w_out.shape[4]
    branch = dot(o[...], w_out[...].reshape(-1, width))
    branch += dot(hidden[...], down[...].reshape(-1, width))
    branch, step, half = branch.astype(BF16), pl.program_id(0), pl.num_programs(0) // 2

    @pl.when(step < half)
    def _():
        outs[0][...] = branch

    @pl.when(step >= half)
    def _():
        outs[1][...] = branch


def normal_kernel(masks, here, d_qkv, d_joined, *rest):
    count = len(masks)
    qkv_parts, gu_parts = rest[:count], rest[count : 3 * count]
    out, w_qkv, gu, sems = rest[3 * count :]

    @pl.when(pl.program_id(0) == 0)
    def _():
        copies = place(here, qkv_parts, masks, by_columns(w_qkv, w_qkv.shape[4] // 2), sems, 0)
        copies += place_gu(here, gu_parts, masks, gu, sems, count)
        for copy in copies:
            copy.wait()

    wide = w_qkv.shape[4]
    width = w_qkv.size // wide
    normal = dot_nt(d_qkv[...], w_qkv[...].reshape(width, -1))
    normal += dot_nt(d_joined[0], gu[0].reshape(width, -1))
    normal += dot_nt(d_joined[1], gu[1].reshape(width, -1))
    out[...] = normal.astype(BF16)


def after(value, *others):
    return lax.optimization_barrier((value,) + others)[0]


def per_device(
    sizes,
    tokens,
    cotangent,
    lengths,
    w_qkv,
    w_out,
    w_gate_up,
    w_down,
    vectors,
    first_qkv,
    first_out,
    first_gate_up,
    first_down,
    first_vectors,
    second_qkv,
    second_out,
    second_gate_up,
    second_down,
    second_vectors,
):
    barrier = lax.optimization_barrier
    n_a, n_t, n_b, n_y = sizes
    total = n_a * n_t * n_b * n_y
    at_a, at_t, at_b, at_y = (lax.axis_index(name).astype(jnp.int32) for name in AXES)
    here = jnp.stack([at_a, at_t, at_b, at_y])
    row_count, width = tokens.shape
    w_rows = w_qkv.shape[0]
    d_rows = w_down.shape[0]
    head_cols = n_b * w_rows
    unit = d_rows
    while unit % 16 or n_a * n_b * unit % 128:
        unit += 1

    def swap(value, name, step):
        mask = {"y": 1, "b": n_y, "t": n_y * n_b, "a": n_y * n_b * n_t}[name] * step
        return lax.ppermute(value, AXES, [(i, i ^ mask) for i in range(total)])

    def exchange(value):
        return lax.all_to_all(value, "t", split_axis=0, concat_axis=0, tiled=True)

    r_bits = [("a", s) for s in reversed(bits(n_a))] + [("b", s) for s in bits(n_b)]
    masks = [(0, 0, 0)]
    for name, step in r_bits:
        masks = masks + [
            (m[0] + step * (name == "a"), m[1] + step * (name == "b"), 0) for m in masks
        ]
    masks = tuple(masks + [(m[0], m[1], 1) for m in masks])

    small = 5 * vectors.shape[1] + lengths.shape[1]
    padded = -(-small // 128) * 128
    packed = jnp.concatenate(
        [
            vectors.reshape(1, 1, -1),
            lengths.astype(F32).reshape(1, 1, -1),
            jnp.zeros((1, 1, padded - small), F32),
        ],
        axis=2,
    )
    packed = jnp.broadcast_to(packed, (total, 1, padded))
    packed = lax.all_to_all(packed, AXES, split_axis=0, concat_axis=0, tiled=True)
    packed = packed.reshape(total, padded)

    def spread_top(part):
        parts = [part]
        for name, step in r_bits:
            parts = parts + [swap(p, name, step) for p in parts]
        return parts

    def over_y(value):
        return swap(value, "y", 1)

    def over_y_rest(parts):
        return [over_y(part) for part in parts[1:]]

    def over_top(value):
        return swap(value.astype(BF16), "a", top)

    def summed(kept, *got):
        return functools.reduce(lambda one, two: one.astype(F32) + two.astype(F32), got, kept)

    top = n_a // 2
    down_own = jnp.pad(w_down.astype(BF16), ((0, unit - d_rows), (0, 0)))[None]
    out_own = w_out.astype(BF16)[None]
    qkv_own, gu_own = prep(sizes, unit, w_qkv, w_gate_up, d_rows)
    x_top, x_middle, down_parts, down_other, qkv_own, gu_own, out_own, packed = barrier(
        (
            swap(tokens, "t", n_t // 2),
            swap(tokens, "t", n_t // 4),
            spread_top(down_own),
            over_y(down_own),
            qkv_own,
            gu_own,
            out_own,
            packed,
        )
    )
    all_vectors = packed[:, : 5 * vectors.shape[1]].reshape(total, 5, -1)
    all_vectors = all_vectors.transpose(1, 0, 2).reshape(5, width)
    group = packed[:, 5 * vectors.shape[1] : small].reshape(n_a, n_t, n_b, n_y, -1)
    group = lax.dynamic_index_in_dim(group, at_a, 0, keepdims=False)
    group = lax.dynamic_index_in_dim(group, at_b, 1, keepdims=False)
    group = jnp.where(at_y == 1, group[:, 0, 1], group[:, 0, 0])
    group = group.reshape(2, 2, 2)
    for dim, step in enumerate((4, 2, 1)):
        group = jnp.where(at_t // step % 2 == 1, jnp.flip(group, dim), group)
    slot_lengths = jnp.round(group.reshape(-1)).astype(jnp.int32)
    bias = all_vectors[2:5].reshape(3 * n_a, n_t, head_cols)
    bias = lax.dynamic_index_in_dim(bias, at_t, 1, keepdims=False).reshape(1, -1)
    vec = all_vectors[:2]
    tables = rotary_lanes(row_count)

    gu_own, out_parts, out_other, cotangent, vec, bias, slot_lengths, tables = barrier(
        (
            exchange(gu_own),
            spread_top(out_own),
            over_y(out_own),
            cotangent,
            vec,
            bias,
            slot_lengths,
            tables,
        )
    )
    cut = n_t * 5 // 8
    gu_first, gu_second = barrier((gu_own[:cut], gu_own[cut:]))
    gu_parts, gu_other, down_far, dy_top, dy_middle, gu_second, qkv_own, x_top = barrier(
        (
            spread_top(gu_first),
            over_y(gu_first),
            over_y_rest(down_parts),
            swap(cotangent, "t", n_t // 2),
            swap(cotangent, "t", n_t // 4),
            gu_second,
            qkv_own,
            x_top,
        )
    )
    down_parts = down_parts + [down_other] + down_far
    gu_two, gu_two_other, gu_far, x_far, dy_far, qkv_own = barrier(
        (
            spread_top(gu_second),
            over_y(gu_second),
            over_y_rest(gu_parts),
            swap(x_top, "t", n_t // 4),
            swap(dy_top, "t", n_t // 4),
            qkv_own,
        )
    )
    x_even = jnp.concatenate([tokens, x_middle, x_top, x_far], axis=0)
    dy_even = jnp.concatenate([cotangent, dy_middle, dy_top, dy_far], axis=0)
    gu_two_far, qkv_own, x_odd, dy_odd = barrier(
        (
            over_y_rest(gu_two),
            exchange(qkv_own),
            swap(x_even, "t", 1),
            swap(dy_even, "t", 1),
        )
    )
    gu_parts = gu_parts + [gu_other] + gu_far + gu_two + [gu_two_other] + gu_two_far


    top = n_a // 2
    upper = at_a // top % 2
    other_half = jnp.stack([1 - upper, at_y])
    lower_bits = r_bits[1:]

    def over_rest(value, parts_shape):
        summed = value.reshape(parts_shape + (value.shape[-1],))
        for name, step in lower_bits:
            dim = 0 if name == "a" else 2
            at = at_a if name == "a" else at_b
            size = summed.shape[dim] // 2
            low_half = lax.slice_in_dim(summed, 0, size, axis=dim)
            high_half = lax.slice_in_dim(summed, size, 2 * size, axis=dim)
            is_upper = (at // step) % 2 == 1
            keep = jnp.where(is_upper, high_half, low_half)
            send = jnp.where(is_upper, low_half, high_half)
            summed = keep + swap(send.astype(BF16), name, step).astype(F32)
        return summed.reshape(summed.shape[1], summed.shape[3], summed.shape[4])

    def piece(raw, middle_bit, top_bit, left):
        columns = slice(0, split) if left else slice(split, width)
        got, kept = (part.reshape(2, 2, row_count, width) for part in raw)
        spot = (middle_bit, top_bit, slice(None), columns)
        return got[spot].astype(F32) + kept[spot].astype(F32)

    split = width * 5 // 8
    every = slice(None)

    def first_sends(raw):
        return piece(raw, 1, every, True).astype(BF16), piece(raw, every, 1, False).astype(BF16)

    def first_swaps(sends):
        return swap(sends[0], "t", n_t // 4), swap(sends[1], "t", n_t // 2)

    def second_sends(raw, got):
        left = piece(raw, 0, 1, True) + got[0][1].astype(F32)
        right = piece(raw, 1, 0, False) + got[1][1].astype(F32)
        return left.astype(BF16), right.astype(BF16)

    def second_swaps(sends):
        return swap(sends[0], "t", n_t // 2), swap(sends[1], "t", n_t // 4)

    def whole_rows(raw, got, last):
        left = piece(raw, 0, 0, True) + got[0][0].astype(F32) + last[0].astype(F32)
        right = piece(raw, 0, 0, False) + got[1][0].astype(F32) + last[1].astype(F32)
        return jnp.concatenate([left, right], axis=1)

    half_width = width // 2
    shape_w = (top, n_t, n_b, w_rows)
    normed, dy, hidden, d_joined = mlp(
        after(here, qkv_own),
        masks,
        (x_even, x_odd, dy_even, dy_odd),
        vec,
        gu_parts,
        down_parts,
        sizes,
        unit,
    )
    qkv_parts, qkv_other, out_far, normed, dy, hidden, d_joined = barrier(
        (
            spread_top(qkv_own),
            over_y(qkv_own),
            over_y_rest(out_parts),
            normed,
            dy,
            hidden,
            d_joined,
        )
    )

    out_parts = out_parts + [out_other] + out_far
    qkv_far = over_y_rest(qkv_parts)
    down_far_sent, down_far_kept, down_sent, down_kept = grads_rows(
        other_half, hidden, dy, "grads_down"
    )
    qkv_far, down_far_sent, down_sent, down_kept = barrier(
        (qkv_far, down_far_sent, down_sent, down_kept)
    )
    down_far_got = over_y(down_far_sent)
    gu_far_sent, gu_far_kept, gu_sent, gu_kept = grads_cols(
        after(other_half, down_kept), normed, d_joined, "grads_gate_up"
    )
    down_far_got, gu_far_sent, down_sent, gu_sent, gu_kept = barrier(
        (down_far_got, gu_far_sent, down_sent, gu_sent, gu_kept)
    )
    qkv_parts = qkv_parts + [qkv_other] + qkv_far

    down_far = barrier(summed(down_far_kept, down_far_got).astype(BF16))
    attended, d_qkv, bias_sums = attention(
        after(here, down_far),
        masks,
        slot_lengths,
        tables,
        normed,
        dy,
        bias,
        qkv_parts,
        out_parts,
        sizes,
    )
    gu_rows = gu_sent.shape[0] // 2
    down_far_got, gu_far_got, down_sent, gu_sent, attended, d_qkv = barrier(
        (
            over_top(down_far),
            over_y(gu_far_sent),
            down_sent,
            (gu_sent[:gu_rows], gu_sent[gu_rows:]),
            attended,
            d_qkv,
        )
    )

    def thirds(value):
        value = value.reshape(value.shape[0] // (n_b * w_rows), n_b * w_rows, -1)
        cuts = [n * value.shape[1] // 8 for n in (0, 2, 5, 8)]
        return [value[:, low:high] for low, high in zip(cuts, cuts[1:])]

    gu_far = [summed(k, g).astype(BF16) for k, g in zip(thirds(gu_far_kept), thirds(gu_far_got))]
    gu_far = barrier(gu_far)
    branch_sent, branch_kept = row_blocks(
        functools.partial(branch_kernel, masks),
        "branch_rows",
        after(here, *gu_far),
        None,
        inputs=(attended, hidden),
        parts=out_parts + down_parts,
        scratch=[
            pltpu.VMEM((n_a, 1, n_b, w_rows, width), BF16),
            pltpu.VMEM((n_a, 1, n_b, unit, width), BF16),
        ],
        slot=row_count,
        width=width,
        n_t=n_t,
    )
    gu_far_one, gu_got, gu_far, branch_sent, branch_kept, gu_sent = barrier(
        (
            over_top(gu_far[0]),
            over_y(gu_sent[0]),
            gu_far,
            branch_sent,
            branch_kept,
            gu_sent[1],
        )
    )

    qo_sent, qo_kept = grads_attention(
        after(other_half, branch_sent), normed, d_qkv, attended, dy
    )
    gu_far_two, branch_got, gu_got_more, gu_far, qo_far_sent, qo_sent = barrier(
        (
            over_top(gu_far[1]),
            swap(branch_sent, "t", 1),
            over_y(gu_sent),
            gu_far,
            qo_sent[0],
            qo_sent[1],
        )
    )

    normal_rows = functools.partial(
        row_blocks,
        functools.partial(normal_kernel, masks),
        "normal_rows",
        inputs=(d_qkv, d_joined),
        parts=qkv_parts + gu_parts,
        scratch=[
            pltpu.VMEM((n_a, n_t, n_b, w_rows, d_qkv.shape[1]), BF16),
            pltpu.VMEM((n_y, n_a, n_t, n_b, w_rows, n_a * n_b * unit), BF16),
        ],
        slot=row_count,
        width=width,
        n_t=n_t,
    )
    branch = (branch_got, branch_kept)
    branch_sends = barrier(first_sends(branch))
    (normal_sent,) = normal_rows(after(here, qo_far_sent, *branch_sends), 0)
    gu_far_three, qo_far_got, branch_got, normal_sent, qo_sent, down_sent = barrier(
        (
            over_top(gu_far[2]),
            over_y(qo_far_sent),
            first_swaps(branch_sends),
            normal_sent,
            qo_sent,
            down_sent,
        )
    )
    qo_far = summed(qo_kept[0], qo_far_got).astype(BF16)
    gu_got = jnp.concatenate([gu_got, gu_got_more], axis=0)
    gu_far_got = jnp.concatenate([gu_far_one, gu_far_two, gu_far_three], axis=1)
    g_gu = summed(gu_kept, gu_got, gu_far_got.reshape(gu_kept.shape))
    g_gu = over_rest(g_gu, shape_w).astype(BF16)
    qo_far_one, qo_far_two, g_gu = barrier((qo_far[:1], qo_far[1:], g_gu))
    (normal_kept,) = normal_rows(after(here, normal_sent, g_gu), 1)
    qo_far_one, normal_got, qo_got, g_gu, normal_kept, qo_far_two, down_sent, branch_got = barrier(
        (
            over_top(qo_far_one),
            swap(normal_sent, "t", 1),
            over_y(qo_sent),
            exchange(g_gu),
            normal_kept,
            qo_far_two,
            down_sent,
            branch_got,
        )
    )

    qo_far_two, down_got = over_top(qo_far_two), over_y(down_sent)
    normal = (normal_got, normal_kept)
    normal_sends = barrier(first_sends(normal))
    new_gu, moment_gu, square_gu = finish(
        functools.partial(finish_gu_kernel, sizes, d_rows, unit),
        "finish_gate_up",
        after(g_gu, *normal_sends),
        w_gate_up,
        first_gate_up,
        second_gate_up,
    )
    branch_sends = second_sends(branch, [after(got, *normal_sends) for got in branch_got])
    normal_got, qo_far_two, down_got, branch_sends, new_gu = barrier(
        (first_swaps(normal_sends), qo_far_two, down_got, branch_sends, new_gu)
    )

    normal_sends = barrier(second_sends(normal, normal_got))
    qo_far_got = jnp.concatenate([qo_far_one, qo_far_two], axis=0)
    qo = after(summed(qo_kept[1], qo_got, qo_far_got), *normal_sends)
    g_qkv = over_rest(qo[:-1].transpose(1, 0, 2).reshape(qo.shape[1], -1), shape_w)
    g_out = qo[-1].reshape(half_width // LANES, -1, LANES).transpose(1, 0, 2)
    g_out = over_rest(g_out.reshape(-1, half_width), (top, 1, n_b, w_rows))
    g_qkv = g_qkv.astype(BF16).reshape(n_t, w_rows, -1, LANES).transpose(0, 2, 1, 3)
    g_qkv = barrier(g_qkv)
    g_down = summed(down_kept, down_got, down_far_got)
    g_down = over_rest(after(g_down, g_qkv), (top, 1, n_b, unit))
    new_down, moment_down, square_down = adam(w_down, g_down[0, :d_rows], first_down, second_down)
    g_qkv, normal_last, g_out, branch_sends, new_down = barrier(
        (g_qkv, second_swaps(normal_sends), g_out, branch_sends, new_down)
    )
    g_qkv = exchange(g_qkv)
    branch_last = second_swaps(branch_sends)
    normal_own = whole_rows(normal, normal_got, normal_last)
    _, scaled_own, inv_own = normalize(tokens.astype(F32), vec[0], vec[1])
    d_scaled = normal_own * vec[0]
    input_grad = cotangent.astype(F32) + inv_own * (
        d_scaled
        - jnp.mean(d_scaled, axis=-1, keepdims=True)
        - scaled_own * jnp.mean(d_scaled * scaled_own, axis=-1, keepdims=True)
    )
    g_bias = jnp.sum(bias_sums, axis=0).reshape(3 * n_a, 1, head_cols)
    is_here = (jnp.arange(n_t) == at_t)[None, :, None]
    g_bias = jnp.where(is_here, g_bias, 0.0).reshape(3, width)
    vector_part = jnp.concatenate(
        [
            jnp.sum(normal_own * scaled_own, axis=0)[None],
            jnp.sum(normal_own, axis=0)[None],
            g_bias,
        ],
        axis=0,
    )
    vector_part = vector_part.reshape(5, total, -1).transpose(1, 0, 2).reshape(total, 1, -1)
    vector_part = jnp.pad(vector_part, ((0, 0), (0, 0), (0, -vector_part.shape[2] % 128)))
    vector_part = lax.all_to_all(vector_part, AXES, split_axis=0, concat_axis=0, tiled=True)
    vector_grad = jnp.sum(vector_part, axis=0)[0, : vectors.size].reshape(vectors.shape)
    branch_own = whole_rows(branch, branch_got, branch_last)
    output = (tokens.astype(F32) + after(branch_own, vector_part)).astype(BF16)
    new_out, moment_out, square_out = adam(w_out, g_out[0], first_out, second_out)
    new_qkv, moment_qkv, square_qkv = finish(
        functools.partial(finish_qkv_kernel, sizes, head_cols),
        "finish_qkv",
        g_qkv,
        w_qkv,
        first_qkv,
        second_qkv,
    )
    new_vec, moment_vec, square_vec = adam_update(
        vectors, vector_grad, first_vectors, second_vectors, rate_vector, 0.0
    )
    return (
        output,
        input_grad.astype(BF16),
        new_qkv,
        new_out,
        new_gu,
        new_down,
        new_vec,
        moment_qkv,
        moment_out,
        moment_gu,
        moment_down,
        moment_vec,
        square_qkv,
        square_out,
        square_gu,
        square_down,
        square_vec,
    )


def solution(mesh):
    n_dp, n_y = mesh.shape["dp"], mesh.shape["branch"]
    n_b = max(1, HEAD * n_dp // (HEADS * HEAD))
    n_t = min(SLICES, n_dp // n_b)
    sizes = (n_dp // (n_t * n_b), n_t, n_b, n_y)
    split = Mesh(mesh.devices.reshape(sizes), AXES)
    dp = ("a", "t", "b")
    rows = P(AXES, None)
    matrix = P(dp, "y")
    vector = P(None, AXES)
    weights = (matrix, matrix, matrix, matrix, vector)
    return jax.shard_map(
        functools.partial(per_device, sizes),
        mesh=split,
        in_specs=(rows, rows, P(dp, None)) + weights * 3,
        out_specs=(rows, rows) + weights * 3,
        check_vma=False,
    )
```
